32 devices in a mesh: dp: 8 (over z, y), tensor: 4 (over x, core).
Axes of the slice: x: 2, y: 2, z: 4, core: 2. Of those that a mesh axis runs over, the one named last changes fastest.
Arguments:
- hidden_in: bfloat16 [32, 1024, 480], P('dp', 'tensor'), may hold values from -6 to 6
- attn_gain: float32 [480], replicated, may hold values from 0.25 to 1.75
- attn_shift: float32 [480], replicated, may hold values from -1.75 to 1.75
- query_key_value_weight: bfloat16 [3, 480, 480], P(None, None, 'tensor'), may hold values from -0.25 to 0.25
- query_key_value_bias: float32 [3, 480], P(None, 'tensor'), may hold values from -1.75 to 1.75
- attention_output_weight: bfloat16 [480, 480], P('tensor'), may hold values from -3.5 to 3.5
- out_bias: float32 [480], replicated, may hold values from -1.75 to 1.75
- ffn_gain: float32 [480], replicated, may hold values from 0.25 to 1.75
- ffn_shift: float32 [480], replicated, may hold values from -1.75 to 1.75
- up_projection_weight: bfloat16 [480, 1920], P('tensor', 'dp'), may hold values from -0.25 to 0.25
- up_projection_bias: float32 [1920], replicated, may hold values from -3 to 3
- down_projection_weight: bfloat16 [1920, 480], P('dp', 'tensor'), may hold values from -0.125 to 0.125
- down_bias: float32 [480], replicated, may hold values from -1.75 to 1.75
- lengths: int32 [32], P('dp'), may hold values from 204 to 1024, as said below
- cotangent: bfloat16 [32, 1024, 480], P('dp', 'tensor'), may hold values from -6 to 6
Outputs:
- hidden_out: bfloat16 [32, 1024, 480], P('dp', 'tensor')
- grad_hidden: bfloat16 [32, 1024, 480], P('dp', 'tensor')
- grad_attn_gain: float32 [480], replicated
- grad_attn_shift: float32 [480], replicated
- grad_qkv_weight: float32 [3, 480, 480], P(None, None, 'tensor')
- grad_qkv_bias: float32 [3, 480], P(None, 'tensor')
- grad_out_weight: float32 [480, 480], P('tensor')
- grad_out_bias: float32 [480], replicated
- grad_ffn_gain: float32 [480], replicated
- grad_ffn_shift: float32 [480], replicated
- grad_up_weight: float32 [480, 1920], P('tensor', 'dp')
- grad_up_bias: float32 [1920], replicated
- grad_down_weight: float32 [1920, 480], P('dp', 'tensor')
- grad_down_bias: float32 [480], replicated
The draws below stay inside these ranges and needn't reach their ends.
Inputs may be any that keep to these rules, and one draw needn't show every extreme that they name: `lengths`: every index of dp holds at least one row longer than 768, and some row has exactly 1024.
All inputs are finite; a program needn't handle non-finite values.
Results may differ from the reference program's by a relative error of at most 0.012.
Values may be sent and summed in bfloat16 or wider, within the bound.
No kernel may reach another device: no remote copies, remote signals or barrier semaphores. Data moves between devices by JAX's collectives and lax.ppermute only.
A program may use at most 192 MiB of HBM per device.

```python
import jax
import jax.numpy as jnp
from jax import lax

D = 480
HEADS = 20
HEAD_DIM = 24
FF = 1920
SEQ_LEN = 1024
SEQS = 4
BATCH = 32
N_DP = 8


def draw_lengths(key, part):
    key = jax.random.fold_in(key, 7)
    keys_all = jax.random.split(key, 5)
    short_len = jax.random.randint(keys_all[0], (BATCH,), SEQ_LEN // 5, 2 * SEQ_LEN // 5 + 1)
    long_len = jax.random.randint(keys_all[1], (BATCH,), 3 * SEQ_LEN // 4 + 1, SEQ_LEN + 1)
    chosen = jax.random.randint(keys_all[2], (BATCH,), 0, 4) == 0
    picked = jax.random.randint(keys_all[3], (BATCH // SEQS,), 0, SEQS)
    row_ids = jnp.arange(BATCH)
    forced = row_ids % SEQS == jnp.repeat(picked, SEQS)
    row_lengths = jnp.where(chosen | forced, long_len, short_len)
    top_row = jax.random.randint(keys_all[4], (), 0, BATCH)
    return jnp.where(row_ids == top_row, SEQ_LEN, row_lengths).astype(jnp.int32)


def shard_levels(stream_key, dims, shards, low, top_value):
    loudness = 1.0
    for position, shards_of in shards:
        draws = jax.random.uniform(jax.random.fold_in(jax.random.fold_in(stream_key, 6), position), (shards_of,), jnp.float32, low / len(shards), top_value / len(shards))
        loudness = loudness * jnp.repeat(jnp.exp(draws), dims[position] // shards_of).reshape((-1,) + (1,) * (len(dims) - 1 - position))
    return loudness


def normal_values(own_key, shape, scale, most, shards=(), dtype=jnp.bfloat16):
    values = jax.random.normal(own_key, shape, jnp.float32) * scale
    if len(shards) > 0:
        values = shard_levels(own_key, shape, shards, -0.22, 0.18) * values
    return jnp.clip(values, min=-most, max=most).astype(dtype)


def setup_inputs(seed: int = 0) -> dict:
    seeds = jax.random.split(jax.random.key(seed), 16)
    hidden_in = normal_values(seeds[0], (BATCH, SEQ_LEN, D), 1.0, 6.0, ((0, 8), (1, 4)))
    attn_gain = jnp.clip(1.0 + 0.15 * jax.random.normal(seeds[1], (D,), jnp.float32), 0.25, 1.75)
    attn_shift = normal_values(seeds[2], (D,), 0.3, 1.75, (), jnp.float32)
    query_key_value_weight = normal_values(seeds[3], (3, D, D), D ** -0.5, 0.25, ((2, 4),))
    query_key_value_bias = normal_values(seeds[4], (3, D), 0.3, 1.75, ((1, 4),), jnp.float32)
    attention_output_weight = normal_values(seeds[5], (D, D), (max(2, D * 8 // SEQ_LEN)) ** -0.5, 3.5, ((0, 4),))
    out_bias = normal_values(seeds[6], (D,), 0.3, 1.75, (), jnp.float32)
    ffn_gain = jnp.clip(1.0 + 0.15 * jax.random.normal(seeds[7], (D,), jnp.float32), 0.25, 1.75)
    ffn_shift = normal_values(seeds[8], (D,), 0.3, 1.75, (), jnp.float32)
    up_projection_weight = normal_values(seeds[9], (D, FF), D ** -0.5, 0.25, ((0, 4), (1, 8)))
    up_projection_bias = normal_values(seeds[10], (FF,), 0.5, 3.0, (), jnp.float32)
    down_projection_weight = normal_values(seeds[11], (FF, D), FF ** -0.5, 0.125, ((0, 8), (1, 4)))
    down_bias = normal_values(seeds[12], (D,), 0.3, 1.75, (), jnp.float32)
    lengths = draw_lengths(jax.random.fold_in(seeds[15], 71), 0)
    cotangent = normal_values(seeds[14], (BATCH, SEQ_LEN, D), 1.0, 6.0, ((0, 8), (1, 4)))
    return {"hidden_in": hidden_in, "attn_gain": attn_gain, "attn_shift": attn_shift, "query_key_value_weight": query_key_value_weight, "query_key_value_bias": query_key_value_bias, "attention_output_weight": attention_output_weight, "out_bias": out_bias, "ffn_gain": ffn_gain, "ffn_shift": ffn_shift, "up_projection_weight": up_projection_weight, "up_projection_bias": up_projection_bias, "down_projection_weight": down_projection_weight, "down_bias": down_bias, "lengths": lengths, "cotangent": cotangent}


@jax.custom_vjp
def low(v):
    return lax.optimization_barrier(v.astype(jnp.bfloat16)).astype(jnp.float32)

@jax.custom_vjp
def narrow_backward(v):
    return v

def low_keep(v):
    return (low(v), None)

def low_pass(kept, grad):
    return (grad,)

def back_keep(v):
    return (v, None)

def back_low(kept, grad):
    return (low(grad),)
low.defvjp(low_keep, low_pass)
narrow_backward.defvjp(back_keep, back_low)
EPS = 1e-05
MASK_FILL = -1000000000.0

def matrix_product(left, right, form):
    return jnp.einsum(form, left, right, precision=lax.Precision.HIGHEST)

def layer_norm(values, norm_gain, norm_shift):
    centre = values - lax.optimization_barrier(jnp.mean(values, axis=-1, keepdims=True))
    spread = lax.optimization_barrier(jnp.mean(centre * centre, axis=-1, keepdims=True))
    return centre * lax.rsqrt(spread + EPS) * norm_gain + norm_shift

def rotary_tables(length, head_dim):
    frequency = 1.0 / 10000.0 ** (jnp.arange(0, head_dim, 2).astype(jnp.float32) / head_dim)
    angles = jnp.arange(length).astype(jnp.float32)[:, None] * frequency[None, :]
    angles = jnp.concatenate([angles, angles], axis=-1)
    return (jnp.cos(angles), jnp.sin(angles))

def rotate(values, cosine_table, sine_table):
    half_dim = values.shape[-1] // 2
    turned = jnp.concatenate([-values[..., half_dim:], values[..., :half_dim]], axis=-1)
    return values * cosine_table + turned * sine_table

def attend_block(pieces):
    query_rows, key_rows, value_rows, row_length = pieces
    scores = narrow_backward(matrix_product(query_rows, key_rows, 'hqd,hkd->hqk'))
    valid = jnp.arange(SEQ_LEN) < row_length
    scores = jnp.where(valid[None, None, :], scores, MASK_FILL)
    attn_probs = low(jax.nn.softmax(scores, axis=-1))
    return matrix_product(attn_probs, value_rows, 'hqk,hkd->hqd')

def forward(hidden_rows, row_lengths, attn_gain, attn_shift, query_key_value_weight, query_key_value_bias, attention_output_weight, out_bias, ffn_gain, ffn_shift, up_projection_weight, up_projection_bias, down_projection_weight, down_bias):
    seq_count = hidden_rows.shape[0]
    first_normalized = low(layer_norm(hidden_rows, attn_gain, attn_shift))
    attention_projected = narrow_backward(matrix_product(first_normalized, query_key_value_weight, 'ugb,tba->tuga')) + query_key_value_bias[:, None, None, :]
    split_heads = attention_projected.reshape(3, seq_count, SEQ_LEN, HEADS, HEAD_DIM).transpose(0, 1, 3, 2, 4)
    cosine_table, sine_table = rotary_tables(SEQ_LEN, HEAD_DIM)
    queries = low(rotate(split_heads[0] * HEAD_DIM ** (-0.5), cosine_table, sine_table))
    key_rows = low(rotate(split_heads[1], cosine_table, sine_table))
    value_rows = low(split_heads[2])
    blended_rows = lax.map(jax.checkpoint(attend_block), (queries, key_rows, value_rows, row_lengths))
    blended_rows = blended_rows.transpose(0, 2, 1, 3).reshape(seq_count, SEQ_LEN, D)
    blended_rows = low(narrow_backward(blended_rows))
    residual_branch = narrow_backward(matrix_product(blended_rows, attention_output_weight, 'ovx,xc->ovc'))
    middle = hidden_rows + residual_branch + out_bias
    second_normalized = low(layer_norm(middle, ffn_gain, ffn_shift))
    up_projected = narrow_backward(matrix_product(second_normalized, up_projection_weight, 'ujr,rg->ujg')) + up_projection_bias
    gelu_output = low(jax.nn.gelu(up_projected, approximate=False))
    down_projected = narrow_backward(matrix_product(gelu_output, down_projection_weight, 'jbz,zq->jbq'))
    return middle + down_projected + down_bias

def reference(hidden_in, attn_gain, attn_shift, query_key_value_weight, query_key_value_bias, attention_output_weight, out_bias, ffn_gain, ffn_shift, up_projection_weight, up_projection_bias, down_projection_weight, down_bias, lengths, cotangent):
    params = tuple((weight.astype(jnp.float32) for weight in (attn_gain, attn_shift, query_key_value_weight, query_key_value_bias, attention_output_weight, out_bias, ffn_gain, ffn_shift, up_projection_weight, up_projection_bias, down_projection_weight, down_bias)))
    grouped_in = hidden_in.astype(jnp.float32).reshape(N_DP, SEQS, SEQ_LEN, D)
    grouped_len = lengths.reshape(N_DP, SEQS)
    grouped_cot = cotangent.astype(jnp.float32).reshape(N_DP, SEQS, SEQ_LEN, D)

    def one_group(totals, pieces):
        block_in, block_len, block_cot = pieces

        def apply_block(block_rows, *weights):
            return forward(block_rows, block_len, *weights)
        produced, pullback = jax.vjp(apply_block, block_in, *params)
        gradients = pullback(block_cot)
        totals = tuple((running + addend for running, addend in zip(totals, gradients[1:])))
        return (totals, (produced.astype(jnp.bfloat16), gradients[0].astype(jnp.bfloat16)))
    zero_grads = tuple((jnp.zeros(weight.shape, jnp.float32) for weight in params))
    totals, (outputs, gradient_rows) = lax.scan(one_group, zero_grads, (grouped_in, grouped_len, grouped_cot))
    return (outputs.reshape(BATCH, SEQ_LEN, D), gradient_rows.reshape(BATCH, SEQ_LEN, D), totals[0], totals[1], totals[2], totals[3], totals[4], totals[5], totals[6], totals[7], totals[8], totals[9], totals[10], totals[11])
```

```python
import math

import jax
import jax.numpy as jnp
import numpy as np
from jax import lax
from jax.experimental import pallas as pl
from jax.experimental.pallas import tpu as pltpu
from jax.sharding import PartitionSpec as P

HEAD_DIM = 24
HEAD_ROWS = 32
EPS = 1e-05
MASK_FILL = -1000000000.0
LOG2E = math.log2(math.e)
SAFE_SCORE = 85.0
LANES = 512
BLOCK = 256
BF16 = jnp.bfloat16
F32 = jnp.float32

NN = (((1,), (0,)), ((), ()))
NT = (((1,), (1,)), ((), ()))


def product(left, right, dims=NN):
    return lax.dot_general(left, right, dims, preferred_element_type=F32)


def vmem(count):
    return [pl.BlockSpec(memory_space=pltpu.VMEM)] * count


def smem():
    return pl.BlockSpec(memory_space=pltpu.SMEM)


def call(kernel, inputs, outs, scratch=(), in_specs=None, aliases=None, limit=40):
    return pl.pallas_call(
        kernel,
        out_shape=outs,
        in_specs=vmem(len(inputs)) if in_specs is None else in_specs,
        out_specs=vmem(len(outs)),
        scratch_shapes=list(scratch),
        input_output_aliases=aliases or {},
        compiler_params=pltpu.CompilerParams(vmem_limit_bytes=limit << 20),
    )(*inputs)


def shape(dims, dtype):
    return jax.ShapeDtypeStruct(dims, dtype)


def rows_at(index, size):
    return pl.ds(pl.multiple_of(index * size, size), size)


def split_three(values):
    high = values.astype(BF16).astype(F32)
    rest = values - high
    middle = rest.astype(BF16).astype(F32)
    return high, middle, rest - middle


def norm_kernel(hidden, gain, shift, *normed):
    width = hidden.shape[-1]
    for row, out in enumerate(normed):
        values = hidden[row].astype(F32)
        centre = values - jnp.mean(values, axis=-1, keepdims=True)
        inverse = lax.rsqrt(jnp.mean(centre * centre, axis=-1, keepdims=True) + EPS)
        result = centre * inverse * gain[...] + shift[...]
        out[:, 384:] = jnp.zeros((out.shape[0], LANES - 384), BF16)
        out[:, :width] = result.astype(BF16)


def rotary_constants(head_count, chunk, chunks):
    element = np.arange(head_count * HEAD_ROWS) % HEAD_ROWS
    live = element < HEAD_DIM
    half = HEAD_DIM // 2
    frequency = (1.0 / 10000.0 ** (np.arange(0, HEAD_DIM, 2).astype(np.float32) / HEAD_DIM)).astype(
        np.float32
    )
    per_row = np.where(live, frequency[element % half], 0.0).astype(np.float32)
    inner = per_row[:, None].astype(np.float64) * np.arange(chunk)[None, :]
    outer = per_row[:, None].astype(np.float64) * (np.arange(chunks) * chunk)[None, :]
    outer = np.repeat(outer[:, :, None], 128, axis=2).transpose(1, 0, 2)
    inner_pair = np.stack([np.cos(inner), np.sin(inner)]).astype(np.float32)
    outer_pair = np.stack([np.cos(outer), np.sin(outer)]).astype(np.float32)
    return inner_pair, outer_pair


def turn_masks(rows, columns):
    element = lax.broadcasted_iota(jnp.int32, (rows, columns), 0) % HEAD_ROWS
    return element < HEAD_DIM // 2, element < HEAD_DIM


def chunk_tables(inner, outer, index, chunk):
    cos_in, sin_in = inner[0], inner[1]
    cos_out = jnp.concatenate([outer[0, index]] * (chunk // 128), axis=1)
    sin_out = jnp.concatenate([outer[1, index]] * (chunk // 128), axis=1)
    return cos_in * cos_out - sin_in * sin_out, sin_in * cos_out + cos_in * sin_out


def rotate(values, cosine, sine, low):
    half = HEAD_DIM // 2
    rows = values.shape[0]
    turned = jnp.where(low, -pltpu.roll(values, rows - half, 0), pltpu.roll(values, half, 0))
    return values * cosine + turned * sine


def rotate_back(values, cosine, sine, low):
    half = HEAD_DIM // 2
    rows = values.shape[0]
    moved = values * sine
    return values * cosine + jnp.where(
        low, pltpu.roll(moved, rows - half, 0), -pltpu.roll(moved, half, 0)
    )


def attend_kernel(heads, chunks, chunk, info, *refs):
    parts = refs[:chunks]
    weight, bias, inner, outer = refs[chunks : chunks + 4]
    mixed_out = refs[chunks + 4 : 2 * chunks + 4]
    queries, keys, values, logsum, mixed_turned, normed, key_rows, peak, mixed_rows = refs[
        2 * chunks + 4 :
    ]
    position, length = info[0], info[1]
    full = chunk * chunks
    span = heads * HEAD_ROWS
    for k in range(chunks):
        normed[rows_at(position ^ k, chunk), :] = parts[k][...]
    low, _ = turn_masks(span, chunk)
    element = lax.broadcasted_iota(jnp.int32, (span, chunk), 0) % HEAD_ROWS
    query_top = jnp.zeros((heads, 1, chunk), F32)
    key_top = jnp.zeros((heads, 1, chunk), F32)
    for j in range(chunks):
        at = slice(j * chunk, (j + 1) * chunk)
        cosine, sine = chunk_tables(inner, outer, j, chunk)
        flat = product(weight[...], normed[at, :], NT) + bias[...]
        query = rotate(flat[:span], cosine, sine, low) * (LOG2E * HEAD_DIM**-0.5)
        key = rotate(flat[span : 2 * span], cosine, sine, low)
        value = flat[2 * span :]
        query_top = jnp.maximum(
            query_top,
            jnp.sum((query * query).reshape(heads, HEAD_ROWS, chunk), axis=1, keepdims=True),
        )
        key_top = jnp.maximum(
            key_top, jnp.sum((key * key).reshape(heads, HEAD_ROWS, chunk), axis=1, keepdims=True)
        )
        ones = (element >= HEAD_DIM) & (element < HEAD_DIM + 3)
        place = lax.broadcasted_iota(jnp.int32, (span, chunk), 1) + j * chunk
        fill = jnp.where(place >= length, MASK_FILL, 0.0)
        query = jnp.where(element == HEAD_DIM + 3, 1.0, query)
        key = jnp.where(ones, 1.0, jnp.where(element == HEAD_DIM + 3, fill, key))
        value = jnp.where(ones, 1.0, value)
        for h in range(heads):
            own = slice(h * HEAD_ROWS, (h + 1) * HEAD_ROWS)
            queries[h, :, at] = query[own].astype(BF16)
            keys[h, :, at] = key[own].astype(BF16)
            values[h, :, at] = value[own].astype(BF16)
            key_rows[h, at, :] = key[own].T.astype(BF16)
    bound = jnp.max(query_top, axis=-1, keepdims=True) * jnp.max(key_top, axis=-1, keepdims=True)
    safe = jnp.max(bound) <= SAFE_SCORE * SAFE_SCORE
    peak[...] = jnp.zeros_like(peak)

    @pl.when(jnp.logical_not(safe))
    def _():
        def one_head(h, carry):
            scores = product(key_rows[h], queries[h])
            peak[h] = jnp.broadcast_to(
                jnp.max(scores, axis=0, keepdims=True).astype(BF16).astype(F32), (8, full)
            )
            return carry

        lax.fori_loop(0, heads, one_head, 0)

    line = lax.broadcasted_iota(jnp.int32, (HEAD_ROWS, full), 0)

    def with_keys(count):
        def one_head(h, carry):
            top = peak[h, 0:1, :]
            query = jnp.where(line == HEAD_DIM, -top, queries[h].astype(F32)).astype(BF16)
            exponent = jnp.exp2(product(key_rows[h, :count, :], query)).astype(BF16)
            blend = product(values[h, :, :count], exponent)
            total = blend[HEAD_DIM : HEAD_DIM + 1, :]
            logsum[h] = jnp.broadcast_to(top + jnp.log2(total), (8, full))
            mixed_turned[pl.ds(pl.multiple_of(h * HEAD_DIM, 8), HEAD_DIM), :] = blend[
                :HEAD_DIM
            ] * (1.0 / total)
            return carry

        lax.fori_loop(0, heads, one_head, 0)

    mixed_turned[heads * HEAD_DIM :, :] = jnp.zeros(
        (mixed_turned.shape[0] - heads * HEAD_DIM, full), F32
    )
    blocks = (length + BLOCK - 1) // BLOCK
    for b in range(1, full // BLOCK + 1):
        pl.when(blocks == b)(lambda b=b: with_keys(b * BLOCK))
    for j in range(chunks):
        at = slice(j * chunk, (j + 1) * chunk)
        mixed_rows[at, :] = mixed_turned[:, at].T.astype(BF16)
    for k in range(chunks):
        mixed_out[k][...] = mixed_rows[rows_at(position ^ k, chunk), :]


def attend_back_kernel(heads, chunks, chunk, first, last, info, *refs):
    parts = refs[:chunks]
    upstream = refs[chunks : 2 * chunks]
    queries, keys, values, logsum, mixed_turned, weight, inner, outer = refs[
        2 * chunks : 2 * chunks + 8
    ]
    refs = refs[2 * chunks + 8 :]
    if not first:
        carried = refs[0]
        refs = refs[1:]
    normed_out = refs[:chunks]
    refs = refs[chunks:]
    if last:
        pieces = refs[:8]
        refs = refs[8:]
    else:
        running = refs[0]
        refs = refs[1:]
    (
        normed,
        upstream_rows,
        query_full,
        upstream_full,
        key_rows,
        value_rows,
        grads,
        grad_low,
        grad_rows,
        total,
        packed,
    ) = refs
    position, length, index = info[0], info[1], info[2]
    full = chunk * chunks
    span = heads * HEAD_ROWS
    for k in range(chunks):
        normed[rows_at(position ^ k, chunk), :] = parts[k][...]
        upstream_rows[rows_at(position ^ k, chunk), :] = upstream[k][...]
    line = lax.broadcasted_iota(jnp.int32, (HEAD_ROWS, chunk), 0)
    for j in range(chunks):
        at = slice(j * chunk, (j + 1) * chunk)
        turned = upstream_rows[at, :].astype(F32).T
        blend = turned * mixed_turned[:, at]
        for h in range(heads):
            own = slice(h * HEAD_DIM, (h + 1) * HEAD_DIM)
            inner_sum = jnp.sum(blend[own], axis=0, keepdims=True)
            high, middle, rest = split_three(-inner_sum)
            grown = turned[h * HEAD_DIM : h * HEAD_DIM + HEAD_ROWS]
            grown = jnp.where(line < HEAD_DIM, grown, 0.0)
            grown = jnp.where(line == HEAD_DIM, high, grown)
            grown = jnp.where(line == HEAD_DIM + 1, middle, grown)
            grown = jnp.where(line == HEAD_DIM + 2, rest, grown)
            upstream_full[h, :, at] = grown.astype(BF16)
            high, middle, rest = split_three(-logsum[h, 0:1, at])
            query = queries[h, :, at].astype(F32)
            query = jnp.where(line == HEAD_DIM, high, query)
            query = jnp.where(line == HEAD_DIM + 1, middle, query)
            query = jnp.where(line == HEAD_DIM + 2, rest, query)
            query_full[h, :, at] = query.astype(BF16)
            key_rows[h, at, :] = keys[h, :, at].astype(F32).T.astype(BF16)
            value_rows[h, at, :] = values[h, :, at].astype(F32).T.astype(BF16)

    def with_keys(count):
        def one_head(h, carry):
            own = pl.ds(pl.multiple_of(h * HEAD_ROWS, HEAD_ROWS), HEAD_ROWS)
            grad_query = jnp.zeros((HEAD_ROWS, full), F32)
            for b in range(count // BLOCK):
                at = slice(b * BLOCK, (b + 1) * BLOCK)
                probs = jnp.exp2(product(key_rows[h, at, :], query_full[h])).astype(BF16)
                grad_probs = product(value_rows[h, at, :], upstream_full[h]).astype(BF16)
                grad_scores = probs * grad_probs
                grads[2, own, at] = product(upstream_full[h], probs, NT)
                grads[1, own, at] = product(query_full[h], grad_scores, NT)
                grad_query += product(keys[h, :, at], grad_scores)
            grads[0, own, :] = grad_query
            return carry

        lax.fori_loop(0, heads, one_head, 0)
        if count < full:
            grads[1, :, count:] = jnp.zeros((span, full - count), F32)
            grads[2, :, count:] = jnp.zeros((span, full - count), F32)

    blocks = (length + BLOCK - 1) // BLOCK
    for b in range(1, full // BLOCK + 1):
        pl.when(blocks == b)(lambda b=b: with_keys(b * BLOCK))

    low, live = turn_masks(span, chunk)
    sums = [jnp.zeros((span, 128), F32) for _ in range(3)]
    for j in range(chunks):
        at = slice(j * chunk, (j + 1) * chunk)
        cosine, sine = chunk_tables(inner, outer, j, chunk)
        query = rotate_back(jnp.where(live, grads[0, :, at], 0.0), cosine, sine, low)
        key = rotate_back(jnp.where(live, grads[1, :, at], 0.0), cosine, sine, low)
        value = jnp.where(live, grads[2, :, at], 0.0)
        for c, part in enumerate((query * HEAD_DIM**-0.5, key * (1.0 / LOG2E), value)):
            for piece in range(chunk // 128):
                sums[c] = sums[c] + part[:, piece * 128 : (piece + 1) * 128]
            grad_low[c * span : (c + 1) * span, at] = part.astype(BF16)
            grad_rows[at, c * span : (c + 1) * span] = part.T.astype(BF16)
    for k in range(chunks):
        normed_out[k][...] = product(
            grad_rows[rows_at(position ^ k, chunk), :], weight[...]
        ).astype(BF16)
    lane = lax.broadcasted_iota(jnp.int32, (span, LANES), 1)
    for c in range(3):
        own = slice(c * span, (c + 1) * span)
        bias_grad = jnp.sum(sums[c], axis=1, keepdims=True)
        result = product(grad_low[own, :], normed[...])
        result = result + jnp.where(lane == 480, bias_grad, 0.0)
        if not first:
            result = result + carried[own, :]
        if last:
            total[own, :] = result
        else:
            running[own, :] = result
    if last:
        packed[...] = jnp.zeros_like(packed)
        for c in range(3):
            for h in range(heads):
                packed[c * 128 + h * HEAD_DIM : c * 128 + (h + 1) * HEAD_DIM, :] = total[
                    c * span + h * HEAD_ROWS : c * span + h * HEAD_ROWS + HEAD_DIM, :
                ]
        size = packed.shape[0] // 8
        for j in range(8):
            pieces[j][...] = packed[rows_at(index ^ j, size), :].astype(BF16)


def gelu_parts(values):
    magnitude = jnp.abs(values) * (0.5**0.5)
    density = jnp.exp2(values * values * (-0.5 * LOG2E))
    step = 1.0 / (1.0 + 0.3275911 * magnitude)
    series = 1.061405429 * step - 1.453152027
    series = series * step + 1.421413741
    series = series * step - 0.284496736
    series = series * step + 0.254829592
    tail = 0.5 * series * step * density
    share = jnp.where(values < 0, tail, 1.0 - tail)
    return share, density * (1.0 / math.sqrt(2.0 * math.pi))


def feed_kernel(rows, chunks, blocks, rows_each, info, *refs):
    hidden, cotangent, out_bias, gain, shift, up_bias, down_bias = refs[:7]
    refs = refs[7:]
    mixed = [refs[r * chunks : (r + 1) * chunks] for r in range(rows)]
    refs = refs[rows * chunks :]
    out_weight = refs[:chunks]
    refs = refs[chunks:]
    near, far = refs[:blocks], refs[blocks : 2 * blocks]
    refs = refs[2 * blocks :]
    hidden_out, grad_middle_out, sums = refs[:3]
    kept_out, sent_out = refs[3 : 3 + blocks], refs[3 + blocks : 3 + 2 * blocks]
    refs = refs[3 + 2 * blocks :]
    out_grad = refs[:chunks]
    refs = refs[chunks:]
    mixed_grads = [refs[r * chunks : (r + 1) * chunks] for r in range(rows)]
    refs = refs[rows * chunks :]
    weights, weight_grads, out_total, mixed_rows, down_total, back_total, low_rows, semaphores = refs
    core = info[0] & 1
    copies = []
    for j in range(blocks):
        copies.append(
            pltpu.make_async_copy(near[j], weights.at[core, j], semaphores.at[0, j])
        )
        copies.append(
            pltpu.make_async_copy(far[j], weights.at[1 - core, j], semaphores.at[1, j])
        )
    for copy in copies:
        copy.start()
    chunk = hidden.shape[1]
    width = hidden.shape[2]
    tokens = rows_each * chunk
    for half in range(rows // rows_each):
        own_rows = range(half * rows_each, (half + 1) * rows_each)
        source = hidden[half * rows_each : (half + 1) * rows_each].reshape(tokens, width)
        given_low = cotangent[half * rows_each : (half + 1) * rows_each].reshape(tokens, width)
        given = given_low.astype(F32)
        middle = source.astype(F32) + out_bias[...]
        for k in range(chunks):
            for place, row in enumerate(own_rows):
                mixed_rows[k, place * chunk : (place + 1) * chunk, :] = mixed[row][k][...]
            middle = middle + product(mixed_rows[k], out_weight[k][...])
        centre = middle - jnp.mean(middle, axis=-1, keepdims=True)
        inverse = lax.rsqrt(jnp.mean(centre * centre, axis=-1, keepdims=True) + EPS)
        unit = centre * inverse
        normed = unit * gain[...] + shift[...]
        low_rows[...] = normed.astype(BF16)
        normed_turned = normed.T.astype(BF16)
        given_turned = given.T.astype(BF16)
        down_total[...] = middle + down_bias[...]
        back_total[...] = jnp.zeros_like(back_total)
        if half == 0:
            for copy in copies:
                copy.wait()

        def one_block(j, carry):
            up_weight, down_weight = weights[0, j], weights[1, j]
            upward = product(low_rows[...], up_weight) + up_bias[pl.ds(j, 1), :]
            share, density = gelu_parts(upward)
            active = (upward * share).astype(BF16)
            down_total[...] += product(active, down_weight, NT)
            grad_up = product(given_low, down_weight) * (share + upward * density)
            bias_grad = jnp.sum(grad_up, axis=0, keepdims=True)
            grad_low = grad_up.astype(BF16)
            back_total[...] += product(grad_low, up_weight, NT)
            up_grad = product(normed_turned, grad_low)
            down_grad = product(given_turned, active)
            if half == 0:
                weight_grads[0, j] = up_grad
                weight_grads[1, j] = down_grad
                sums[pl.ds(8 + j, 1), :BLOCK] = bias_grad
            else:
                weight_grads[0, j] += up_grad
                weight_grads[1, j] += down_grad
                sums[pl.ds(8 + j, 1), :BLOCK] += bias_grad
            return carry

        lax.fori_loop(0, blocks, one_block, 0)
        hidden_out[half * rows_each : (half + 1) * rows_each] = (
            down_total[...].astype(BF16).reshape(rows_each, chunk, width)
        )
        back = back_total[...]
        scaled = back * gain[...]
        centred = scaled - jnp.mean(scaled, axis=-1, keepdims=True)
        grad_middle = given + inverse * (
            centred - unit * jnp.mean(scaled * unit, axis=-1, keepdims=True)
        )
        grad_middle_out[half * rows_each : (half + 1) * rows_each] = grad_middle.reshape(
            rows_each, chunk, width
        )
        totals = (back * unit, back, grad_middle, given)
        for place, values in enumerate(totals):
            line = jnp.sum(values, axis=0, keepdims=True)
            if half == 0:
                sums[place : place + 1, :width] = line
            else:
                sums[place : place + 1, :width] += line
        branch = grad_middle.astype(BF16)
        for k in range(chunks):
            grad = product(branch, out_weight[k][...], NT).astype(BF16)
            for place, row in enumerate(own_rows):
                mixed_grads[row][k][...] = grad[place * chunk : (place + 1) * chunk]
            out_part = product(mixed_rows[k].astype(F32).T.astype(BF16), branch)
            if half == 0:
                out_total[k] = out_part
            else:
                out_grad[k][...] = (out_total[k] + out_part).astype(BF16)

    def write(kept):
        for j in range(blocks):
            kept_out[j][...] = weight_grads[kept, j].astype(BF16)
            sent_out[j][...] = weight_grads[1 - kept, j].astype(BF16)

    pl.when(core == 0)(lambda: write(0))
    pl.when(core == 1)(lambda: write(1))


def norm_back_kernel(rows, hidden, middle_grad, gain, *refs):
    parts, (out, sums) = refs[: 3 * rows], refs[3 * rows :]
    width = hidden.shape[-1]
    gain_total = jnp.zeros((1, width), F32)
    shift_total = jnp.zeros((1, width), F32)
    for row in range(rows):
        values = hidden[row].astype(F32)
        centre = values - jnp.mean(values, axis=-1, keepdims=True)
        inverse = lax.rsqrt(jnp.mean(centre * centre, axis=-1, keepdims=True) + EPS)
        unit = centre * inverse
        grad = (
            parts[3 * row][...].astype(F32)
            + parts[3 * row + 1][...].astype(F32)
            + parts[3 * row + 2][...].astype(F32)
        )[:, :width]
        gain_total = gain_total + jnp.sum(grad * unit, axis=0, keepdims=True)
        shift_total = shift_total + jnp.sum(grad, axis=0, keepdims=True)
        scaled = grad * gain[...]
        centred = scaled - jnp.mean(scaled, axis=-1, keepdims=True)
        result = middle_grad[row] + inverse * (
            centred - unit * jnp.mean(scaled * unit, axis=-1, keepdims=True)
        )
        out[row] = result.astype(BF16)
    sums[0:1, :width] = gain_total
    sums[1:2, :width] = shift_total


def unpack_kernel(info, *refs):
    pieces, (weight_grad, bias_grad, whole) = refs[:8], refs[8:]
    size = pieces[0].shape[0]
    for j in range(8):
        whole[rows_at(info[2] ^ j, size), :] = pieces[j][...].astype(F32)
    columns = weight_grad.shape[2]
    for c in range(3):
        turned = whole[c * 128 : (c + 1) * 128, :].T
        weight_grad[c] = turned[: weight_grad.shape[1], :columns]
        bias_grad[c : c + 1, :] = turned[480:481, :columns]


def swap(values, axis, bit):
    size = lax.axis_size(axis)
    return lax.ppermute(values, axis, [(i, i ^ bit) for i in range(size)])


def gather_four(own):
    beside = swap(own, "tensor", 1)
    across = swap(own, "tensor", 2)
    return [own, beside, across, swap(across, "tensor", 1)]


def spread_four(parts):
    return [parts[0]] + [swap(parts[k], "tensor", k) for k in range(1, 4)]


def add_low(left, right):
    return (left.astype(F32) + right.astype(F32)).astype(BF16)


def tree_sum(parts):
    while len(parts) > 1:
        parts = [parts[i] + parts[i + 1] for i in range(0, len(parts), 2)]
    return parts[0]


def sum_all(values):
    if lax.axis_size("dp") != 8:
        return lax.psum(values, ("dp", "tensor"))
    values = tree_sum([values] + [swap(values, "dp", j) for j in range(1, 8)])
    return tree_sum([values] + [swap(values, "tensor", k) for k in range(1, 4)])


def gather_feed(up, down, core, position, index):
    pair = jnp.stack([up, down.T])
    pair = jnp.pad(pair, ((0, 0), (0, 0), (0, BLOCK - pair.shape[2])))
    mine = lax.dynamic_index_in_dim(pair, core, 0, keepdims=False)
    other = lax.dynamic_index_in_dim(pair, 1 - core, 0, keepdims=False)
    duo = jnp.stack([mine, swap(other, "tensor", 1)])
    four = jnp.concatenate([duo, swap(duo, "tensor", 2)])
    four = jnp.take(four, position ^ jnp.arange(4), axis=0)
    near = [None] * 8
    near[0] = four.reshape(-1, BLOCK)
    for e in (2, 4, 6):
        near[e] = swap(near[0], "dp", e)
    for e in (0, 2, 4, 6):
        near[e + 1] = swap(near[e], "dp", 1)
    far = [swap(part, "tensor", 1) for part in near]
    return near, far


def gather_feed_plain(up, down, core):
    pair = jnp.stack([up, down.T])
    pair = lax.all_gather(pair, "tensor", axis=1, tiled=True)
    pair = lax.all_gather(pair, "dp", axis=2, tiled=True)
    pair = pair.reshape(2, pair.shape[1], 8, -1).transpose(0, 2, 1, 3)
    pair = jnp.pad(pair, ((0, 0), (0, 0), (0, 0), (0, BLOCK - pair.shape[3])))
    mine = lax.dynamic_index_in_dim(pair, core, 0, keepdims=False)
    other = lax.dynamic_index_in_dim(pair, 1 - core, 0, keepdims=False)
    return [mine[j] for j in range(8)], [other[j] for j in range(8)]


def scatter_feed(kept, sent, core, position, hidden_count):
    kept = [add_low(kept[j], swap(sent[j], "tensor", 1)) for j in range(8)]
    odd = [swap(kept[e + 1], "dp", 1) for e in (0, 2, 4, 6)]
    kept = [add_low(kept[e], odd[e // 2]) for e in (0, 2, 4, 6)]
    total = kept[0].astype(F32)
    for e in (2, 4, 6):
        total = total + swap(kept[e // 2], "dp", e).astype(F32)
    total = total.astype(BF16)
    total = total.reshape(2, -1, BLOCK)
    chip = position // 2
    total = add_low(
        lax.dynamic_index_in_dim(total, chip, 0, keepdims=False),
        swap(lax.dynamic_index_in_dim(total, 1 - chip, 0, keepdims=False), "tensor", 2),
    )
    total = total.reshape(2, -1, BLOCK)
    mine = lax.dynamic_index_in_dim(total, core, 0, keepdims=False)
    other = swap(lax.dynamic_index_in_dim(total, 1 - core, 0, keepdims=False), "tensor", 1)
    up = jnp.where(core == 0, mine, other)
    down = jnp.where(core == 0, other, mine)
    return (
        up[:, :hidden_count].astype(F32),
        down[:, :hidden_count].astype(F32).T,
    )


def scatter_feed_plain(kept, sent, core, hidden_count):
    grads = jnp.stack([jnp.stack(kept), jnp.stack(sent)])
    grads = jnp.where(core == 0, grads, grads[::-1]).astype(F32)
    grads = grads[:, :, :, : hidden_count * lax.axis_size("dp") // 8]
    grads = grads.transpose(0, 2, 1, 3).reshape(2, grads.shape[2], -1)
    grads = lax.psum_scatter(grads, "dp", scatter_dimension=2, tiled=True)
    grads = lax.psum_scatter(grads, "tensor", scatter_dimension=1, tiled=True)
    return grads[0], grads[1].T


def shards(
    hidden_in,
    attn_gain,
    attn_shift,
    query_key_value_weight,
    query_key_value_bias,
    attention_output_weight,
    out_bias,
    ffn_gain,
    ffn_shift,
    up_projection_weight,
    up_projection_bias,
    down_projection_weight,
    down_bias,
    lengths,
    cotangent,
):
    chunks = lax.axis_size("tensor")
    ring = lax.axis_size("dp") == 8
    position = lax.axis_index("tensor")
    index = lax.axis_index("dp") if ring else jnp.int32(0)
    core = position & 1
    rows, chunk, width = hidden_in.shape
    full = chunk * chunks
    columns = query_key_value_weight.shape[2]
    heads = columns // HEAD_DIM
    span = heads * HEAD_ROWS
    hidden_count = up_projection_weight.shape[1]
    feed_blocks = 8

    weight = query_key_value_weight.transpose(0, 2, 1).reshape(3, heads, HEAD_DIM, width)
    weight = jnp.pad(
        weight, ((0, 0), (0, 0), (0, HEAD_ROWS - HEAD_DIM), (0, LANES - width))
    ).reshape(3 * span, LANES)
    bias = jnp.pad(
        query_key_value_bias.reshape(3, heads, HEAD_DIM), ((0, 0), (0, 0), (0, HEAD_ROWS - HEAD_DIM))
    ).reshape(3 * span, 1)
    inner_table, outer_table = (
        jnp.asarray(table) for table in rotary_constants(heads, chunk, chunks)
    )

    normed = call(
        norm_kernel,
        (hidden_in, attn_gain[None], attn_shift[None]),
        [shape((chunk, LANES), BF16)] * rows,
    )
    gathered = [gather_four(normed[r]) for r in range(rows)]
    out_weight = gather_four(jnp.pad(attention_output_weight, ((0, 128 - columns), (0, 0))))
    if ring:
        near, far = gather_feed(
            up_projection_weight, down_projection_weight, core, position, index
        )
        bias_blocks = jnp.take(
            up_projection_bias.reshape(8, -1), index ^ jnp.arange(8), axis=0
        )
    else:
        near, far = gather_feed_plain(up_projection_weight, down_projection_weight, core)
        bias_blocks = up_projection_bias.reshape(8, -1)
    block_width = bias_blocks.shape[1]
    bias_blocks = jnp.pad(bias_blocks, ((0, 0), (0, BLOCK - block_width)))

    kept = []
    mixed = []
    for r in range(rows):
        info = jnp.stack([position, lengths[r], index]).astype(jnp.int32)
        inputs = (info, *gathered[r], weight, bias, inner_table, outer_table)
        outs = call(
            lambda *refs: attend_kernel(heads, chunks, chunk, *refs),
            inputs,
            [shape((chunk, 128), BF16)] * chunks
            + [shape((heads, HEAD_ROWS, full), BF16)] * 3
            + [shape((heads, 8, full), F32), shape((128, full), F32)],
            scratch=[
                pltpu.VMEM((full, LANES), BF16),
                pltpu.VMEM((heads, full, HEAD_ROWS), BF16),
                pltpu.VMEM((heads, 8, full), F32),
                pltpu.VMEM((full, 128), BF16),
            ],
            in_specs=[smem()] + vmem(len(inputs) - 1),
        )
        mixed.append(spread_four(outs[:chunks]))
        kept.append((info, outs[chunks:]))

    rows_each = 2
    inputs = (
        jnp.stack([position, index]).astype(jnp.int32),
        hidden_in,
        cotangent,
        out_bias[None],
        ffn_gain[None],
        ffn_shift[None],
        bias_blocks,
        down_bias[None],
        *[part for row in mixed for part in row],
        *out_weight,
        *near,
        *far,
    )
    plain = len(inputs) - 1 - 2 * feed_blocks
    outs = call(
        lambda *refs: feed_kernel(rows, chunks, feed_blocks, rows_each, *refs),
        inputs,
        [
            shape((rows, chunk, width), BF16),
            shape((rows, chunk, width), F32),
            shape((16, LANES), F32),
        ]
        + [shape((width, BLOCK), BF16)] * (2 * feed_blocks)
        + [shape((128, width), BF16)] * chunks
        + [shape((chunk, 128), BF16)] * (rows * chunks),
        scratch=[
            pltpu.VMEM((2, feed_blocks, width, BLOCK), BF16),
            pltpu.VMEM((2, feed_blocks, width, BLOCK), F32),
            pltpu.VMEM((chunks, 128, width), F32),
            pltpu.VMEM((chunks, rows_each * chunk, 128), BF16),
            pltpu.VMEM((rows_each * chunk, width), F32),
            pltpu.VMEM((rows_each * chunk, width), F32),
            pltpu.VMEM((rows_each * chunk, width), BF16),
            pltpu.SemaphoreType.DMA((2, feed_blocks)),
        ],
        in_specs=[smem()]
        + vmem(plain)
        + [pl.BlockSpec(memory_space=pl.ANY)] * (2 * feed_blocks),
        limit=56,
    )
    hidden_out, grad_middle, feed_sums = outs[:3]
    outs = outs[3:]
    feed_kept, feed_sent = outs[:feed_blocks], outs[feed_blocks : 2 * feed_blocks]
    outs = outs[2 * feed_blocks :]
    out_grads, outs = outs[:chunks], outs[chunks:]
    mixed_grads = [spread_four(outs[r * chunks : (r + 1) * chunks]) for r in range(rows)]

    if ring:
        grad_up_weight, grad_down_weight = scatter_feed(
            feed_kept, feed_sent, core, position, hidden_count
        )
    else:
        grad_up_weight, grad_down_weight = scatter_feed_plain(
            feed_kept, feed_sent, core, hidden_count
        )
    first = add_low(out_grads[0], swap(out_grads[1], "tensor", 1))
    second = add_low(out_grads[2], swap(out_grads[3], "tensor", 1))
    out_total = add_low(first, swap(second, "tensor", 2))
    if ring:
        for bit in (1, 2, 4):
            out_total = add_low(out_total, swap(out_total, "dp", bit))
        out_total = out_total.astype(F32)
        order = jnp.concatenate([jnp.arange(8), 8 + (index ^ jnp.arange(8))])
        feed_sums = jnp.take(feed_sums, order, axis=0)
    else:
        out_total = lax.psum(out_total.astype(F32), "dp")
    grad_out_weight = out_total[:columns]
    feed_sums = sum_all(feed_sums)

    running = None
    reduced = []
    for r in range(rows):
        info, saved = kept[r]
        last = r == rows - 1
        inputs = (info, *gathered[r], *mixed_grads[r], *saved, weight, inner_table, outer_table)
        if r > 0:
            inputs = inputs + (running,)
        outs = call(
            lambda *refs, r=r, last=last: attend_back_kernel(
                heads, chunks, chunk, r == 0, last, *refs
            ),
            inputs,
            [shape((chunk, LANES), BF16)] * chunks
            + (
                [shape((48, LANES), BF16)] * 8 if last else [shape((3 * span, LANES), F32)]
            ),
            scratch=[
                pltpu.VMEM((full, LANES), BF16),
                pltpu.VMEM((full, 128), BF16),
                pltpu.VMEM((heads, HEAD_ROWS, full), BF16),
                pltpu.VMEM((heads, HEAD_ROWS, full), BF16),
                pltpu.VMEM((heads, full, HEAD_ROWS), BF16),
                pltpu.VMEM((heads, full, HEAD_ROWS), BF16),
                pltpu.VMEM((3, span, full), F32),
                pltpu.VMEM((3 * span, full), BF16),
                pltpu.VMEM((full, 3 * span), BF16),
                pltpu.VMEM((3 * span, LANES), F32),
                pltpu.VMEM((384, LANES), F32),
            ],
            in_specs=[smem()] + vmem(len(inputs) - 1),
        )
        parts = outs[:chunks]
        across = add_low(parts[2], swap(parts[3], "tensor", 1))
        reduced += [parts[0], swap(parts[1], "tensor", 1), swap(across, "tensor", 2)]
        if last:
            pieces = outs[chunks:]
        else:
            running = outs[chunks]

    if ring:
        arrived = [swap(pieces[j], "dp", j) for j in range(1, 8)]
        own = tree_sum([part.astype(F32) for part in (pieces[0], *arrived)]).astype(BF16)
        pieces = [own] + [swap(own, "dp", j) for j in range(1, 8)]
    else:
        pieces = [
            part.astype(BF16)
            for part in lax.psum(jnp.stack(pieces).astype(F32), "dp")
        ]
    grad_qkv_weight, grad_qkv_bias = call(
        unpack_kernel,
        (kept[0][0], *pieces),
        [shape((3, width, columns), F32), shape((3, columns), F32)],
        scratch=[pltpu.VMEM((384, LANES), F32)],
        in_specs=[smem()] + vmem(8),
    )
    grad_hidden, norm_sums = call(
        lambda *refs: norm_back_kernel(rows, *refs),
        (hidden_in, grad_middle, attn_gain[None], *reduced),
        [shape((rows, chunk, width), BF16), shape((8, LANES), F32)],
    )
    norm_sums = sum_all(norm_sums)
    return (
        hidden_out,
        grad_hidden,
        norm_sums[0, :width],
        norm_sums[1, :width],
        grad_qkv_weight,
        grad_qkv_bias,
        grad_out_weight,
        feed_sums[2, :width],
        feed_sums[0, :width],
        feed_sums[1, :width],
        grad_up_weight,
        feed_sums[8:, :block_width].reshape(-1),
        grad_down_weight,
        feed_sums[3, :width],
    )


def solution(mesh):
    return jax.shard_map(
        shards,
        mesh=mesh,
        in_specs=(
            P("dp", "tensor", None),
            P(),
            P(),
            P(None, None, "tensor"),
            P(None, "tensor"),
            P("tensor", None),
            P(),
            P(),
            P(),
            P("tensor", "dp"),
            P(),
            P("dp", "tensor"),
            P(),
            P("dp"),
            P("dp", "tensor", None),
        ),
        out_specs=(
            P("dp", "tensor", None),
            P("dp", "tensor", None),
            P(),
            P(),
            P(None, None, "tensor"),
            P(None, "tensor"),
            P("tensor", None),
            P(),
            P(),
            P(),
            P("tensor", "dp"),
            P(),
            P("dp", "tensor"),
            P(),
        ),
        check_vma=False,
    )
```

```python
import math

import jax
import jax.numpy as jnp
import numpy as np
from jax import lax
from jax.experimental import pallas as pl
from jax.experimental.pallas import tpu as pltpu
from jax.sharding import PartitionSpec as P

HEAD_DIM = 24
HEAD_ROWS = 32
EPS = 1e-05
MASK_FILL = -1000000000.0
LOG2E = math.log2(math.e)
SAFE_SCORE = 85.0
WORK_SCALE = 0.1
BLOCK = 256
LANES = 512
BF16 = jnp.bfloat16
F32 = jnp.float32

NN = (((1,), (0,)), ((), ()))
NT = (((1,), (1,)), ((), ()))
TN = (((0,), (0,)), ((), ()))


def product(left, right, dims=NN):
    return lax.dot_general(left, right, dims, preferred_element_type=F32)


def vmem(count):
    return [pl.BlockSpec(memory_space=pltpu.VMEM)] * count


def smem():
    return pl.BlockSpec(memory_space=pltpu.SMEM)


def hbm(count=1):
    return [pl.BlockSpec(memory_space=pltpu.HBM)] * count


def call(kernel, inputs, outs, scratch=(), in_specs=None, out_specs=None, limit=40, tiles=0):
    flops = int(2 * 256**3 * tiles * WORK_SCALE)
    in_specs = vmem(len(inputs)) if in_specs is None else in_specs
    inputs = [
        pltpu.with_memory_space_constraint(part, pltpu.HBM)
        if spec.memory_space is pltpu.HBM
        else part
        for part, spec in zip(inputs, in_specs)
    ]
    out_specs = vmem(len(outs)) if out_specs is None else out_specs
    outs = [
        pltpu.HBM(part.shape, part.dtype) if spec.memory_space is pltpu.HBM else part
        for part, spec in zip(outs, out_specs)
    ]
    return pl.pallas_call(
        kernel,
        out_shape=outs,
        in_specs=in_specs,
        out_specs=out_specs,
        scratch_shapes=list(scratch),
        compiler_params=pltpu.CompilerParams(vmem_limit_bytes=limit << 20),
        cost_estimate=pl.CostEstimate(flops=flops, transcendentals=0, bytes_accessed=0),
    )(*inputs)


def shape(dims, dtype):
    return jax.ShapeDtypeStruct(dims, dtype)


def at_block(index, size):
    return pl.ds(pl.multiple_of(index * size, size), size)


def split_three(values):
    high = values.astype(BF16).astype(F32)
    rest = values - high
    middle = rest.astype(BF16).astype(F32)
    return high, middle, rest - middle


def after(values, *others):
    return lax.optimization_barrier((values, *others))[0]


def norm_columns(values):
    centre = values - jnp.mean(values, axis=0, keepdims=True)
    inverse = lax.rsqrt(jnp.mean(centre * centre, axis=0, keepdims=True) + EPS)
    return centre * inverse, inverse


def norm_columns_back(upstream, unit, inverse, gain):
    scaled = upstream * gain
    centred = scaled - jnp.mean(scaled, axis=0, keepdims=True)
    return inverse * (centred - unit * jnp.mean(scaled * unit, axis=0, keepdims=True))


def pair_kernel(info, up, down, pair, up_inside, down_inside, semaphores):
    copies = [
        pltpu.make_async_copy(up, up_inside, semaphores.at[0]),
        pltpu.make_async_copy(down, down_inside, semaphores.at[1]),
    ]
    for copy in copies:
        copy.start()
    pair[...] = jnp.zeros_like(pair)
    for copy in copies:
        copy.wait()
    size = up.shape[1]
    up_half = up_inside[...]
    down_half = down_inside[...].astype(F32).T.astype(BF16)

    @pl.when(info[0] & 1 == 0)
    def _():
        pair[:, :size] = up_half
        pair[:, BLOCK : BLOCK + size] = down_half

    @pl.when(info[0] & 1 == 1)
    def _():
        pair[:, :size] = down_half
        pair[:, BLOCK : BLOCK + size] = up_half


def norm_kernel(
    hidden_in,
    gain,
    shift,
    out_weight_in,
    first_out,
    second_out,
    hidden,
    gain_inside,
    shift_inside,
    out_weight,
    rows_scratch,
    semaphores,
):
    rows, width, chunk = hidden.shape
    copies = [
        pltpu.make_async_copy(hidden_in.at[row], hidden.at[row], semaphores.at[row])
        for row in range(rows)
    ]
    others = [
        pltpu.make_async_copy(gain, gain_inside, semaphores.at[4]),
        pltpu.make_async_copy(shift, shift_inside, semaphores.at[5]),
        pltpu.make_async_copy(out_weight_in, out_weight, semaphores.at[6]),
    ]
    for copy in others[:2] + copies + others[2:]:
        copy.start()
    rows_scratch[...] = jnp.zeros_like(rows_scratch)
    others[0].wait()
    others[1].wait()
    rows_scratch[0:1, :] = gain_inside[...]
    rows_scratch[1:2, :] = shift_inside[...]
    columns = rows_scratch[...].T
    half = rows // 2
    for row in range(rows):
        copies[row].wait()
        unit, _ = norm_columns(hidden[row].astype(F32))
        target = first_out if row < half else second_out
        place = row % half * width
        target[place : place + width, :] = (unit * columns[:, 0:1] + columns[:, 1:2]).astype(
            BF16
        )
    others[2].wait()
    own = out_weight.shape[0]
    second_out[half * width : half * width + own, :] = out_weight[:, :chunk]
    rest = width - chunk
    second_out[half * width + own : half * width + 2 * own, :] = jnp.zeros((own, chunk), BF16)
    second_out[half * width + own : half * width + 2 * own, :rest] = out_weight[:, chunk:]


def prepare_kernel(heads, info, *refs):
    outside, refs = refs[:9], refs[9:]
    weight_out, weight_turned_out, columns_out, bias_out, up_bias_out, vector_rows = refs[:6]
    weight_scratch, bias_rows = refs[6:8]
    inside, semaphores = refs[8:17], refs[17]
    copies = [
        pltpu.make_async_copy(source, target, semaphores.at[place])
        for place, (source, target) in enumerate(zip(outside, inside))
    ]
    for copy in copies:
        copy.start()
    vectors, (up_bias, weight, bias) = inside[:6], inside[6:]
    width = weight.shape[1]
    vector_rows[...] = jnp.zeros_like(vector_rows)
    for copy in copies:
        copy.wait()
    for place, vector in enumerate(vectors):
        vector_rows[place : place + 1, :] = vector[...]
    columns_out[...] = jnp.concatenate([vector_rows[...], jnp.zeros((120, width), F32)]).T
    span = heads * HEAD_DIM
    for c in range(3):
        own = slice(c * span, (c + 1) * span)
        weight_scratch[own, :] = weight[c].astype(F32).T
        bias_out[own, :] = jnp.broadcast_to(bias[c : c + 1, :], (128, span)).T
    weight_out[...] = weight_scratch[...].astype(BF16)
    weight_turned_out[...] = weight_scratch[...].T.astype(BF16)
    bias_rows[...] = jnp.zeros_like(bias_rows)
    count = up_bias.shape[1]
    block = count // 8
    spread = jnp.broadcast_to(up_bias[...], (8, count))
    for j in range(8):
        moved = pltpu.roll(spread, lax.rem(count - (info[1] ^ j) * block, count), 1)
        bias_rows[j : j + 1, :block] = moved[0:1, :block]
    up_bias_out[...] = bias_rows[...].T


def assemble_kernel(chunks, info, *refs):
    parts, (out, rows) = refs[:chunks], refs[chunks:]
    size = parts[0].shape[0]
    for k in range(chunks):
        half = parts[k][:, (k & 1) * BLOCK : ((k & 1) + 1) * BLOCK]
        rows[at_block(info[0] ^ k, size), :] = half.astype(F32)
    out[...] = rows[...].astype(BF16)


def rotary_constants(chunk, chunks):
    half = HEAD_DIM // 2
    element = np.arange(HEAD_DIM)
    frequency = (1.0 / 10000.0 ** (np.arange(0, HEAD_DIM, 2).astype(np.float32) / HEAD_DIM)).astype(
        np.float32
    )
    per_row = frequency[element % half].astype(np.float64)
    inner = per_row[:, None] * np.arange(chunk)[None, :]
    outer = per_row[:, None] * (np.arange(chunks) * chunk)[None, :]
    outer = np.repeat(outer[:, :, None], chunk, axis=2).transpose(1, 0, 2)
    inner_pair = np.stack([np.cos(inner), np.sin(inner)]).astype(np.float32)
    outer_pair = np.stack([np.cos(outer), np.sin(outer)]).astype(np.float32)
    return inner_pair, outer_pair


def chunk_tables(inner, outer, index):
    cos_in, sin_in = inner[0], inner[1]
    cos_out, sin_out = outer[0, index], outer[1, index]
    element = lax.broadcasted_iota(jnp.int32, cos_in.shape, 0)
    sine = sin_in * cos_out + cos_in * sin_out
    return cos_in * cos_out - sin_in * sin_out, jnp.where(
        element < HEAD_DIM // 2, -sine, sine
    )


def swap_halves(values):
    return pltpu.roll(values, HEAD_DIM // 2, 0)


def attend_kernel(heads, chunks, chunk, first_row, rows, info, lengths, *refs):
    parts = refs[:chunks]
    weight, bias, inner, outer, own_out, near_out, cross_out = refs[chunks : chunks + 7]
    queries, keys, values, logsum, mixed_turned, normed_out, key_rows, peak, flat = refs[
        chunks + 7 : chunks + 16
    ]
    normed, semaphores = refs[chunks + 16 :]
    position = info[0]
    width = normed.shape[1]
    full = chunk * chunks
    span = heads * HEAD_DIM
    scale = LOG2E * HEAD_DIM**-0.5
    blocks_full = full // BLOCK

    def one_row(r, carry):
        length = lengths[first_row + r]
        for k in range(chunks):
            normed[r, :, at_block(position ^ k, chunk)] = parts[k][at_block(r, width), :]
        pltpu.make_async_copy(normed.at[r], normed_out.at[r], semaphores.at[r]).start()
        flat[...] = product(weight[...], normed[r])
        line = lax.broadcasted_iota(jnp.int32, (8, chunk), 0)
        ones = jnp.where(line < 3, 1.0, 0.0)
        query_line = jnp.where(line == 3, 1.0, 0.0)
        query_top = [jnp.zeros((1, chunk), F32) for _ in range(heads)]
        key_top = [jnp.zeros((1, chunk), F32) for _ in range(heads)]
        for j in range(chunks):
            at = slice(j * chunk, (j + 1) * chunk)
            cosine, sine = chunk_tables(inner, outer, j)
            query_cosine, query_sine = cosine * scale, sine * scale
            place = lax.broadcasted_iota(jnp.int32, (8, chunk), 1) + j * chunk
            key_line = jnp.where((line == 3) & (place >= length), MASK_FILL, ones)
            for h in range(heads):
                here = h * HEAD_DIM
                query, key, value = (
                    flat[c * span + here : c * span + here + HEAD_DIM, at]
                    + jnp.concatenate(
                        [bias[c * span + here : c * span + here + HEAD_DIM, :]] * (chunk // 128),
                        axis=1,
                    )
                    for c in range(3)
                )
                query = query * query_cosine + swap_halves(query) * query_sine
                key = key * cosine + swap_halves(key) * sine
                query_top[h] = jnp.maximum(
                    query_top[h], jnp.sum(query * query, axis=0, keepdims=True)
                )
                key_top[h] = jnp.maximum(key_top[h], jnp.sum(key * key, axis=0, keepdims=True))
                key_full = jnp.concatenate([key, key_line])
                queries[r, h, :, at] = jnp.concatenate([query, query_line]).astype(BF16)
                keys[r, h, :, at] = key_full.astype(BF16)
                values[r, h, :, at] = jnp.concatenate([value, ones]).astype(BF16)
                key_rows[h, at, :] = key_full.T.astype(BF16)
        bound = jnp.zeros((1, 1), F32)
        for h in range(heads):
            bound = jnp.maximum(
                bound,
                jnp.max(query_top[h], axis=-1, keepdims=True)
                * jnp.max(key_top[h], axis=-1, keepdims=True),
            )
        safe = jnp.max(bound) <= SAFE_SCORE * SAFE_SCORE
        peak[...] = jnp.zeros_like(peak)

        @pl.when(jnp.logical_not(safe))
        def _():
            def one_head(h, carry):
                scores = product(key_rows[h], queries[r, h])
                peak[pl.ds(h, 1), :] = (
                    jnp.max(scores, axis=0, keepdims=True).astype(BF16).astype(F32)
                )
                return carry

            lax.fori_loop(0, heads, one_head, 0)

        head_line = lax.broadcasted_iota(jnp.int32, (HEAD_ROWS, full), 0)

        def with_keys(count):
            def one_head(h, carry):
                top = peak[pl.ds(h, 1), :]
                query = jnp.where(
                    head_line == HEAD_DIM, -top, queries[r, h].astype(F32)
                ).astype(BF16)
                exponent = jnp.exp2(product(key_rows[h, :count, :], query)).astype(BF16)
                blend = product(values[r, h, :, :count], exponent)
                total = blend[HEAD_DIM : HEAD_DIM + 1, :]
                logsum[r, pl.ds(h, 1), :] = top + jnp.log2(total)
                mixed_turned[r, pl.ds(pl.multiple_of(h * HEAD_DIM, 8), HEAD_DIM), :] = blend[
                    :HEAD_DIM
                ] * (1.0 / total)
                return carry

            lax.fori_loop(0, heads, one_head, 0)

        blocks = (length + BLOCK - 1) // BLOCK
        for b in range(1, blocks_full + 1):
            pl.when(blocks == b)(lambda b=b: with_keys(b * BLOCK))
        mixed_turned[r, span:, :] = jnp.zeros((mixed_turned.shape[1] - span, full), F32)
        own_out[r] = mixed_turned[r, :, at_block(position, chunk)].astype(BF16)
        near_out[r] = mixed_turned[r, :, at_block(position ^ 1, chunk)].astype(BF16)
        cross_out[r, 0] = mixed_turned[r, :, at_block(position ^ 2, chunk)].astype(BF16)
        cross_out[r, 1] = mixed_turned[r, :, at_block(position ^ 3, chunk)].astype(BF16)
        return carry

    lax.fori_loop(0, rows, one_row, 0)
    for r in range(rows):
        pltpu.make_async_copy(normed.at[r], normed_out.at[r], semaphores.at[r]).wait()


def attend_back_kernel(heads, chunks, chunk, row, local, first, last, info, lengths, *refs):
    upstream_own, upstream_near, upstream_cross, upstream_far = refs[:4]
    queries, keys, values, logsum, mixed_turned, normed_in, weight_turned, inner, outer = refs[
        4:13
    ]
    refs = refs[13:]
    if not first:
        carried = refs[0]
        refs = refs[1:]
    if last:
        out_own, out_near, out_cross, weight, vector_rows = refs[:5]
        refs = refs[5:]
    own_out, near_out, cross_out = refs[:3]
    refs = refs[3:]
    if last:
        even_pieces, odd_pieces, norm_sums = refs[:3]
        refs = refs[3:]
    else:
        running = refs[0]
        refs = refs[1:]
    (
        upstream,
        query_full,
        upstream_full,
        key_rows,
        value_rows,
        grads,
        grad_low,
        packed,
        normed,
        semaphore,
    ) = refs
    fetch = pltpu.make_async_copy(normed_in.at[local], normed, semaphore)
    fetch.start()
    position, index, length = info[0], info[1], lengths[row]
    full = chunk * chunks
    span = heads * HEAD_DIM
    upstream[:, at_block(position, chunk)] = upstream_own[local]
    upstream[:, at_block(position ^ 1, chunk)] = upstream_near[local]
    upstream[:, at_block(position ^ 2, chunk)] = upstream_cross[local, 0]
    upstream[:, at_block(position ^ 3, chunk)] = upstream_far[local, 1]
    zeros = jnp.zeros((5, chunk), F32)
    line = lax.broadcasted_iota(jnp.int32, (8, chunk), 0)
    for j in range(chunks):
        at = slice(j * chunk, (j + 1) * chunk)
        turned = upstream[:, at].astype(F32)
        blend = turned * mixed_turned[local, :, at]
        for h in range(heads):
            own = slice(h * HEAD_DIM, (h + 1) * HEAD_DIM)
            high, middle, rest = split_three(-jnp.sum(blend[own], axis=0, keepdims=True))
            extra = jnp.where(
                line == 0, high, jnp.where(line == 1, middle, jnp.where(line == 2, rest, 0.0))
            )
            upstream_full[h, :, at] = jnp.concatenate([turned[own], extra]).astype(BF16)
            high, middle, rest = split_three(-logsum[local, h : h + 1, at])
            extra = jnp.where(
                line == 0,
                high,
                jnp.where(
                    line == 1, middle, jnp.where(line == 2, rest, jnp.where(line == 3, 1.0, 0.0))
                ),
            )
            query = queries[local, h, :, at].astype(F32)[:HEAD_DIM]
            query_full[h, :, at] = jnp.concatenate([query, extra]).astype(BF16)
            key_rows[h, at, :] = keys[local, h, :, at].astype(F32).T.astype(BF16)
            value_rows[h, at, :] = values[local, h, :, at].astype(F32).T.astype(BF16)

    def with_keys(count):
        def one_head(h, carry):
            own = pl.ds(pl.multiple_of(h * HEAD_DIM, 8), HEAD_DIM)
            grad_query = jnp.zeros((HEAD_ROWS, full), F32)
            for b in range(count // BLOCK):
                at = slice(b * BLOCK, (b + 1) * BLOCK)
                probs = jnp.exp2(product(key_rows[h, at, :], query_full[h])).astype(BF16)
                grad_probs = product(value_rows[h, at, :], upstream_full[h]).astype(BF16)
                grad_scores = probs * grad_probs
                grads[2, own, at] = product(upstream_full[h], probs, NT)[:HEAD_DIM]
                grads[1, own, at] = product(query_full[h], grad_scores, NT)[:HEAD_DIM]
                grad_query += product(keys[local, h, :, at], grad_scores)
            grads[0, own, :] = grad_query[:HEAD_DIM]
            return carry

        lax.fori_loop(0, heads, one_head, 0)
        if count < full:
            grads[1, :, count:] = jnp.zeros((span, full - count), F32)
            grads[2, :, count:] = jnp.zeros((span, full - count), F32)

    blocks = (length + BLOCK - 1) // BLOCK
    for b in range(1, full // BLOCK + 1):
        pl.when(blocks == b)(lambda b=b: with_keys(b * BLOCK))

    sums = [[jnp.zeros((HEAD_DIM, 128), F32) for _ in range(heads)] for _ in range(3)]
    for j in range(chunks):
        at = slice(j * chunk, (j + 1) * chunk)
        cosine, sine = chunk_tables(inner, outer, j)
        query_cosine, query_sine = cosine * HEAD_DIM**-0.5, sine * HEAD_DIM**-0.5
        key_cosine, key_sine = cosine * (1.0 / LOG2E), sine * (1.0 / LOG2E)
        for h in range(heads):
            own = slice(h * HEAD_DIM, (h + 1) * HEAD_DIM)
            query, key, value = (grads[c, own, at] for c in range(3))
            query = query * query_cosine - swap_halves(query) * query_sine
            key = key * key_cosine - swap_halves(key) * key_sine
            for c, part in enumerate((query, key, value)):
                for piece in range(chunk // 128):
                    sums[c][h] = sums[c][h] + part[:, piece * 128 : (piece + 1) * 128]
                grads[c, own, at] = part
    for c in range(3):
        grad_low[c * span : (c + 1) * span, :] = grads[c].astype(BF16)
    for k in range(chunks):
        result = product(
            weight_turned[...], grad_low[:, at_block(position ^ k, chunk)]
        ).astype(BF16)
        if k == 0:
            own_out[...] = result
        elif k == 2:
            cross_out[...] = result
        else:
            near_out[k // 2] = result
    width = weight_turned.shape[0]
    fetch.wait()
    result = product(grad_low[...], normed[...], NT)
    bias_grad = jnp.concatenate(
        [jnp.sum(part, axis=1, keepdims=True) for group in sums for part in group]
    )
    bias_grad = jnp.broadcast_to(bias_grad, (3 * span, 128))
    if not first:
        result = result + carried[:, :width]
        bias_grad = bias_grad + carried[:, LANES:]
    if not last:
        running[:, :width] = result
        running[:, LANES:] = bias_grad
        return
    packed[: 3 * span, :width] = result
    gain_sum = jnp.zeros((8, width), F32)
    shift_sum = jnp.zeros((8, width), F32)
    gain, shift = vector_rows[0:1, :], vector_rows[1:2, :]
    for place in range(0, 3 * span, 8):
        own = slice(place, place + 8)
        factor = weight[own, :].astype(F32)
        column = bias_grad[own, 0:1]
        gain_sum = gain_sum + factor * (result[own] - shift * column)
        shift_sum = shift_sum + factor * column
    norm_sums[...] = jnp.zeros_like(norm_sums)
    norm_sums[0:1, :] = jnp.sum(gain_sum, axis=0, keepdims=True) / gain
    norm_sums[1:2, :] = jnp.sum(shift_sum, axis=0, keepdims=True)
    lane = lax.broadcasted_iota(jnp.int32, (3 * span, 128), 1)
    packed[: 3 * span, LANES - 128 :] = jnp.where(
        lane >= width - (LANES - 128), bias_grad, packed[: 3 * span, LANES - 128 :]
    )
    shared = (out_own[...].astype(F32) + out_near[0].astype(F32)) + out_cross[...].astype(F32)
    packed[3 * span : 4 * span, :] = shared[:span]
    packed[4 * span : 4 * span + 16, :] = shared[128:144]
    packed[4 * span + 16 :, :] = jnp.zeros((packed.shape[0] - 4 * span - 16, LANES), F32)
    size = packed.shape[0] // 8
    for j in range(8):
        target = odd_pieces if j % 2 else even_pieces
        target[j // 2] = packed[at_block(index ^ j, size), :].astype(BF16)


def gelu_parts(values):
    magnitude = jnp.abs(values) * (0.5**0.5)
    density = jnp.exp2(values * values * (-0.5 * LOG2E))
    step = 1.0 / (1.0 + 0.3275911 * magnitude)
    series = 1.061405429 * step - 1.453152027
    series = series * step + 1.421413741
    series = series * step - 0.284496736
    series = series * step + 0.254829592
    tail = 0.5 * series * step * density
    share = jnp.where(values < 0, tail, 1.0 - tail)
    return share, density * (1.0 / math.sqrt(2.0 * math.pi))


def feed_kernel(chunks, blocks, first_row, rows, last, info, *refs):
    hidden, cotangent, columns, up_bias = refs[:4]
    mixed_own, mixed_near, mixed_cross, mixed_far = refs[4:8]
    out_weight = refs[8 : 8 + chunks]
    refs = refs[8 + chunks :]
    if last:
        weights, carried, out_carried, sums_carried, bias_carried, hidden_before = refs[:6]
        refs = refs[6:]
    else:
        feeds, refs = refs[:12], refs[12:]
    hidden_out, grad_middle_out, grad_own, grad_near, grad_cross = refs[:5]
    refs = refs[5:]
    if last:
        kept_out, sent_out, out_own, out_near, out_cross = refs[:5]
    else:
        weights, carried, out_carried, sums_carried, bias_carried = refs[:5]
    refs = refs[5:]
    (
        out_rows,
        mixed,
        source,
        given,
        low_rows,
        down_total,
        back_total,
        bias_total,
        semaphores,
    ) = refs
    core, index = info[0] & 1, info[1]
    width, chunk = hidden.shape[1:]
    tokens = rows * chunk
    columns_held = mixed_own.shape[1]
    if not last:
        copies = []
        for side in range(2):
            sources = list(feeds[6 * side : 6 * side + 4])
            duo, duo_beside = feeds[6 * side + 4 : 6 * side + 6]
            place = core if side == 0 else 1 - core
            for e in range(2):
                sources += [duo.at[e], duo_beside.at[e]]
            for j in range(blocks):
                copies.append(
                    pltpu.make_async_copy(
                        sources[j], weights.at[place, j], semaphores.at[side, j]
                    )
                )
        for copy in copies:
            copy.start()
    own_rows = (out_weight[0].shape[0] - 2 * width) // 2
    for k in range(chunks):
        base = 2 * width
        out_rows[k] = jnp.zeros(out_rows.shape[1:], BF16)
        out_rows[k, :own_rows, :chunk] = out_weight[k][base : base + own_rows, :]
        out_rows[k, :own_rows, chunk:] = out_weight[k][
            base + own_rows : base + 2 * own_rows, : width - chunk
        ]
    for r in range(rows):
        at = slice(r * chunk, (r + 1) * chunk)
        mixed[0, :, at] = mixed_own[r]
        mixed[1, :, at] = mixed_near[r]
        mixed[2, :, at] = mixed_cross[r, 0]
        mixed[3, :, at] = mixed_far[r, 1]
        source[:, at] = hidden[first_row + r].astype(F32)
        given[:, at] = cotangent[first_row + r]
    middle = source[...] + columns[:, 2:3]
    for k in range(chunks):
        middle = middle + product(out_rows[k], mixed[k], TN)
    source[...] = middle
    unit, inverse = norm_columns(middle)
    low_rows[...] = (unit * columns[:, 3:4] + columns[:, 4:5]).astype(BF16)
    down_total[...] = middle + columns[:, 5:6]
    back_total[...] = jnp.zeros_like(back_total)
    bias_total[...] = jnp.zeros_like(bias_total)
    lane = lax.broadcasted_iota(jnp.int32, (BLOCK, 128), 1)
    if not last:
        for copy in copies:
            copy.wait()

    def one_block(j, carry):
        up_weight, down_weight = weights[0, j], weights[1, j]
        bias = jnp.sum(jnp.where(lane == j, up_bias[...], 0.0), axis=1, keepdims=True)
        upward = product(up_weight, low_rows[...], TN) + bias
        share, density = gelu_parts(upward)
        active = (upward * share).astype(BF16)
        down_total[...] += product(down_weight, active)
        grad_up = product(down_weight, given[...], TN) * (share + upward * density)
        bias_total[...] += jnp.where(lane == j, jnp.sum(grad_up, axis=1, keepdims=True), 0.0)
        grad_low = grad_up.astype(BF16)
        back_total[...] += product(up_weight, grad_low)
        up_grad = product(low_rows[...], grad_low, NT)
        down_grad = product(given[...], active, NT)
        if last:
            up_grad = (up_grad + carried[0, j]).astype(BF16)
            down_grad = (down_grad + carried[1, j]).astype(BF16)
            odd, place = j & 1, j >> 1

            @pl.when(core == 0)
            def _():
                kept_out[odd, place] = up_grad
                sent_out[odd, place] = down_grad

            @pl.when(core == 1)
            def _():
                kept_out[odd, place] = down_grad
                sent_out[odd, place] = up_grad
        else:
            carried[0, j] = up_grad
            carried[1, j] = down_grad
        return carry

    lax.fori_loop(0, blocks, one_block, 0)
    shift = first_row if last else 0
    if last:
        hidden_out[:first_row] = hidden_before[...]
    for r in range(rows):
        hidden_out[shift + r] = down_total[:, r * chunk : (r + 1) * chunk].astype(BF16)
    unit, inverse = norm_columns(source[...])
    back = back_total[...]
    given_wide = given[...].astype(F32)
    grad_middle = given_wide + norm_columns_back(back, unit, inverse, columns[:, 3:4])
    for r in range(rows):
        grad_middle_out[r] = grad_middle[:, r * chunk : (r + 1) * chunk]
    column_lane = lax.broadcasted_iota(jnp.int32, (width, 128), 1)
    totals = jnp.zeros((width, 128), F32)
    for place, values in enumerate((back * unit, back, grad_middle, given_wide)):
        totals = jnp.where(column_lane == place, jnp.sum(values, axis=1, keepdims=True), totals)
    branch = grad_middle.astype(BF16)
    targets = (out_own, out_near.at[0], out_cross, out_near.at[1]) if last else (None,) * 4
    for k in range(chunks):
        grad = product(out_rows[k], branch).astype(BF16)
        for r in range(rows):
            own = grad[:, r * chunk : (r + 1) * chunk]
            if k == 0:
                grad_own[r] = own
            elif k == 1:
                grad_near[r] = own
            else:
                grad_cross[r, k - 2] = own
        out_part = product(mixed[k], branch, NT)
        if last:
            targets[k][:columns_held, 384:] = jnp.zeros((columns_held, LANES - 384), BF16)
            targets[k][:columns_held, :width] = (out_part + out_carried[k]).astype(BF16)
        else:
            out_carried[k] = out_part
    if last:
        totals = (totals + sums_carried[...]).T
        bias_rows = (bias_total[...] + bias_carried[...]).T
        down_total[0:16, :] = jnp.zeros((16, tokens), F32)
        down_total[0:4, :width] = totals[:4]
        for j in range(blocks):
            down_total[pl.ds(4 + (index ^ j), 1), :BLOCK] = bias_rows[j : j + 1, :]
        for k in range(chunks):
            targets[k][columns_held:, :] = down_total[0:16, :LANES].astype(BF16)
    else:
        sums_carried[...] = totals
        bias_carried[...] = bias_total[...]


def norm_back_kernel(rows, hidden, columns, *refs):
    middle_grads, refs = refs[:2], refs[2:]
    own_parts, near_parts = refs[0 : 2 * rows : 2], refs[1 : 2 * rows : 2]
    cross_parts, (out,) = refs[2 * rows : 3 * rows - 1], refs[3 * rows - 1 :]
    cross_parts = list(cross_parts[:-1]) + [cross_parts[-1].at[0], cross_parts[-1].at[1]]
    gain = columns[:, 0:1]
    for row in range(rows):
        unit, inverse = norm_columns(hidden[row].astype(F32))
        grad = (
            own_parts[row][...].astype(F32)
            + near_parts[row][0].astype(F32)
            + cross_parts[row][...].astype(F32)
        )
        half = rows // 2
        result = middle_grads[row // half][row % half] + norm_columns_back(
            grad, unit, inverse, gain
        )
        out[row] = result.astype(BF16)


def add_pieces_kernel(even, beside, *outs):
    for i, out in enumerate(outs):
        out[...] = (even[i].astype(F32) + beside[i].astype(F32)).astype(BF16)


def own_piece_kernel(first, second, fourth, sixth, norm_sums, out):
    size = first.shape[0]
    total = first[...].astype(F32) + second[...].astype(F32)
    total = total + fourth[...].astype(F32) + sixth[...].astype(F32)
    out[:size, :] = total.astype(BF16)
    width = norm_sums.shape[1]
    values = norm_sums[...]
    high = values.astype(BF16)
    rest = (values - high.astype(F32)).astype(BF16)
    out[size:, 384:] = jnp.zeros((16, LANES - 384), BF16)
    out[size:, :width] = jnp.concatenate([high.astype(F32), rest.astype(F32)]).astype(BF16)


def feed_sum_kernel(info, first, second, fourth, sixth, keep, send, rows):
    total = first[...].astype(F32) + second[...].astype(F32)
    rows[...] = total + fourth[...].astype(F32) + sixth[...].astype(F32)
    size = keep.shape[0]
    chip = info[0] >> 1
    keep[...] = rows[at_block(chip, size), :].astype(BF16)
    send[...] = rows[at_block(1 - chip, size), :].astype(BF16)


def feed_pair_kernel(info, kept, came, mine, other, rows):
    rows[...] = kept[...].astype(F32) + came[...].astype(F32)
    size = mine.shape[0]
    core = info[0] & 1
    mine[...] = rows[at_block(core, size), :].astype(BF16)
    other[...] = rows[at_block(1 - core, size), :].astype(BF16)


def unpack_kernel(info, *refs):
    evens, beside = refs[:4], refs[4]
    refs = refs[5:]
    if len(refs) > 12:
        mine, came, refs = refs[0], refs[1], refs[2:]
        up_grad, down_grad = refs[10:12]
        refs = refs[:10] + refs[12:]
        count = up_grad.shape[1]

        def write(up, down):
            up_grad[...] = up[:, :count].astype(F32)
            down_grad[...] = down[...].astype(F32).T[:count, :]

        pl.when(info[0] & 1 == 0)(lambda: write(mine, came))
        pl.when(info[0] & 1 == 1)(lambda: write(came, mine))
    weight_grad, bias_grad, out_grad, gain, shift, out_bias, down_bias, up_bias = refs[:8]
    norm_gain, norm_shift, whole, line = refs[8:]
    size = whole.shape[0] // 8
    width = weight_grad.shape[1]
    norms = [evens[0][size:, :].astype(F32) + beside[0, size:, :].astype(F32)]
    for i in range(4):
        whole[at_block(info[1] ^ (2 * i), size), :] = evens[i][:size, :].astype(F32)
        whole[at_block(info[1] ^ (2 * i + 1), size), :] = beside[i, :size, :].astype(F32)
        if i > 0:
            norms.append(evens[i][size:, :].astype(F32) + beside[i, size:, :].astype(F32))
    norms = (norms[0] + norms[1]) + (norms[2] + norms[3])
    norms = norms[:8] + norms[8:16]
    norm_gain[...] = norms[0:1, :width]
    norm_shift[...] = norms[1:2, :width]
    columns = weight_grad.shape[2]
    for c in range(3):
        turned = whole[c * columns : (c + 1) * columns, :].T
        weight_grad[c] = turned[:width, :]
        bias_grad[c : c + 1, :] = turned[width : width + 1, :]
    out_grad[...] = whole[3 * columns : 4 * columns, :width]
    for place, target in enumerate((gain, shift, out_bias, down_bias)):
        target[...] = whole[4 * columns + place : 4 * columns + place + 1, :width]
    block = up_bias.shape[0] // 8
    for j in range(8):
        line[:, j * block : (j + 1) * block] = whole[
            4 * columns + 4 + j : 4 * columns + 5 + j, :block
        ]
    up_bias[...] = line[0, :]


def swap(values, axis, bit):
    size = lax.axis_size(axis)
    return lax.ppermute(values, axis, [(i, i ^ bit) for i in range(size)])


def gather_four(own, *others):
    beside = swap(own, "tensor", 1)
    across = swap(own, "tensor", 2)
    return [own, beside, across, swap(after(across, *others), "tensor", 1)]


def spread_four(own, near, cross, *others):
    beside = swap(near, "tensor", 1)
    across = swap(cross, "tensor", 2)
    return [own, beside, across, swap(after(across, *others), "tensor", 1)]


def add_low(*parts):
    total = parts[0].astype(F32)
    for part in parts[1:]:
        total = total + part.astype(F32)
    return total.astype(BF16)


def gather_feed_plain(up, down, core):
    pair = jnp.stack([up, down.T])
    pair = lax.all_gather(pair, "tensor", axis=1, tiled=True)
    pair = lax.all_gather(pair, "dp", axis=2, tiled=True)
    pair = pair.reshape(2, pair.shape[1], 8, -1).transpose(0, 2, 1, 3)
    pair = jnp.pad(pair, ((0, 0), (0, 0), (0, 0), (0, BLOCK - pair.shape[3])))
    pair = jnp.where(core == 0, pair, pair[::-1])
    feeds = []
    for half in (pair[0], pair[1]):
        feeds += [half[0], half[1], half[2], half[3], half[4::2], half[5::2]]
    return feeds


def scatter_feed_plain(kept, sent, core, hidden_count):
    grads = jnp.stack([kept, sent]).swapaxes(1, 2).reshape(2, 8, *kept.shape[2:])
    grads = jnp.where(core == 0, grads, grads[::-1]).astype(F32)
    grads = grads[:, :, :, : hidden_count * lax.axis_size("dp") // 8]
    grads = grads.transpose(0, 2, 1, 3).reshape(2, grads.shape[2], -1)
    grads = lax.psum_scatter(grads, "dp", scatter_dimension=2, tiled=True)
    grads = lax.psum_scatter(grads, "tensor", scatter_dimension=1, tiled=True)
    return grads[0], grads[1].T


def sum_pieces(even, odd, norm_sums):
    parts = call(
        add_pieces_kernel,
        (even, swap(odd, "dp", 1)),
        [shape(even.shape[1:], BF16)] * 4,
        limit=4,
    )
    parts = [parts[0]] + [swap(parts[i], "dp", 2 * i) for i in (1, 2, 3)]
    for bit in (2, 1):
        norm_sums = norm_sums + swap(norm_sums, "tensor", bit)
    (own,) = call(
        own_piece_kernel,
        (*parts, norm_sums),
        [shape((even.shape[1] + 16, LANES), BF16)],
        limit=4,
    )
    back = [own] + [swap(own, "dp", e) for e in (2, 4, 6)]
    return back + [swap(jnp.stack(back), "dp", 1)]


def sum_pieces_plain(even, odd, norm_sums):
    even, odd = (lax.psum(part.astype(F32), "dp").astype(BF16) for part in (even, odd))
    norm_sums = lax.psum(norm_sums, ("dp", "tensor"))
    high = norm_sums.astype(BF16)
    rest = (norm_sums - high.astype(F32)).astype(BF16)
    rows = jnp.concatenate([high, rest])
    rows = jnp.pad(rows, ((0, 0), (0, LANES - rows.shape[1])))
    even = jnp.concatenate([even, jnp.stack([rows] + [jnp.zeros_like(rows)] * 3)], axis=1)
    odd = jnp.concatenate([odd, jnp.zeros((4, *rows.shape), BF16)], axis=1)
    return [even[i] for i in range(4)] + [odd]


def shards(
    hidden_in,
    attn_gain,
    attn_shift,
    query_key_value_weight,
    query_key_value_bias,
    attention_output_weight,
    out_bias,
    ffn_gain,
    ffn_shift,
    up_projection_weight,
    up_projection_bias,
    down_projection_weight,
    down_bias,
    lengths,
    cotangent,
):
    chunks = lax.axis_size("tensor")
    ring = lax.axis_size("dp") == 8
    position = lax.axis_index("tensor")
    index = lax.axis_index("dp") if ring else jnp.int32(0)
    core = position & 1
    rows, chunk, width = hidden_in.shape
    full = chunk * chunks
    columns = query_key_value_weight.shape[2]
    heads = columns // HEAD_DIM
    hidden_count = up_projection_weight.shape[1]
    blocks = 8
    half = rows // 2

    info = jnp.stack([position, index]).astype(jnp.int32)
    lengths = lengths.astype(jnp.int32)
    inner_table, outer_table = (jnp.asarray(table) for table in rotary_constants(chunk, chunks))
    hidden = hidden_in.transpose(0, 2, 1)
    given = cotangent.transpose(0, 2, 1)

    if ring:
        inputs = (info, up_projection_weight, down_projection_weight)
        (pair,) = call(
            pair_kernel,
            inputs,
            [shape((columns, 2 * BLOCK), BF16)],
            scratch=[pltpu.VMEM(part.shape, part.dtype) for part in inputs[1:]]
            + [pltpu.SemaphoreType.DMA((2,))],
            in_specs=[smem()] + hbm(2),
            limit=4,
            tiles=20,
        )
        pair_across = swap(pair, "tensor", 2)
    inputs = (
        after(hidden, pair) if ring else hidden,
        attn_gain[None],
        attn_shift[None],
        attention_output_weight,
    )
    first, second = call(
        norm_kernel,
        inputs,
        [
            shape((half * width, chunk), BF16),
            shape((half * width + 2 * columns, chunk), BF16),
        ],
        scratch=[pltpu.VMEM(part.shape, part.dtype) for part in inputs]
        + [pltpu.VMEM((128, width), F32), pltpu.SemaphoreType.DMA((8,))],
        in_specs=hbm(4),
        limit=8,
        tiles=80,
    )
    inputs = (
        info,
        attn_gain[None],
        attn_shift[None],
        out_bias[None],
        ffn_gain[None],
        ffn_shift[None],
        down_bias[None],
        up_projection_bias[None],
        query_key_value_weight,
        query_key_value_bias,
    )
    weight, weight_turned, vectors, bias, up_bias, vector_rows = call(
        lambda *refs: prepare_kernel(heads, *refs),
        inputs,
        [
            shape((3 * columns, width), BF16),
            shape((width, 3 * columns), BF16),
            shape((width, 128), F32),
            shape((3 * columns, 128), F32),
            shape((BLOCK, 128), F32),
            shape((8, width), F32),
        ],
        scratch=[
            pltpu.VMEM((3 * columns, width), F32),
            pltpu.VMEM((128, BLOCK), F32),
        ]
        + [pltpu.VMEM(part.shape, part.dtype) for part in inputs[1:]]
        + [pltpu.SemaphoreType.DMA((9,))],
        in_specs=[smem()] + hbm(len(inputs) - 1),
        limit=8,
        tiles=60,
    )
    if ring:
        parts = [
            pair,
            swap(pair, "tensor", 1),
            pair_across,
            swap(after(pair_across, first), "tensor", 1),
        ]
        (own_feed,) = call(
            lambda *refs: assemble_kernel(chunks, *refs),
            (info, *parts),
            [shape((width, BLOCK), BF16)],
            scratch=[pltpu.VMEM((width, BLOCK), F32)],
            in_specs=[smem()] + vmem(chunks),
            limit=6,
            tiles=20,
        )
        came = [swap(own_feed, "dp", e) for e in (2, 4, 6)]
        beside = swap(own_feed, "dp", 1)
        second_beside = swap(came[0], "dp", 1)
        gathered = [gather_four(first, own_feed)]
    else:
        gathered = [gather_four(first)]

    kept = []
    mixed = []
    for g in range(2):
        if g == 1 and ring:
            gathered[1][0] = after(gathered[1][0], duo, beside, second_beside)
        inputs = (info, lengths, *gathered[g], weight, bias, inner_table, outer_table)
        outs = call(
            lambda *refs, g=g: attend_kernel(heads, chunks, chunk, g * half, half, *refs),
            inputs,
            [
                shape((half, 128, chunk), BF16),
                shape((half, 128, chunk), BF16),
                shape((half, 2, 128, chunk), BF16),
            ]
            + [shape((half, heads, HEAD_ROWS, full), BF16)] * 3
            + [
                shape((half, 8, full), F32),
                shape((half, 128, full), F32),
                shape((half, width, full), BF16),
            ],
            scratch=[
                pltpu.VMEM((heads, full, HEAD_ROWS), BF16),
                pltpu.VMEM((8, full), F32),
                pltpu.VMEM((3 * columns, full), F32),
                pltpu.VMEM((half, width, full), BF16),
                pltpu.SemaphoreType.DMA((half,)),
            ],
            in_specs=[smem(), smem()] + vmem(len(inputs) - 2),
            out_specs=vmem(8) + hbm(),
            limit=14,
            tiles=400,
        )
        kept.append(outs[3:])
        mixed.append(outs[:3])
        if g == 0:
            gathered.append(gather_four(second, outs[0]))
            if ring:
                duo = jnp.stack([after(part, outs[0], second_beside) for part in came[1:]])
                duo_beside = swap(duo, "dp", 1)
            else:
                feeds = gather_feed_plain(up_projection_weight, down_projection_weight, core)

    if ring:
        duo_beside = after(duo_beside, kept[1][0])
        feeds = [own_feed, beside, came[0], second_beside, duo, duo_beside]
        feeds += [swap(part, "tensor", 1) for part in feeds]
    feed_outs = []
    for g in range(2):
        last = g == 1
        others = (kept[1][0],) if g == 0 else (feed_outs[0][2],)
        inputs = (
            info,
            hidden,
            given,
            vectors,
            up_bias,
            *spread_four(*mixed[g], *others),
            *gathered[1],
        )
        if last:
            inputs = inputs + tuple(feed_outs[0][5:]) + (feed_outs[0][0],)
        else:
            inputs = inputs + tuple(feeds)
        carried = [
            shape((2, blocks, width, BLOCK), BF16),
            shape((2, blocks, width, BLOCK), F32),
            shape((chunks, 128, width), F32),
            shape((width, 128), F32),
            shape((BLOCK, 128), F32),
        ]
        sent = [
            shape((2, blocks // 2, width, BLOCK), BF16),
            shape((2, blocks // 2, width, BLOCK), BF16),
            shape((144, LANES), BF16),
            shape((2, 144, LANES), BF16),
            shape((144, LANES), BF16),
        ]
        tokens = half * chunk
        outs = call(
            lambda *refs, g=g, last=last: feed_kernel(
                chunks, blocks, g * half, half, last, *refs
            ),
            inputs,
            [
                shape((rows if last else half, width, chunk), BF16),
                shape((half, width, chunk), F32),
                shape((half, 128, chunk), BF16),
                shape((half, 128, chunk), BF16),
                shape((half, 2, 128, chunk), BF16),
            ]
            + (sent if last else carried),
            scratch=[
                pltpu.VMEM((chunks, 128, width), BF16),
                pltpu.VMEM((chunks, 128, tokens), BF16),
                pltpu.VMEM((width, tokens), F32),
                pltpu.VMEM((width, tokens), BF16),
                pltpu.VMEM((width, tokens), BF16),
                pltpu.VMEM((width, tokens), F32),
                pltpu.VMEM((width, tokens), F32),
                pltpu.VMEM((BLOCK, 128), F32),
                pltpu.SemaphoreType.DMA((2, blocks)),
            ],
            in_specs=[smem()]
            + (
                vmem(len(inputs) - 1)
                if last
                else vmem(len(inputs) - 1 - len(feeds)) + hbm(len(feeds))
            ),
            limit=12,
            tiles=500,
        )
        feed_outs.append(outs)
    hidden_out = feed_outs[1][0]
    middle_grads = [outs[1] for outs in feed_outs]
    feed_kept, feed_sent, out_own, out_near, out_cross = feed_outs[1][5:]

    out_came = swap(out_near, "tensor", 1)
    feed_came = swap(feed_sent, "tensor", 1)
    running = None
    reduced = []
    sums = []
    crossing = []
    mixed_grads = [spread_four(*feed_outs[0][2:5], feed_outs[1][2])]
    for r in range(rows):
        last = r == rows - 1
        g = r // half
        inputs = (
            info,
            lengths,
            *mixed_grads[g],
            *kept[g],
            weight_turned,
            inner_table,
            outer_table,
        )
        if r >= 2:
            running = after(running, sums[r - 2])
        if last:
            running = after(running, reduced[2])
        if last and ring:
            running = after(running, *evens)
        if r > 0:
            inputs = inputs + (running,)
        if last:
            inputs = inputs + (out_own, out_came, out_across, weight, vector_rows)
        outs = call(
            lambda *refs, r=r, last=last: attend_back_kernel(
                heads, chunks, chunk, r, r % half, r == 0, last, *refs
            ),
            inputs,
            [
                shape((width, chunk), BF16),
                shape((2, width, chunk), BF16),
                shape((width, chunk), BF16),
            ]
            + (
                [shape((4, 64, LANES), BF16)] * 2 + [shape((8, width), F32)]
                if last
                else [shape((3 * columns, LANES + 128), F32)]
            ),
            scratch=[
                pltpu.VMEM((128, full), BF16),
                pltpu.VMEM((heads, HEAD_ROWS, full), BF16),
                pltpu.VMEM((heads, HEAD_ROWS, full), BF16),
                pltpu.VMEM((heads, full, HEAD_ROWS), BF16),
                pltpu.VMEM((heads, full, HEAD_ROWS), BF16),
                pltpu.VMEM((3, columns, full), F32),
                pltpu.VMEM((3 * columns, full), BF16),
                pltpu.VMEM((512, LANES), F32),
                pltpu.VMEM((width, full), BF16),
                pltpu.SemaphoreType.DMA(()),
            ],
            in_specs=[smem(), smem()] + vmem(9) + hbm() + vmem(len(inputs) - 12),
            limit=12,
            tiles=420,
        )
        near = swap(outs[1], "tensor", 1)
        reduced += [outs[0], near, None]
        if r < half:
            sums.append(add_low(outs[2], near[1]))
            reduced[-1] = swap(sums[-1], "tensor", 2)
        else:
            crossing.append((outs[2], near))
        if last:
            pair_sum = jnp.stack([add_low(cross, near[1]) for cross, near in crossing])
            reduced[-1] = swap(pair_sum, "tensor", 2)
        if last:
            even, odd, norm_sums = outs[3:]
        else:
            running = outs[3]
        if r == 1:
            mixed_grads.append(spread_four(*feed_outs[1][2:5], outs[0]))
        if r == 0:
            out_across = swap(
                add_low(after(out_cross, outs[0]), out_came[1]), "tensor", 2
            )
            if ring:
                feed_odd = swap(
                    add_low(after(feed_kept[1], outs[0]), feed_came[1]), "dp", 1
                )
        if r == 2 and ring:
            feed_kept = after(feed_kept, outs[0])
            evens = [
                add_low(feed_kept[0, i], feed_came[0, i], feed_odd[i]) for i in range(4)
            ]
            feed_came = [swap(evens[i], "dp", 2 * i) for i in (1, 2, 3)]
    if ring:
        keep, send = call(
            feed_sum_kernel,
            (info, after(evens[0], even), *feed_came),
            [shape((width // 2, BLOCK), BF16)] * 2,
            scratch=[pltpu.VMEM((width, BLOCK), F32)],
            in_specs=[smem()] + vmem(4),
            limit=4,
            tiles=20,
        )
        mine, other = call(
            feed_pair_kernel,
            (info, keep, swap(send, "tensor", 2)),
            [shape((columns, BLOCK), BF16)] * 2,
            scratch=[pltpu.VMEM((width // 2, BLOCK), F32)],
            in_specs=[smem()] + vmem(2),
            limit=4,
            tiles=20,
        )
        feed_parts = (mine, swap(other, "tensor", 1))
    else:
        grad_up_weight, grad_down_weight = scatter_feed_plain(
            feed_kept, feed_sent, core, hidden_count
        )

    parts = (sum_pieces if ring else sum_pieces_plain)(even, odd, norm_sums)
    own_parts = [part for place, part in enumerate(reduced) if place % 3 < 2]
    cross_parts = [part for part in reduced[2::3] if part is not None]
    inputs = (hidden, vectors, *middle_grads, *own_parts, *cross_parts)
    (grad_hidden,) = call(
        lambda *refs: norm_back_kernel(rows, *refs),
        inputs,
        [shape((rows, width, chunk), BF16)],
        limit=12,
        tiles=120,
    )
    parts[0] = after(parts[0], grad_hidden)
    inputs = (info, *parts) + (feed_parts if ring else ())
    outs = [
        shape((3, width, columns), F32),
        shape((3, columns), F32),
        shape((columns, width), F32),
    ]
    outs += [shape((1, width), F32)] * 4
    outs += [shape(up_projection_bias.shape, F32)]
    outs += [shape((1, width), F32)] * 2
    if ring:
        outs += [shape((columns, hidden_count), F32), shape((hidden_count, columns), F32)]
    outs = call(
        unpack_kernel,
        inputs,
        outs,
        scratch=[
            pltpu.VMEM((512, LANES), F32),
            pltpu.VMEM((1, up_projection_bias.shape[0]), F32),
        ],
        in_specs=[smem()] + vmem(len(inputs) - 1),
        limit=8,
        tiles=60,
    )
    grad_qkv_weight, grad_qkv_bias, grad_out_weight = outs[:3]
    grad_ffn_gain, grad_ffn_shift, grad_out_bias, grad_down_bias, grad_up_bias = outs[3:8]
    grad_attn_gain, grad_attn_shift = outs[8:10]
    if ring:
        grad_up_weight, grad_down_weight = outs[10:]
    return (
        hidden_out.transpose(0, 2, 1),
        grad_hidden.transpose(0, 2, 1),
        grad_attn_gain[0],
        grad_attn_shift[0],
        grad_qkv_weight,
        grad_qkv_bias,
        grad_out_weight,
        grad_out_bias[0],
        grad_ffn_gain[0],
        grad_ffn_shift[0],
        grad_up_weight,
        grad_up_bias,
        grad_down_weight,
        grad_down_bias[0],
    )


def solution(mesh):
    return jax.shard_map(
        shards,
        mesh=mesh,
        in_specs=(
            P("dp", "tensor", None),
            P(),
            P(),
            P(None, None, "tensor"),
            P(None, "tensor"),
            P("tensor", None),
            P(),
            P(),
            P(),
            P("tensor", "dp"),
            P(),
            P("dp", "tensor"),
            P(),
            P("dp"),
            P("dp", "tensor", None),
        ),
        out_specs=(
            P("dp", "tensor", None),
            P("dp", "tensor", None),
            P(),
            P(),
            P(None, None, "tensor"),
            P(None, "tensor"),
            P("tensor", None),
            P(),
            P(),
            P(),
            P("tensor", "dp"),
            P(),
            P("dp", "tensor"),
            P(),
        ),
        check_vma=False,
    )
```

```python
import math

import jax
import jax.numpy as jnp
import numpy as np
from jax import lax
from jax.experimental import pallas as pl
from jax.experimental.pallas import tpu as pltpu
from jax.sharding import PartitionSpec as P

HEAD_DIM = 24
HEAD_ROWS = 32
EPS = 1e-05
MASK_FILL = -1000000000.0
LOG2E = math.log2(math.e)
SAFE_SCORE = 85.0
WORK_SCALE = 0.01
BLOCK = 256
LANES = 512
BF16 = jnp.bfloat16
F32 = jnp.float32

NN = (((1,), (0,)), ((), ()))
NT = (((1,), (1,)), ((), ()))
TN = (((0,), (0,)), ((), ()))


def product(left, right, dims=NN):
    return lax.dot_general(left, right, dims, preferred_element_type=F32)


def vmem(count):
    return [pl.BlockSpec(memory_space=pltpu.VMEM)] * count


def smem():
    return pl.BlockSpec(memory_space=pltpu.SMEM)


def hbm(count=1):
    return [pl.BlockSpec(memory_space=pltpu.HBM)] * count


def call(kernel, inputs, outs, scratch=(), in_specs=None, out_specs=None, limit=40, tiles=0):
    flops = int(2 * 256**3 * tiles * WORK_SCALE)
    in_specs = vmem(len(inputs)) if in_specs is None else in_specs
    inputs = [
        pltpu.with_memory_space_constraint(part, pltpu.HBM)
        if spec.memory_space is pltpu.HBM
        else part
        for part, spec in zip(inputs, in_specs)
    ]
    out_specs = vmem(len(outs)) if out_specs is None else out_specs
    outs = [
        pltpu.HBM(part.shape, part.dtype) if spec.memory_space is pltpu.HBM else part
        for part, spec in zip(outs, out_specs)
    ]
    return pl.pallas_call(
        kernel,
        out_shape=outs,
        in_specs=in_specs,
        out_specs=out_specs,
        scratch_shapes=list(scratch),
        compiler_params=pltpu.CompilerParams(vmem_limit_bytes=limit << 20),
        cost_estimate=pl.CostEstimate(flops=flops, transcendentals=0, bytes_accessed=0),
    )(*inputs)


def shape(dims, dtype):
    return jax.ShapeDtypeStruct(dims, dtype)


def at_block(index, size):
    return pl.ds(pl.multiple_of(index * size, size), size)


def split_three(values):
    high = values.astype(BF16).astype(F32)
    rest = values - high
    middle = rest.astype(BF16).astype(F32)
    return high, middle, rest - middle


def row_of(lengths, slot, rows):
    chosen = jnp.int32(0)
    for i in range(rows):
        rank = jnp.int32(0)
        for j in range(rows):
            if j < i:
                rank += jnp.where(lengths[j] <= lengths[i], 1, 0)
            elif j > i:
                rank += jnp.where(lengths[j] < lengths[i], 1, 0)
        chosen += jnp.where(rank == slot, i, 0)
    return chosen


def after(values, *others):
    return lax.optimization_barrier((values, *others))[0]


def norm_columns(values):
    centre = values - jnp.mean(values, axis=0, keepdims=True)
    inverse = lax.rsqrt(jnp.mean(centre * centre, axis=0, keepdims=True) + EPS)
    return centre * inverse, inverse


def norm_columns_back(upstream, unit, inverse, gain):
    scaled = upstream * gain
    centred = scaled - jnp.mean(scaled, axis=0, keepdims=True)
    return inverse * (centred - unit * jnp.mean(scaled * unit, axis=0, keepdims=True))


def pair_kernel(info, up, down, pair, up_inside, down_inside, semaphores):
    copies = [
        pltpu.make_async_copy(up, up_inside, semaphores.at[0]),
        pltpu.make_async_copy(down, down_inside, semaphores.at[1]),
    ]
    for copy in copies:
        copy.start()
    pair[...] = jnp.zeros_like(pair)
    for copy in copies:
        copy.wait()
    size = up.shape[1]
    up_half = up_inside[...]
    down_half = down_inside[...].astype(F32).T.astype(BF16)

    @pl.when(info[0] & 1 == 0)
    def _():
        pair[:, :size] = up_half
        pair[:, BLOCK : BLOCK + size] = down_half

    @pl.when(info[0] & 1 == 1)
    def _():
        pair[:, :size] = down_half
        pair[:, BLOCK : BLOCK + size] = up_half


def norm_kernel(
    lengths,
    hidden_in,
    gain,
    shift,
    out_weight_in,
    first_out,
    second_out,
    hidden,
    gain_inside,
    shift_inside,
    out_weight,
    rows_scratch,
    semaphores,
):
    rows, width, chunk = hidden.shape
    copies = [
        pltpu.make_async_copy(
            hidden_in.at[row_of(lengths, slot, rows)], hidden.at[slot], semaphores.at[slot]
        )
        for slot in range(rows)
    ]
    others = [
        pltpu.make_async_copy(gain, gain_inside, semaphores.at[4]),
        pltpu.make_async_copy(shift, shift_inside, semaphores.at[5]),
        pltpu.make_async_copy(out_weight_in, out_weight, semaphores.at[6]),
    ]
    for copy in others[:2] + copies + others[2:]:
        copy.start()
    rows_scratch[...] = jnp.zeros_like(rows_scratch)
    others[0].wait()
    others[1].wait()
    rows_scratch[0:1, :] = gain_inside[...]
    rows_scratch[1:2, :] = shift_inside[...]
    columns = rows_scratch[...].T
    half = rows // 2
    for row in range(rows):
        copies[row].wait()
        unit, _ = norm_columns(hidden[row].astype(F32))
        target = first_out if row < half else second_out
        place = row % half * width
        target[place : place + width, :] = (unit * columns[:, 0:1] + columns[:, 1:2]).astype(
            BF16
        )
    others[2].wait()
    own = out_weight.shape[0]
    second_out[half * width : half * width + own, :] = out_weight[:, :chunk]
    rest = width - chunk
    second_out[half * width + own : half * width + 2 * own, :] = jnp.zeros((own, chunk), BF16)
    second_out[half * width + own : half * width + 2 * own, :rest] = out_weight[:, chunk:]


def prepare_kernel(heads, info, *refs):
    outside, refs = refs[:9], refs[9:]
    weight_out, weight_turned_out, columns_out, bias_out, up_bias_out, vector_rows = refs[:6]
    weight_scratch, bias_rows = refs[6:8]
    inside, semaphores = refs[8:17], refs[17]
    copies = [
        pltpu.make_async_copy(source, target, semaphores.at[place])
        for place, (source, target) in enumerate(zip(outside, inside))
    ]
    for copy in copies:
        copy.start()
    vectors, (up_bias, weight, bias) = inside[:6], inside[6:]
    width = weight.shape[1]
    vector_rows[...] = jnp.zeros_like(vector_rows)
    for copy in copies:
        copy.wait()
    for place, vector in enumerate(vectors):
        vector_rows[place : place + 1, :] = vector[...]
    columns_out[...] = jnp.concatenate([vector_rows[...], jnp.zeros((120, width), F32)]).T
    span = heads * HEAD_DIM
    for c in range(3):
        own = slice(c * span, (c + 1) * span)
        weight_scratch[own, :] = weight[c].astype(F32).T
        bias_out[own, :] = jnp.broadcast_to(bias[c : c + 1, :], (128, span)).T
    weight_out[...] = weight_scratch[...].astype(BF16)
    weight_turned_out[...] = weight_scratch[...].T.astype(BF16)
    bias_rows[...] = jnp.zeros_like(bias_rows)
    count = up_bias.shape[1]
    block = count // 8
    spread = jnp.broadcast_to(up_bias[...], (8, count))
    for j in range(8):
        moved = pltpu.roll(spread, lax.rem(count - (info[1] ^ j) * block, count), 1)
        bias_rows[j : j + 1, :block] = moved[0:1, :block]
    up_bias_out[...] = bias_rows[...].T


def assemble_kernel(chunks, info, *refs):
    parts, (out, rows) = refs[:chunks], refs[chunks:]
    size = parts[0].shape[0]
    for k in range(chunks):
        half = parts[k][:, (k & 1) * BLOCK : ((k & 1) + 1) * BLOCK]
        rows[at_block(info[0] ^ k, size), :] = half.astype(F32)
    out[...] = rows[...].astype(BF16)


def rotary_constants(chunk, chunks):
    half = HEAD_DIM // 2
    element = np.arange(HEAD_DIM)
    frequency = (1.0 / 10000.0 ** (np.arange(0, HEAD_DIM, 2).astype(np.float32) / HEAD_DIM)).astype(
        np.float32
    )
    per_row = frequency[element % half].astype(np.float64)
    inner = per_row[:, None] * np.arange(chunk)[None, :]
    outer = per_row[:, None] * (np.arange(chunks) * chunk)[None, :]
    outer = np.repeat(outer[:, :, None], chunk, axis=2).transpose(1, 0, 2)
    inner_pair = np.stack([np.cos(inner), np.sin(inner)]).astype(np.float32)
    outer_pair = np.stack([np.cos(outer), np.sin(outer)]).astype(np.float32)
    return inner_pair, outer_pair


def chunk_tables(inner, outer, index):
    cos_in, sin_in = inner[0], inner[1]
    cos_out, sin_out = outer[0, index], outer[1, index]
    element = lax.broadcasted_iota(jnp.int32, cos_in.shape, 0)
    sine = sin_in * cos_out + cos_in * sin_out
    return cos_in * cos_out - sin_in * sin_out, jnp.where(
        element < HEAD_DIM // 2, -sine, sine
    )


def swap_halves(values):
    return pltpu.roll(values, HEAD_DIM // 2, 0)


def attend_kernel(heads, chunks, chunk, first_row, rows, info, lengths, *refs):
    parts = refs[:chunks]
    weight, bias, inner, outer, own_out, near_out, cross_out = refs[chunks : chunks + 7]
    queries, keys, values, logsum, mixed_turned, normed_out, key_rows, peak, flat = refs[
        chunks + 7 : chunks + 16
    ]
    normed, semaphores = refs[chunks + 16 :]
    position = info[0]
    width = normed.shape[1]
    full = chunk * chunks
    span = heads * HEAD_DIM
    scale = LOG2E * HEAD_DIM**-0.5
    blocks_full = full // BLOCK

    def one_row(r, carry):
        length = lengths[row_of(lengths, first_row + r, lengths.shape[0])]
        for k in range(chunks):
            normed[r, :, at_block(position ^ k, chunk)] = parts[k][at_block(r, width), :]
        pltpu.make_async_copy(normed.at[r], normed_out.at[r], semaphores.at[r]).start()
        flat[...] = product(weight[...], normed[r])
        line = lax.broadcasted_iota(jnp.int32, (8, chunk), 0)
        ones = jnp.where(line < 3, 1.0, 0.0)
        query_line = jnp.where(line == 3, 1.0, 0.0)
        query_top = [jnp.zeros((1, chunk), F32) for _ in range(heads)]
        key_top = [jnp.zeros((1, chunk), F32) for _ in range(heads)]
        for j in range(chunks):
            at = slice(j * chunk, (j + 1) * chunk)
            cosine, sine = chunk_tables(inner, outer, j)
            query_cosine, query_sine = cosine * scale, sine * scale
            place = lax.broadcasted_iota(jnp.int32, (8, chunk), 1) + j * chunk
            key_line = jnp.where((line == 3) & (place >= length), MASK_FILL, ones)
            for h in range(heads):
                here = h * HEAD_DIM
                query, key, value = (
                    flat[c * span + here : c * span + here + HEAD_DIM, at]
                    + jnp.concatenate(
                        [bias[c * span + here : c * span + here + HEAD_DIM, :]] * (chunk // 128),
                        axis=1,
                    )
                    for c in range(3)
                )
                query = query * query_cosine + swap_halves(query) * query_sine
                key = key * cosine + swap_halves(key) * sine
                query_top[h] = jnp.maximum(
                    query_top[h], jnp.sum(query * query, axis=0, keepdims=True)
                )
                key_top[h] = jnp.maximum(key_top[h], jnp.sum(key * key, axis=0, keepdims=True))
                key_full = jnp.concatenate([key, key_line])
                queries[r, h, :, at] = jnp.concatenate([query, query_line]).astype(BF16)
                keys[r, h, :, at] = key_full.astype(BF16)
                values[r, h, :, at] = jnp.concatenate([value, ones]).astype(BF16)
                key_rows[h, at, :] = key_full.T.astype(BF16)
        bound = jnp.zeros((1, 1), F32)
        for h in range(heads):
            bound = jnp.maximum(
                bound,
                jnp.max(query_top[h], axis=-1, keepdims=True)
                * jnp.max(key_top[h], axis=-1, keepdims=True),
            )
        safe = jnp.max(bound) <= SAFE_SCORE * SAFE_SCORE
        peak[...] = jnp.zeros_like(peak)

        @pl.when(jnp.logical_not(safe))
        def _():
            def one_head(h, carry):
                scores = product(key_rows[h], queries[r, h])
                peak[pl.ds(h, 1), :] = (
                    jnp.max(scores, axis=0, keepdims=True).astype(BF16).astype(F32)
                )
                return carry

            lax.fori_loop(0, heads, one_head, 0)

        head_line = lax.broadcasted_iota(jnp.int32, (HEAD_ROWS, full), 0)

        def with_keys(count):
            def one_head(h, carry):
                top = peak[pl.ds(h, 1), :]
                query = jnp.where(
                    head_line == HEAD_DIM, -top, queries[r, h].astype(F32)
                ).astype(BF16)
                exponent = jnp.exp2(product(key_rows[h, :count, :], query)).astype(BF16)
                blend = product(values[r, h, :, :count], exponent)
                total = blend[HEAD_DIM : HEAD_DIM + 1, :]
                logsum[r, pl.ds(h, 1), :] = top + jnp.log2(total)
                mixed_turned[r, pl.ds(pl.multiple_of(h * HEAD_DIM, 8), HEAD_DIM), :] = blend[
                    :HEAD_DIM
                ] * (1.0 / total)
                return carry

            lax.fori_loop(0, heads, one_head, 0, unroll=True)

        blocks = (length + BLOCK - 1) // BLOCK
        for b in range(1, blocks_full + 1):
            pl.when(blocks == b)(lambda b=b: with_keys(b * BLOCK))
        mixed_turned[r, span:, :] = jnp.zeros((mixed_turned.shape[1] - span, full), F32)
        own_out[r] = mixed_turned[r, :, at_block(position, chunk)].astype(BF16)
        near_out[r] = mixed_turned[r, :, at_block(position ^ 1, chunk)].astype(BF16)
        cross_out[r, 0] = mixed_turned[r, :, at_block(position ^ 2, chunk)].astype(BF16)
        cross_out[r, 1] = mixed_turned[r, :, at_block(position ^ 3, chunk)].astype(BF16)
        return carry

    lax.fori_loop(0, rows, one_row, 0)
    for r in range(rows):
        pltpu.make_async_copy(normed.at[r], normed_out.at[r], semaphores.at[r]).wait()


def attend_back_kernel(heads, chunks, chunk, row, local, first, last, info, lengths, *refs):
    upstream_own, upstream_near, upstream_cross, upstream_far = refs[:4]
    queries, keys, values, logsum, mixed_turned, normed_in, weight_turned, inner, outer = refs[
        4:13
    ]
    refs = refs[13:]
    if not first:
        carried = refs[0]
        refs = refs[1:]
    if last:
        out_own, out_near, out_cross, weight, vector_rows = refs[:5]
        refs = refs[5:]
    own_out, near_out, cross_out = refs[:3]
    refs = refs[3:]
    if last:
        even_pieces, odd_pieces, norm_sums = refs[:3]
        refs = refs[3:]
    else:
        running = refs[0]
        refs = refs[1:]
    (
        upstream,
        query_full,
        upstream_full,
        key_rows,
        value_rows,
        grads,
        grad_low,
        packed,
        normed,
        semaphore,
    ) = refs
    fetch = pltpu.make_async_copy(normed_in.at[local], normed, semaphore)
    fetch.start()
    position, index = info[0], info[1]
    length = lengths[row_of(lengths, row, lengths.shape[0])]
    full = chunk * chunks
    span = heads * HEAD_DIM
    upstream[:, at_block(position, chunk)] = upstream_own[local]
    upstream[:, at_block(position ^ 1, chunk)] = upstream_near[local]
    upstream[:, at_block(position ^ 2, chunk)] = upstream_cross[local, 0]
    upstream[:, at_block(position ^ 3, chunk)] = upstream_far[local, 1]
    zeros = jnp.zeros((5, chunk), F32)
    line = lax.broadcasted_iota(jnp.int32, (8, chunk), 0)
    for j in range(chunks):
        at = slice(j * chunk, (j + 1) * chunk)
        turned = upstream[:, at].astype(F32)
        blend = turned * mixed_turned[local, :, at]
        for h in range(heads):
            own = slice(h * HEAD_DIM, (h + 1) * HEAD_DIM)
            high, middle, rest = split_three(-jnp.sum(blend[own], axis=0, keepdims=True))
            extra = jnp.where(
                line == 0, high, jnp.where(line == 1, middle, jnp.where(line == 2, rest, 0.0))
            )
            upstream_full[h, :, at] = jnp.concatenate([turned[own], extra]).astype(BF16)
            high, middle, rest = split_three(-logsum[local, h : h + 1, at])
            extra = jnp.where(
                line == 0,
                high,
                jnp.where(
                    line == 1, middle, jnp.where(line == 2, rest, jnp.where(line == 3, 1.0, 0.0))
                ),
            )
            query = queries[local, h, :, at].astype(F32)[:HEAD_DIM]
            query_full[h, :, at] = jnp.concatenate([query, extra]).astype(BF16)
            key_rows[h, at, :] = keys[local, h, :, at].astype(F32).T.astype(BF16)
            value_rows[h, at, :] = values[local, h, :, at].astype(F32).T.astype(BF16)

    def with_keys(count):
        def one_head(h, carry):
            own = pl.ds(pl.multiple_of(h * HEAD_DIM, 8), HEAD_DIM)
            grad_query = jnp.zeros((HEAD_ROWS, full), F32)
            for b in range(count // BLOCK):
                at = slice(b * BLOCK, (b + 1) * BLOCK)
                probs = jnp.exp2(product(key_rows[h, at, :], query_full[h])).astype(BF16)
                grad_probs = product(value_rows[h, at, :], upstream_full[h]).astype(BF16)
                grad_scores = probs * grad_probs
                grads[2, own, at] = product(upstream_full[h], probs, NT)[:HEAD_DIM]
                grads[1, own, at] = product(query_full[h], grad_scores, NT)[:HEAD_DIM]
                grad_query += product(keys[local, h, :, at], grad_scores)
            grads[0, own, :] = grad_query[:HEAD_DIM]
            return carry

        lax.fori_loop(0, heads, one_head, 0)
        if count < full:
            grads[1, :, count:] = jnp.zeros((span, full - count), F32)
            grads[2, :, count:] = jnp.zeros((span, full - count), F32)

    blocks = (length + BLOCK - 1) // BLOCK
    for b in range(1, full // BLOCK + 1):
        pl.when(blocks == b)(lambda b=b: with_keys(b * BLOCK))

    sums = [[jnp.zeros((HEAD_DIM, 128), F32) for _ in range(heads)] for _ in range(3)]
    for j in range(chunks):
        at = slice(j * chunk, (j + 1) * chunk)
        cosine, sine = chunk_tables(inner, outer, j)
        query_cosine, query_sine = cosine * HEAD_DIM**-0.5, sine * HEAD_DIM**-0.5
        key_cosine, key_sine = cosine * (1.0 / LOG2E), sine * (1.0 / LOG2E)
        for h in range(heads):
            own = slice(h * HEAD_DIM, (h + 1) * HEAD_DIM)
            query, key, value = (grads[c, own, at] for c in range(3))
            query = query * query_cosine - swap_halves(query) * query_sine
            key = key * key_cosine - swap_halves(key) * key_sine
            for c, part in enumerate((query, key, value)):
                for piece in range(chunk // 128):
                    sums[c][h] = sums[c][h] + part[:, piece * 128 : (piece + 1) * 128]
                grads[c, own, at] = part
    for c in range(3):
        grad_low[c * span : (c + 1) * span, :] = grads[c].astype(BF16)
    for k in range(chunks):
        result = product(
            weight_turned[...], grad_low[:, at_block(position ^ k, chunk)]
        ).astype(BF16)
        if k == 0:
            own_out[...] = result
        elif k == 2:
            cross_out[...] = result
        else:
            near_out[k // 2] = result
    width = weight_turned.shape[0]
    fetch.wait()
    result = product(grad_low[...], normed[...], NT)
    bias_grad = jnp.concatenate(
        [jnp.sum(part, axis=1, keepdims=True) for group in sums for part in group]
    )
    bias_grad = jnp.broadcast_to(bias_grad, (3 * span, 128))
    if not first:
        result = result + carried[:, :width]
        bias_grad = bias_grad + carried[:, LANES:]
    if not last:
        running[:, :width] = result
        running[:, LANES:] = bias_grad
        return
    packed[: 3 * span, :width] = result
    gain_sum = jnp.zeros((8, width), F32)
    shift_sum = jnp.zeros((8, width), F32)
    gain, shift = vector_rows[0:1, :], vector_rows[1:2, :]
    for place in range(0, 3 * span, 8):
        own = slice(place, place + 8)
        factor = weight[own, :].astype(F32)
        column = bias_grad[own, 0:1]
        gain_sum = gain_sum + factor * (result[own] - shift * column)
        shift_sum = shift_sum + factor * column
    norm_sums[...] = jnp.zeros_like(norm_sums)
    norm_sums[0:1, :] = jnp.sum(gain_sum, axis=0, keepdims=True) / gain
    norm_sums[1:2, :] = jnp.sum(shift_sum, axis=0, keepdims=True)
    lane = lax.broadcasted_iota(jnp.int32, (3 * span, 128), 1)
    packed[: 3 * span, LANES - 128 :] = jnp.where(
        lane >= width - (LANES - 128), bias_grad, packed[: 3 * span, LANES - 128 :]
    )
    shared = (out_own[...].astype(F32) + out_near[0].astype(F32)) + out_cross[...].astype(F32)
    packed[3 * span : 4 * span, :] = shared[:span]
    packed[4 * span : 4 * span + 16, :] = shared[128:144]
    packed[4 * span + 16 :, :] = jnp.zeros((packed.shape[0] - 4 * span - 16, LANES), F32)
    size = packed.shape[0] // 8
    for j in range(8):
        target = odd_pieces if j % 2 else even_pieces
        target[j // 2] = packed[at_block(index ^ j, size), :].astype(BF16)


def gelu_parts(values):
    magnitude = jnp.abs(values) * (0.5**0.5)
    density = jnp.exp2(values * values * (-0.5 * LOG2E))
    step = 1.0 / (1.0 + 0.3275911 * magnitude)
    series = 1.061405429 * step - 1.453152027
    series = series * step + 1.421413741
    series = series * step - 0.284496736
    series = series * step + 0.254829592
    tail = 0.5 * series * step * density
    share = jnp.where(values < 0, tail, 1.0 - tail)
    return share, density * (1.0 / math.sqrt(2.0 * math.pi))


def lane_groups(values):
    total = values[:, :128]
    for place in range(128, values.shape[1], 128):
        total = total + values[:, place : place + 128]
    return total


def row_sum(values):
    total = values[:8]
    for place in range(8, values.shape[0], 8):
        total = total + values[place : place + 8]
    return total


def feed_kernel(chunks, blocks, first_row, rows, last, info, lengths, *refs):
    hidden, cotangent, columns, up_bias = refs[:4]
    mixed_own, mixed_near, mixed_cross, mixed_far = refs[4:8]
    out_weight = refs[8 : 8 + chunks]
    refs = refs[8 + chunks :]
    if last:
        weights, carried, out_carried, sums_carried, bias_carried, hidden_before = refs[:6]
        refs = refs[6:]
    else:
        feeds, refs = refs[:12], refs[12:]
    hidden_out, grad_middle_out, grad_own, grad_near, grad_cross = refs[:5]
    refs = refs[5:]
    if last:
        kept_out, sent_out, out_own, out_near, out_cross = refs[:5]
    else:
        weights, carried, out_carried, sums_carried, bias_carried = refs[:5]
    refs = refs[5:]
    (
        out_rows,
        mixed,
        source,
        given,
        low_rows,
        down_total,
        back_total,
        upward,
        upstream,
        active,
        grad_low,
        sums_total,
        bias_total,
        shared,
        semaphores,
    ) = refs
    core, index = info[0] & 1, info[1]
    width, chunk = hidden.shape[1:]
    tokens = rows * chunk
    held = mixed_own.shape[1]
    places = [row_of(lengths, first_row + r, hidden.shape[0]) for r in range(rows)]
    if not last:
        copies = []
        for side in range(2):
            sources = list(feeds[6 * side : 6 * side + 4])
            duo, duo_beside = feeds[6 * side + 4 : 6 * side + 6]
            place = core if side == 0 else 1 - core
            for e in range(2):
                sources += [duo.at[e], duo_beside.at[e]]
            for j in range(blocks):
                copies.append(
                    pltpu.make_async_copy(
                        sources[j], weights.at[place, j], semaphores.at[side, j]
                    )
                )
        for copy in copies:
            copy.start()
    own_rows = (out_weight[0].shape[0] - 2 * width) // 2
    for k in range(chunks):
        base = 2 * width
        at = k * held
        out_rows[at : at + held, :] = jnp.zeros((held, width), BF16)
        out_rows[at : at + own_rows, :chunk] = out_weight[k][base : base + own_rows, :]
        out_rows[at : at + own_rows, chunk:] = out_weight[k][
            base + own_rows : base + 2 * own_rows, : width - chunk
        ]
    for r in range(rows):
        at = slice(r * chunk, (r + 1) * chunk)
        mixed[0 * held : 1 * held, at] = mixed_own[r]
        mixed[1 * held : 2 * held, at] = mixed_near[r]
        mixed[2 * held : 3 * held, at] = mixed_cross[r, 0]
        mixed[3 * held : 4 * held, at] = mixed_far[r, 1]
        given[:, at] = cotangent[places[r]]
    source[...] = product(out_rows[...], mixed[...], TN)
    step = 32
    pieces = [slice(place, place + step) for place in range(0, width, step)]

    total = jnp.zeros((8, tokens), F32)
    for own in pieces:
        entered = jnp.concatenate([hidden[places[r], own, :] for r in range(rows)], axis=1)
        middle = source[own, :] + entered.astype(F32) + columns[own, 2:3]
        source[own, :] = middle
        total = total + row_sum(middle)
    mean = jnp.sum(total, axis=0, keepdims=True) * (1.0 / width)
    total = jnp.zeros((8, tokens), F32)
    for own in pieces:
        centre = source[own, :] - mean
        total = total + row_sum(centre * centre)
    inverse = lax.rsqrt(jnp.sum(total, axis=0, keepdims=True) * (1.0 / width) + EPS)
    for own in pieces:
        middle = source[own, :]
        unit = (middle - mean) * inverse
        low_rows[own, :] = (unit * columns[own, 3:4] + columns[own, 4:5]).astype(BF16)
        down_total[own, :] = middle + columns[own, 5:6]
        source[own, :] = unit
    back_total[...] = jnp.zeros_like(back_total)
    if not last:
        for copy in copies:
            copy.wait()

    def enter(j, slot):
        upward[slot] = product(weights[0, j], low_rows[...], TN)
        upstream[slot] = product(weights[1, j], given[...], TN)

    lane = lax.broadcasted_iota(jnp.int32, (step, 128), 1)

    def bend(j, slot):
        for place in range(0, BLOCK, step):
            own = slice(place, place + step)
            bias = jnp.sum(jnp.where(lane == j, up_bias[own, :], 0.0), axis=1, keepdims=True)
            values = upward[slot, own, :] + bias
            share, density = gelu_parts(values)
            active[slot, own, :] = (values * share).astype(BF16)
            grad_up = upstream[slot, own, :] * (share + values * density)
            grad_low[slot, own, :] = grad_up.astype(BF16)
            bias_sum = lane_groups(grad_up)
            if last:
                bias_total[j, own, :] = bias_sum + bias_carried[j, own, :]
            else:
                bias_carried[j, own, :] = bias_sum

    def leave(j, slot):
        down_total[...] += product(weights[1, j], active[slot])
        back_total[...] += product(weights[0, j], grad_low[slot])
        up_grad = product(low_rows[...], grad_low[slot], NT)
        down_grad = product(given[...], active[slot], NT)
        if not last:
            carried[0, j] = up_grad
            carried[1, j] = down_grad
            return
        up_grad = (up_grad + carried[0, j]).astype(BF16)
        down_grad = (down_grad + carried[1, j]).astype(BF16)
        place = j >> 1

        @pl.when(core == 0)
        def _():
            kept_out[slot, place] = up_grad
            sent_out[slot, place] = down_grad

        @pl.when(core == 1)
        def _():
            kept_out[slot, place] = down_grad
            sent_out[slot, place] = up_grad

    def two_blocks(i, carry):
        j = 2 * i
        enter(j + 1, 1)
        bend(j, 0)
        leave(j, 0)
        enter(lax.rem(j + 2, blocks), 0)
        bend(j + 1, 1)
        leave(j + 1, 1)
        return carry

    enter(0, 0)
    lax.fori_loop(0, blocks // 2, two_blocks, 0)
    if last:
        for r in range(first_row):
            hidden_out[row_of(lengths, r, hidden.shape[0])] = hidden_before[r]
    for r in range(rows):
        place = places[r] if last else r
        hidden_out[place] = down_total[:, r * chunk : (r + 1) * chunk].astype(BF16)
    scaled_total = jnp.zeros((8, tokens), F32)
    unit_total = jnp.zeros((8, tokens), F32)
    for own in pieces:
        scaled = back_total[own, :] * columns[own, 3:4]
        scaled_total = scaled_total + row_sum(scaled)
        unit_total = unit_total + row_sum(scaled * source[own, :])
    scaled_mean = jnp.sum(scaled_total, axis=0, keepdims=True) * (1.0 / width)
    unit_mean = jnp.sum(unit_total, axis=0, keepdims=True) * (1.0 / width)
    for own in pieces:
        back, unit = back_total[own, :], source[own, :]
        given_wide = given[own, :].astype(F32)
        scaled = back * columns[own, 3:4]
        grad_middle = given_wide + inverse * (scaled - scaled_mean - unit * unit_mean)
        for r in range(rows):
            grad_middle_out[r, own, :] = grad_middle[:, r * chunk : (r + 1) * chunk]
        low_rows[own, :] = grad_middle.astype(BF16)
        for place, part in enumerate((back * unit, back, grad_middle, given_wide)):
            part = lane_groups(part)
            if last:
                sums_total[place, own, :] = part + sums_carried[place, own, :]
            else:
                sums_carried[place, own, :] = part
    mixed_grad = product(out_rows[...], low_rows[...]).astype(BF16)
    for r in range(rows):
        at = slice(r * chunk, (r + 1) * chunk)
        grad_own[r] = mixed_grad[:held, at]
        grad_near[r] = mixed_grad[held : 2 * held, at]
        grad_cross[r, 0] = mixed_grad[2 * held : 3 * held, at]
        grad_cross[r, 1] = mixed_grad[3 * held :, at]
    out_part = product(mixed[...], low_rows[...], NT)
    if not last:
        out_carried[...] = out_part
        return
    out_part = (out_part + out_carried[...]).astype(BF16)
    shared[...] = jnp.zeros_like(shared)
    for place in range(4):
        line = row_sum(sums_total[place].T)
        shared[place : place + 1, :width] = jnp.sum(line, axis=0, keepdims=True)
    for j in range(blocks):
        line = row_sum(bias_total[j].T)
        shared[pl.ds(4 + (index ^ j), 1), :BLOCK] = jnp.sum(line, axis=0, keepdims=True)
    shared_low = shared[...].astype(BF16)
    for k, target in enumerate((out_own, out_near.at[0], out_cross, out_near.at[1])):
        target[:held, 384:] = jnp.zeros((held, LANES - 384), BF16)
        target[:held, :width] = out_part[k * held : (k + 1) * held]
        target[held:, :] = shared_low


def norm_back_kernel(rows, lengths, hidden, columns, *refs):
    middle_grads, refs = refs[:2], refs[2:]
    own_parts, near_parts = refs[0 : 2 * rows : 2], refs[1 : 2 * rows : 2]
    cross_parts, (out,) = refs[2 * rows : 3 * rows - 1], refs[3 * rows - 1 :]
    cross_parts = list(cross_parts[:-1]) + [cross_parts[-1].at[0], cross_parts[-1].at[1]]
    gain = columns[:, 0:1]
    for row in range(rows):
        place = row_of(lengths, row, rows)
        unit, inverse = norm_columns(hidden[place].astype(F32))
        grad = (
            own_parts[row][...].astype(F32)
            + near_parts[row][0].astype(F32)
            + cross_parts[row][...].astype(F32)
        )
        half = rows // 2
        result = middle_grads[row // half][row % half] + norm_columns_back(
            grad, unit, inverse, gain
        )
        out[place] = result.astype(BF16)


def add_pieces_kernel(even, beside, *outs):
    for i, out in enumerate(outs):
        out[...] = (even[i].astype(F32) + beside[i].astype(F32)).astype(BF16)


def own_piece_kernel(first, second, fourth, sixth, norm_sums, out):
    size = first.shape[0]
    total = first[...].astype(F32) + second[...].astype(F32)
    total = total + fourth[...].astype(F32) + sixth[...].astype(F32)
    out[:size, :] = total.astype(BF16)
    width = norm_sums.shape[1]
    values = norm_sums[...]
    high = values.astype(BF16)
    rest = (values - high.astype(F32)).astype(BF16)
    out[size:, 384:] = jnp.zeros((16, LANES - 384), BF16)
    out[size:, :width] = jnp.concatenate([high.astype(F32), rest.astype(F32)]).astype(BF16)


def feed_sum_kernel(info, first, second, fourth, sixth, keep, send, rows):
    total = first[...].astype(F32) + second[...].astype(F32)
    rows[...] = total + fourth[...].astype(F32) + sixth[...].astype(F32)
    size = keep.shape[0]
    chip = info[0] >> 1
    keep[...] = rows[at_block(chip, size), :].astype(BF16)
    send[...] = rows[at_block(1 - chip, size), :].astype(BF16)


def feed_pair_kernel(info, kept, came, mine, other, rows):
    rows[...] = kept[...].astype(F32) + came[...].astype(F32)
    size = mine.shape[0]
    core = info[0] & 1
    mine[...] = rows[at_block(core, size), :].astype(BF16)
    other[...] = rows[at_block(1 - core, size), :].astype(BF16)


def unpack_kernel(info, *refs):
    evens, beside = refs[:4], refs[4]
    refs = refs[5:]
    if len(refs) > 12:
        mine, came, refs = refs[0], refs[1], refs[2:]
        up_grad, down_grad = refs[10:12]
        refs = refs[:10] + refs[12:]
        count = up_grad.shape[1]

        def write(up, down):
            up_grad[...] = up[:, :count].astype(F32)
            down_grad[...] = down[...].astype(F32).T[:count, :]

        pl.when(info[0] & 1 == 0)(lambda: write(mine, came))
        pl.when(info[0] & 1 == 1)(lambda: write(came, mine))
    weight_grad, bias_grad, out_grad, gain, shift, out_bias, down_bias, up_bias = refs[:8]
    norm_gain, norm_shift, whole, line = refs[8:]
    size = whole.shape[0] // 8
    width = weight_grad.shape[1]
    norms = [evens[0][size:, :].astype(F32) + beside[0, size:, :].astype(F32)]
    for i in range(4):
        whole[at_block(info[1] ^ (2 * i), size), :] = evens[i][:size, :].astype(F32)
        whole[at_block(info[1] ^ (2 * i + 1), size), :] = beside[i, :size, :].astype(F32)
        if i > 0:
            norms.append(evens[i][size:, :].astype(F32) + beside[i, size:, :].astype(F32))
    norms = (norms[0] + norms[1]) + (norms[2] + norms[3])
    norms = norms[:8] + norms[8:16]
    norm_gain[...] = norms[0:1, :width]
    norm_shift[...] = norms[1:2, :width]
    columns = weight_grad.shape[2]
    for c in range(3):
        turned = whole[c * columns : (c + 1) * columns, :].T
        weight_grad[c] = turned[:width, :]
        bias_grad[c : c + 1, :] = turned[width : width + 1, :]
    out_grad[...] = whole[3 * columns : 4 * columns, :width]
    for place, target in enumerate((gain, shift, out_bias, down_bias)):
        target[...] = whole[4 * columns + place : 4 * columns + place + 1, :width]
    block = up_bias.shape[0] // 8
    for j in range(8):
        line[:, j * block : (j + 1) * block] = whole[
            4 * columns + 4 + j : 4 * columns + 5 + j, :block
        ]
    up_bias[...] = line[0, :]


def swap(values, axis, bit):
    size = lax.axis_size(axis)
    return lax.ppermute(values, axis, [(i, i ^ bit) for i in range(size)])


def gather_four(own, *others):
    beside = swap(own, "tensor", 1)
    across = swap(own, "tensor", 2)
    return [own, beside, across, swap(after(across, *others), "tensor", 1)]


def spread_four(own, near, cross, *others):
    beside = swap(near, "tensor", 1)
    across = swap(cross, "tensor", 2)
    return [own, beside, across, swap(after(across, *others), "tensor", 1)]


def add_low(*parts):
    total = parts[0].astype(F32)
    for part in parts[1:]:
        total = total + part.astype(F32)
    return total.astype(BF16)


def gather_feed_plain(up, down, core):
    pair = jnp.stack([up, down.T])
    pair = lax.all_gather(pair, "tensor", axis=1, tiled=True)
    pair = lax.all_gather(pair, "dp", axis=2, tiled=True)
    pair = pair.reshape(2, pair.shape[1], 8, -1).transpose(0, 2, 1, 3)
    pair = jnp.pad(pair, ((0, 0), (0, 0), (0, 0), (0, BLOCK - pair.shape[3])))
    pair = jnp.where(core == 0, pair, pair[::-1])
    feeds = []
    for half in (pair[0], pair[1]):
        feeds += [half[0], half[1], half[2], half[3], half[4::2], half[5::2]]
    return feeds


def scatter_feed_plain(kept, sent, core, hidden_count):
    grads = jnp.stack([kept, sent]).swapaxes(1, 2).reshape(2, 8, *kept.shape[2:])
    grads = jnp.where(core == 0, grads, grads[::-1]).astype(F32)
    grads = grads[:, :, :, : hidden_count * lax.axis_size("dp") // 8]
    grads = grads.transpose(0, 2, 1, 3).reshape(2, grads.shape[2], -1)
    grads = lax.psum_scatter(grads, "dp", scatter_dimension=2, tiled=True)
    grads = lax.psum_scatter(grads, "tensor", scatter_dimension=1, tiled=True)
    return grads[0], grads[1].T


def sum_pieces(even, odd, norm_sums, crossed, grad_hidden):
    parts = call(
        add_pieces_kernel,
        (even, swap(odd, "dp", 1)),
        [shape(even.shape[1:], BF16)] * 4,
        limit=4,
    )
    parts = [parts[0]] + [swap(parts[i], "dp", 2 * i) for i in (1, 2, 3)]
    norm_sums = norm_sums + after(swap(norm_sums, "tensor", 2), parts[0])
    norm_sums = norm_sums + swap(norm_sums, "tensor", 1)
    norm_sums = after(norm_sums, crossed)
    (own,) = call(
        own_piece_kernel,
        (*parts, norm_sums),
        [shape((even.shape[1] + 16, LANES), BF16)],
        limit=4,
    )
    back = [own] + [swap(own, "dp", e) for e in (2, 4, 6)]
    return back + [swap(after(jnp.stack(back), grad_hidden), "dp", 1)], own


def sum_pieces_plain(even, odd, norm_sums):
    even, odd = (lax.psum(part.astype(F32), "dp").astype(BF16) for part in (even, odd))
    norm_sums = lax.psum(norm_sums, ("dp", "tensor"))
    high = norm_sums.astype(BF16)
    rest = (norm_sums - high.astype(F32)).astype(BF16)
    rows = jnp.concatenate([high, rest])
    rows = jnp.pad(rows, ((0, 0), (0, LANES - rows.shape[1])))
    even = jnp.concatenate([even, jnp.stack([rows] + [jnp.zeros_like(rows)] * 3)], axis=1)
    odd = jnp.concatenate([odd, jnp.zeros((4, *rows.shape), BF16)], axis=1)
    return [even[i] for i in range(4)] + [odd]


def shards(
    hidden_in,
    attn_gain,
    attn_shift,
    query_key_value_weight,
    query_key_value_bias,
    attention_output_weight,
    out_bias,
    ffn_gain,
    ffn_shift,
    up_projection_weight,
    up_projection_bias,
    down_projection_weight,
    down_bias,
    lengths,
    cotangent,
):
    chunks = lax.axis_size("tensor")
    ring = lax.axis_size("dp") == 8
    position = lax.axis_index("tensor")
    index = lax.axis_index("dp") if ring else jnp.int32(0)
    core = position & 1
    rows, chunk, width = hidden_in.shape
    full = chunk * chunks
    columns = query_key_value_weight.shape[2]
    heads = columns // HEAD_DIM
    hidden_count = up_projection_weight.shape[1]
    blocks = 8
    half = rows // 2

    info = jnp.stack([position, index]).astype(jnp.int32)
    lengths = lengths.astype(jnp.int32)
    inner_table, outer_table = (jnp.asarray(table) for table in rotary_constants(chunk, chunks))
    hidden = hidden_in.transpose(0, 2, 1)
    given = cotangent.transpose(0, 2, 1)

    if ring:
        inputs = (info, up_projection_weight, down_projection_weight)
        (pair,) = call(
            pair_kernel,
            inputs,
            [shape((columns, 2 * BLOCK), BF16)],
            scratch=[pltpu.VMEM(part.shape, part.dtype) for part in inputs[1:]]
            + [pltpu.SemaphoreType.DMA((2,))],
            in_specs=[smem()] + hbm(2),
            limit=4,
            tiles=20,
        )
        pair_across = swap(pair, "tensor", 2)
    inputs = (
        lengths,
        after(hidden, pair) if ring else hidden,
        attn_gain[None],
        attn_shift[None],
        attention_output_weight,
    )
    first, second = call(
        norm_kernel,
        inputs,
        [
            shape((half * width, chunk), BF16),
            shape((half * width + 2 * columns, chunk), BF16),
        ],
        scratch=[pltpu.VMEM(part.shape, part.dtype) for part in inputs[1:]]
        + [pltpu.VMEM((128, width), F32), pltpu.SemaphoreType.DMA((8,))],
        in_specs=[smem()] + hbm(4),
        limit=8,
        tiles=80,
    )
    inputs = (
        info,
        attn_gain[None],
        attn_shift[None],
        out_bias[None],
        ffn_gain[None],
        ffn_shift[None],
        down_bias[None],
        up_projection_bias[None],
        query_key_value_weight,
        query_key_value_bias,
    )
    weight, weight_turned, vectors, bias, up_bias, vector_rows = call(
        lambda *refs: prepare_kernel(heads, *refs),
        inputs,
        [
            shape((3 * columns, width), BF16),
            shape((width, 3 * columns), BF16),
            shape((width, 128), F32),
            shape((3 * columns, 128), F32),
            shape((BLOCK, 128), F32),
            shape((8, width), F32),
        ],
        scratch=[
            pltpu.VMEM((3 * columns, width), F32),
            pltpu.VMEM((128, BLOCK), F32),
        ]
        + [pltpu.VMEM(part.shape, part.dtype) for part in inputs[1:]]
        + [pltpu.SemaphoreType.DMA((9,))],
        in_specs=[smem()] + hbm(len(inputs) - 1),
        limit=8,
        tiles=60,
    )
    if ring:
        parts = [
            pair,
            swap(pair, "tensor", 1),
            pair_across,
            swap(after(pair_across, first), "tensor", 1),
        ]
        (own_feed,) = call(
            lambda *refs: assemble_kernel(chunks, *refs),
            (info, *parts),
            [shape((width, BLOCK), BF16)],
            scratch=[pltpu.VMEM((width, BLOCK), F32)],
            in_specs=[smem()] + vmem(chunks),
            limit=6,
            tiles=20,
        )
        came = [swap(own_feed, "dp", e) for e in (2, 4, 6)]
        beside = swap(own_feed, "dp", 1)
        second_beside = swap(came[0], "dp", 1)
        gathered = [gather_four(after(first, pair_across), own_feed, came[0], beside)]
    else:
        gathered = [gather_four(first)]

    kept = []
    mixed = []
    for g in range(2):
        if g == 1 and ring:
            gathered[1][0] = after(gathered[1][0], duo, beside, second_beside)
        inputs = (info, lengths, *gathered[g], weight, bias, inner_table, outer_table)
        outs = call(
            lambda *refs, g=g: attend_kernel(heads, chunks, chunk, g * half, half, *refs),
            inputs,
            [
                shape((half, 128, chunk), BF16),
                shape((half, 128, chunk), BF16),
                shape((half, 2, 128, chunk), BF16),
            ]
            + [shape((half, heads, HEAD_ROWS, full), BF16)] * 3
            + [
                shape((half, 8, full), F32),
                shape((half, 128, full), F32),
                shape((half, width, full), BF16),
            ],
            scratch=[
                pltpu.VMEM((heads, full, HEAD_ROWS), BF16),
                pltpu.VMEM((8, full), F32),
                pltpu.VMEM((3 * columns, full), F32),
                pltpu.VMEM((half, width, full), BF16),
                pltpu.SemaphoreType.DMA((half,)),
            ],
            in_specs=[smem(), smem()] + vmem(len(inputs) - 2),
            out_specs=vmem(8) + hbm(),
            limit=14,
            tiles=400,
        )
        kept.append(outs[3:])
        mixed.append(outs[:3])
        if g == 0:
            gathered.append(gather_four(second, outs[0]))
            if ring:
                duo = jnp.stack([after(part, outs[0], second_beside) for part in came[1:]])
                duo_beside = swap(duo, "dp", 1)
            else:
                feeds = gather_feed_plain(up_projection_weight, down_projection_weight, core)

    if ring:
        duo_beside = after(duo_beside, kept[1][0])
        feeds = [own_feed, beside, came[0], second_beside, duo, duo_beside]
        feeds += [swap(part, "tensor", 1) for part in feeds]
    feed_outs = []
    for g in range(2):
        last = g == 1
        others = (kept[1][0],) if g == 0 else (feed_outs[0][2],)
        inputs = (
            info,
            lengths,
            hidden,
            given,
            vectors,
            up_bias,
            *spread_four(*mixed[g], *others),
            *gathered[1],
        )
        if last:
            inputs = inputs + tuple(feed_outs[0][5:]) + (feed_outs[0][0],)
        else:
            inputs = inputs + tuple(feeds)
        carried = [
            shape((2, blocks, width, BLOCK), BF16),
            shape((2, blocks, width, BLOCK), F32),
            shape((chunks * 128, width), F32),
            shape((4, width, 128), F32),
            shape((blocks, BLOCK, 128), F32),
        ]
        sent = [
            shape((2, blocks // 2, width, BLOCK), BF16),
            shape((2, blocks // 2, width, BLOCK), BF16),
            shape((144, LANES), BF16),
            shape((2, 144, LANES), BF16),
            shape((144, LANES), BF16),
        ]
        tokens = half * chunk
        outs = call(
            lambda *refs, g=g, last=last: feed_kernel(
                chunks, blocks, g * half, half, last, *refs
            ),
            inputs,
            [
                shape((rows if last else half, width, chunk), BF16),
                shape((half, width, chunk), F32),
                shape((half, 128, chunk), BF16),
                shape((half, 128, chunk), BF16),
                shape((half, 2, 128, chunk), BF16),
            ]
            + (sent if last else carried),
            scratch=[
                pltpu.VMEM((chunks * 128, width), BF16),
                pltpu.VMEM((chunks * 128, tokens), BF16),
                pltpu.VMEM((width, tokens), F32),
                pltpu.VMEM((width, tokens), BF16),
                pltpu.VMEM((width, tokens), BF16),
                pltpu.VMEM((width, tokens), F32),
                pltpu.VMEM((width, tokens), F32),
                pltpu.VMEM((2, BLOCK, tokens), F32),
                pltpu.VMEM((2, BLOCK, tokens), F32),
                pltpu.VMEM((2, BLOCK, tokens), BF16),
                pltpu.VMEM((2, BLOCK, tokens), BF16),
                pltpu.VMEM((4, width, 128), F32),
                pltpu.VMEM((blocks, BLOCK, 128), F32),
                pltpu.VMEM((16, LANES), F32),
                pltpu.SemaphoreType.DMA((2, blocks)),
            ],
            in_specs=[smem(), smem()]
            + (
                vmem(len(inputs) - 2)
                if last
                else vmem(len(inputs) - 2 - len(feeds)) + [pl.BlockSpec(memory_space=pl.ANY)] * len(feeds)
            ),
            limit=18,
            tiles=500,
        )
        feed_outs.append(outs)
    hidden_out = feed_outs[1][0]
    middle_grads = [outs[1] for outs in feed_outs]
    feed_kept, feed_sent, out_own, out_near, out_cross = feed_outs[1][5:]

    mixed_grads = [spread_four(*feed_outs[0][2:5], feed_outs[1][2])]
    feed_sent, out_near = after((feed_sent, out_near), mixed_grads[0][2])
    out_came = swap(out_near, "tensor", 1)
    feed_came = swap(feed_sent, "tensor", 1)
    running = None
    reduced = []
    sums = []
    crossing = []
    for r in range(rows):
        last = r == rows - 1
        g = r // half
        inputs = (
            info,
            lengths,
            *mixed_grads[g],
            *kept[g],
            weight_turned,
            inner_table,
            outer_table,
        )
        if r >= 2:
            running = after(running, sums[r - 2])
        if last:
            running = after(running, reduced[2])
        if last and ring:
            running = after(running, *evens)
        if r > 0:
            inputs = inputs + (running,)
        if last:
            inputs = inputs + (out_own, out_came, out_across, weight, vector_rows)
        outs = call(
            lambda *refs, r=r, last=last: attend_back_kernel(
                heads, chunks, chunk, r, r % half, r == 0, last, *refs
            ),
            inputs,
            [
                shape((width, chunk), BF16),
                shape((2, width, chunk), BF16),
                shape((width, chunk), BF16),
            ]
            + (
                [shape((4, 64, LANES), BF16)] * 2 + [shape((8, width), F32)]
                if last
                else [shape((3 * columns, LANES + 128), F32)]
            ),
            scratch=[
                pltpu.VMEM((128, full), BF16),
                pltpu.VMEM((heads, HEAD_ROWS, full), BF16),
                pltpu.VMEM((heads, HEAD_ROWS, full), BF16),
                pltpu.VMEM((heads, full, HEAD_ROWS), BF16),
                pltpu.VMEM((heads, full, HEAD_ROWS), BF16),
                pltpu.VMEM((3, columns, full), F32),
                pltpu.VMEM((3 * columns, full), BF16),
                pltpu.VMEM((512, LANES), F32),
                pltpu.VMEM((width, full), BF16),
                pltpu.SemaphoreType.DMA(()),
            ],
            in_specs=[smem(), smem()] + vmem(9) + hbm() + vmem(len(inputs) - 12),
            limit=12,
            tiles=420,
        )
        if last:
            outs = list(outs)
            outs[1] = after(outs[1], reduced[5], *(feed_came if ring else ()))
        near = swap(outs[1], "tensor", 1)
        reduced += [outs[0], near, None]
        if r < half:
            sums.append(add_low(outs[2], near[1]))
            reduced[-1] = swap(sums[-1], "tensor", 2)
        else:
            crossing.append((outs[2], near))
        if last:
            pair_sum = jnp.stack([add_low(cross, near[1]) for cross, near in crossing])
            reduced[-1] = swap(pair_sum, "tensor", 2)
        if last:
            even, odd, norm_sums = outs[3:]
            if ring:
                odd = after(odd, *feed_came)
        else:
            running = outs[3]
        if r == 1:
            mixed_grads.append(spread_four(*feed_outs[1][2:5], outs[0]))
        if r == 0:
            out_across = swap(
                add_low(after(out_cross, outs[0]), out_came[1]), "tensor", 2
            )
            if ring:
                feed_odd = swap(
                    add_low(after(feed_kept[1], outs[0]), feed_came[1]), "dp", 1
                )
        if r == 2 and ring:
            feed_kept = after(feed_kept, outs[0])
            evens = [
                add_low(feed_kept[0, i], feed_came[0, i], feed_odd[i]) for i in range(4)
            ]
            feed_came = [swap(evens[i], "dp", 2 * i) for i in (1, 2, 3)]
    own_parts = [part for place, part in enumerate(reduced) if place % 3 < 2]
    cross_parts = [part for part in reduced[2::3] if part is not None]
    inputs = (lengths, hidden, vectors, *middle_grads, *own_parts, *cross_parts)
    (grad_hidden,) = call(
        lambda *refs: norm_back_kernel(rows, *refs),
        inputs,
        [shape((rows, width, chunk), BF16)],
        in_specs=[smem()] + vmem(len(inputs) - 1),
        limit=12,
        tiles=120,
    )
    if ring:
        parts, own = sum_pieces(even, odd, norm_sums, cross_parts[-1], grad_hidden)
    else:
        parts = sum_pieces_plain(even, odd, norm_sums)
    if ring:
        keep, send = call(
            feed_sum_kernel,
            (info, after(evens[0], own), *feed_came),
            [shape((width // 2, BLOCK), BF16)] * 2,
            scratch=[pltpu.VMEM((width, BLOCK), F32)],
            in_specs=[smem()] + vmem(4),
            limit=4,
            tiles=20,
        )
        mine, other = call(
            feed_pair_kernel,
            (info, keep, swap(send, "tensor", 2)),
            [shape((columns, BLOCK), BF16)] * 2,
            scratch=[pltpu.VMEM((width // 2, BLOCK), F32)],
            in_specs=[smem()] + vmem(2),
            limit=4,
            tiles=20,
        )
        feed_parts = (mine, swap(other, "tensor", 1))
    else:
        grad_up_weight, grad_down_weight = scatter_feed_plain(
            feed_kept, feed_sent, core, hidden_count
        )

    inputs = (info, *parts) + (feed_parts if ring else ())
    outs = [
        shape((3, width, columns), F32),
        shape((3, columns), F32),
        shape((columns, width), F32),
    ]
    outs += [shape((1, width), F32)] * 4
    outs += [shape(up_projection_bias.shape, F32)]
    outs += [shape((1, width), F32)] * 2
    if ring:
        outs += [shape((columns, hidden_count), F32), shape((hidden_count, columns), F32)]
    outs = call(
        unpack_kernel,
        inputs,
        outs,
        scratch=[
            pltpu.VMEM((512, LANES), F32),
            pltpu.VMEM((1, up_projection_bias.shape[0]), F32),
        ],
        in_specs=[smem()] + vmem(len(inputs) - 1),
        limit=8,
        tiles=60,
    )
    grad_qkv_weight, grad_qkv_bias, grad_out_weight = outs[:3]
    grad_ffn_gain, grad_ffn_shift, grad_out_bias, grad_down_bias, grad_up_bias = outs[3:8]
    grad_attn_gain, grad_attn_shift = outs[8:10]
    if ring:
        grad_up_weight, grad_down_weight = outs[10:]
    return (
        hidden_out.transpose(0, 2, 1),
        grad_hidden.transpose(0, 2, 1),
        grad_attn_gain[0],
        grad_attn_shift[0],
        grad_qkv_weight,
        grad_qkv_bias,
        grad_out_weight,
        grad_out_bias[0],
        grad_ffn_gain[0],
        grad_ffn_shift[0],
        grad_up_weight,
        grad_up_bias,
        grad_down_weight,
        grad_down_bias[0],
    )


def solution(mesh):
    return jax.shard_map(
        shards,
        mesh=mesh,
        in_specs=(
            P("dp", "tensor", None),
            P(),
            P(),
            P(None, None, "tensor"),
            P(None, "tensor"),
            P("tensor", None),
            P(),
            P(),
            P(),
            P("tensor", "dp"),
            P(),
            P("dp", "tensor"),
            P(),
            P("dp"),
            P("dp", "tensor", None),
        ),
        out_specs=(
            P("dp", "tensor", None),
            P("dp", "tensor", None),
            P(),
            P(),
            P(None, None, "tensor"),
            P(None, "tensor"),
            P("tensor", None),
            P(),
            P(),
            P(),
            P("tensor", "dp"),
            P(),
            P("dp", "tensor"),
            P(),
        ),
        check_vma=False,
    )
```

```python
import math

import jax
import jax.numpy as jnp
import numpy as np
from jax import lax
from jax.experimental import pallas as pl
from jax.experimental.pallas import tpu as pltpu
from jax.sharding import PartitionSpec as P

HEAD_DIM = 24
HEAD_ROWS = 32
EPS = 1e-05
MASK_FILL = -1000000000.0
LOG2E = math.log2(math.e)
SAFE_SCORE = 85.0
WORK_SCALE = 0.01
BLOCK = 256
KEY_STEP = 256
LANES = 512
BF16 = jnp.bfloat16
F32 = jnp.float32

NN = (((1,), (0,)), ((), ()))
NT = (((1,), (1,)), ((), ()))
TN = (((0,), (0,)), ((), ()))


def product(left, right, dims=NN):
    return lax.dot_general(left, right, dims, preferred_element_type=F32)


def vmem(count):
    return [pl.BlockSpec(memory_space=pltpu.VMEM)] * count


def smem():
    return pl.BlockSpec(memory_space=pltpu.SMEM)


def hbm(count=1):
    return [pl.BlockSpec(memory_space=pltpu.HBM)] * count


def call(kernel, inputs, outs, scratch=(), in_specs=None, out_specs=None, limit=40, tiles=0):
    flops = int(2 * 256**3 * tiles * WORK_SCALE)
    in_specs = vmem(len(inputs)) if in_specs is None else in_specs
    inputs = [
        pltpu.with_memory_space_constraint(part, pltpu.HBM)
        if spec.memory_space is pltpu.HBM
        else part
        for part, spec in zip(inputs, in_specs)
    ]
    out_specs = vmem(len(outs)) if out_specs is None else out_specs
    outs = [
        pltpu.HBM(part.shape, part.dtype) if spec.memory_space is pltpu.HBM else part
        for part, spec in zip(outs, out_specs)
    ]
    return pl.pallas_call(
        kernel,
        out_shape=outs,
        in_specs=in_specs,
        out_specs=out_specs,
        scratch_shapes=list(scratch),
        compiler_params=pltpu.CompilerParams(vmem_limit_bytes=limit << 20),
        cost_estimate=pl.CostEstimate(flops=flops, transcendentals=0, bytes_accessed=0),
    )(*inputs)


def shape(dims, dtype):
    return jax.ShapeDtypeStruct(dims, dtype)


def at_block(index, size):
    return pl.ds(pl.multiple_of(index * size, size), size)


def split_three(values):
    high = values.astype(BF16).astype(F32)
    rest = values - high
    middle = rest.astype(BF16).astype(F32)
    return high, middle, rest - middle


def row_of(lengths, slot, rows):
    slot = jnp.where(slot == 0, 0, jnp.where(slot == 1, rows - 1, slot - 1))
    chosen = jnp.int32(0)
    for i in range(rows):
        rank = jnp.int32(0)
        for j in range(rows):
            if j < i:
                rank += jnp.where(lengths[j] <= lengths[i], 1, 0)
            elif j > i:
                rank += jnp.where(lengths[j] < lengths[i], 1, 0)
        chosen += jnp.where(rank == slot, i, 0)
    return chosen


def after(values, *others):
    return lax.optimization_barrier((values, *others))[0]


def norm_columns(values):
    centre = values - jnp.mean(values, axis=0, keepdims=True)
    inverse = lax.rsqrt(jnp.mean(centre * centre, axis=0, keepdims=True) + EPS)
    return centre * inverse, inverse


def norm_columns_back(upstream, unit, inverse, gain):
    scaled = upstream * gain
    centred = scaled - jnp.mean(scaled, axis=0, keepdims=True)
    return inverse * (centred - unit * jnp.mean(scaled * unit, axis=0, keepdims=True))


def pair_kernel(info, up, down, pair, up_inside, down_inside, semaphores):
    copies = [
        pltpu.make_async_copy(up, up_inside, semaphores.at[0]),
        pltpu.make_async_copy(down, down_inside, semaphores.at[1]),
    ]
    for copy in copies:
        copy.start()
    pair[...] = jnp.zeros_like(pair)
    for copy in copies:
        copy.wait()
    size = up.shape[1]
    up_half = up_inside[...]
    down_half = down_inside[...].astype(F32).T.astype(BF16)

    @pl.when(info[0] & 1 == 0)
    def _():
        pair[:, :size] = up_half
        pair[:, BLOCK : BLOCK + size] = down_half

    @pl.when(info[0] & 1 == 1)
    def _():
        pair[:, :size] = down_half
        pair[:, BLOCK : BLOCK + size] = up_half


def norm_kernel(
    lengths,
    hidden_in,
    gain,
    shift,
    out_weight_in,
    first_out,
    second_out,
    hidden,
    gain_inside,
    shift_inside,
    out_weight,
    rows_scratch,
    semaphores,
):
    rows, width, chunk = hidden.shape
    copies = [
        pltpu.make_async_copy(
            hidden_in.at[row_of(lengths, slot, rows)], hidden.at[slot], semaphores.at[slot]
        )
        for slot in range(rows)
    ]
    others = [
        pltpu.make_async_copy(gain, gain_inside, semaphores.at[4]),
        pltpu.make_async_copy(shift, shift_inside, semaphores.at[5]),
        pltpu.make_async_copy(out_weight_in, out_weight, semaphores.at[6]),
    ]
    for copy in others[:2] + copies + others[2:]:
        copy.start()
    rows_scratch[...] = jnp.zeros_like(rows_scratch)
    others[0].wait()
    others[1].wait()
    rows_scratch[0:1, :] = gain_inside[...]
    rows_scratch[1:2, :] = shift_inside[...]
    columns = rows_scratch[...].T
    half = rows // 2
    for row in range(rows):
        copies[row].wait()
        unit, _ = norm_columns(hidden[row].astype(F32))
        target = first_out if row < half else second_out
        place = row % half * width
        target[place : place + width, :] = (unit * columns[:, 0:1] + columns[:, 1:2]).astype(
            BF16
        )
    others[2].wait()
    own = out_weight.shape[0]
    second_out[half * width : half * width + own, :] = out_weight[:, :chunk]
    rest = width - chunk
    second_out[half * width + own : half * width + 2 * own, :] = jnp.zeros((own, chunk), BF16)
    second_out[half * width + own : half * width + 2 * own, :rest] = out_weight[:, chunk:]


def prepare_kernel(heads, info, *refs):
    outside, refs = refs[:9], refs[9:]
    weight_out, weight_turned_out, columns_out, bias_out, up_bias_out, vector_rows = refs[:6]
    weight_scratch, bias_rows = refs[6:8]
    inside, semaphores = refs[8:17], refs[17]
    copies = [
        pltpu.make_async_copy(source, target, semaphores.at[place])
        for place, (source, target) in enumerate(zip(outside, inside))
    ]
    for copy in copies:
        copy.start()
    vectors, (up_bias, weight, bias) = inside[:6], inside[6:]
    width = weight.shape[1]
    vector_rows[...] = jnp.zeros_like(vector_rows)
    for copy in copies:
        copy.wait()
    for place, vector in enumerate(vectors):
        vector_rows[place : place + 1, :] = vector[...]
    columns_out[...] = jnp.concatenate([vector_rows[...], jnp.zeros((120, width), F32)]).T
    span = heads * HEAD_DIM
    for c in range(3):
        own = slice(c * span, (c + 1) * span)
        weight_scratch[own, :] = weight[c].astype(F32).T
        bias_out[own, :] = jnp.broadcast_to(bias[c : c + 1, :], (128, span)).T
    weight_out[...] = weight_scratch[...].astype(BF16)
    weight_turned_out[...] = weight_scratch[...].T.astype(BF16)
    bias_rows[...] = jnp.zeros_like(bias_rows)
    count = up_bias.shape[1]
    block = count // 8
    spread = jnp.broadcast_to(up_bias[...], (8, count))
    for j in range(8):
        moved = pltpu.roll(spread, lax.rem(count - (info[1] ^ j) * block, count), 1)
        bias_rows[j : j + 1, :block] = moved[0:1, :block]
    up_bias_out[...] = bias_rows[...].T


def assemble_kernel(chunks, info, *refs):
    parts, (out, rows) = refs[:chunks], refs[chunks:]
    size = parts[0].shape[0]
    for k in range(chunks):
        half = parts[k][:, (k & 1) * BLOCK : ((k & 1) + 1) * BLOCK]
        rows[at_block(info[0] ^ k, size), :] = half.astype(F32)
    out[...] = rows[...].astype(BF16)


def rotary_constants(chunk, chunks):
    half = HEAD_DIM // 2
    element = np.arange(HEAD_DIM)
    frequency = (1.0 / 10000.0 ** (np.arange(0, HEAD_DIM, 2).astype(np.float32) / HEAD_DIM)).astype(
        np.float32
    )
    per_row = frequency[element % half].astype(np.float64)
    inner = per_row[:, None] * np.arange(chunk)[None, :]
    outer = per_row[:, None] * (np.arange(chunks) * chunk)[None, :]
    outer = np.repeat(outer[:, :, None], chunk, axis=2).transpose(1, 0, 2)
    inner_pair = np.stack([np.cos(inner), np.sin(inner)]).astype(np.float32)
    outer_pair = np.stack([np.cos(outer), np.sin(outer)]).astype(np.float32)
    return inner_pair, outer_pair


def chunk_tables(inner, outer, index):
    cos_in, sin_in = inner[0], inner[1]
    cos_out, sin_out = outer[0, index], outer[1, index]
    element = lax.broadcasted_iota(jnp.int32, cos_in.shape, 0)
    sine = sin_in * cos_out + cos_in * sin_out
    return cos_in * cos_out - sin_in * sin_out, jnp.where(
        element < HEAD_DIM // 2, -sine, sine
    )


def swap_halves(values):
    return pltpu.roll(values, HEAD_DIM // 2, 0)


def attend_kernel(heads, chunks, chunk, first_row, rows, info, lengths, *refs):
    parts = refs[:chunks]
    weight, bias, inner, outer, own_out, near_out, cross_out = refs[chunks : chunks + 7]
    queries, keys, values, logsum, mixed_turned, normed_out, key_rows, peak, flat = refs[
        chunks + 7 : chunks + 16
    ]
    normed, semaphores = refs[chunks + 16 :]
    position = info[0]
    width = normed.shape[1]
    full = chunk * chunks
    span = heads * HEAD_DIM
    scale = LOG2E * HEAD_DIM**-0.5

    def one_row(r, carry):
        length = lengths[row_of(lengths, first_row + r, lengths.shape[0])]
        for k in range(chunks):
            normed[r, :, at_block(position ^ k, chunk)] = parts[k][at_block(r, width), :]
        pltpu.make_async_copy(normed.at[r], normed_out.at[r], semaphores.at[r]).start()
        flat[...] = product(weight[...], normed[r])
        line = lax.broadcasted_iota(jnp.int32, (8, chunk), 0)
        ones = jnp.where(line < 3, 1.0, 0.0)
        query_line = jnp.where(line == 3, 1.0, 0.0)
        query_top = [jnp.zeros((1, chunk), F32) for _ in range(heads)]
        key_top = [jnp.zeros((1, chunk), F32) for _ in range(heads)]
        for j in range(chunks):
            at = slice(j * chunk, (j + 1) * chunk)
            cosine, sine = chunk_tables(inner, outer, j)
            query_cosine, query_sine = cosine * scale, sine * scale
            place = lax.broadcasted_iota(jnp.int32, (8, chunk), 1) + j * chunk
            key_line = jnp.where((line == 3) & (place >= length), MASK_FILL, ones)
            for h in range(heads):
                here = h * HEAD_DIM
                query, key, value = (
                    flat[c * span + here : c * span + here + HEAD_DIM, at]
                    + jnp.concatenate(
                        [bias[c * span + here : c * span + here + HEAD_DIM, :]] * (chunk // 128),
                        axis=1,
                    )
                    for c in range(3)
                )
                query = query * query_cosine + swap_halves(query) * query_sine
                key = key * cosine + swap_halves(key) * sine
                query_top[h] = jnp.maximum(
                    query_top[h], jnp.sum(query * query, axis=0, keepdims=True)
                )
                key_top[h] = jnp.maximum(key_top[h], jnp.sum(key * key, axis=0, keepdims=True))
                key_full = jnp.concatenate([key, key_line])
                queries[r, h, :, at] = jnp.concatenate([query, query_line]).astype(BF16)
                keys[r, h, :, at] = key_full.astype(BF16)
                values[r, h, :, at] = jnp.concatenate([value, ones]).astype(BF16)
                key_rows[h, at, :] = key_full.T.astype(BF16)
        bound = jnp.zeros((1, 1), F32)
        for h in range(heads):
            bound = jnp.maximum(
                bound,
                jnp.max(query_top[h], axis=-1, keepdims=True)
                * jnp.max(key_top[h], axis=-1, keepdims=True),
            )
        safe = jnp.max(bound) <= SAFE_SCORE * SAFE_SCORE
        peak[...] = jnp.zeros_like(peak)

        @pl.when(jnp.logical_not(safe))
        def _():
            def one_head(h, carry):
                scores = product(key_rows[h], queries[r, h])
                peak[pl.ds(h, 1), :] = (
                    jnp.max(scores, axis=0, keepdims=True).astype(BF16).astype(F32)
                )
                return carry

            lax.fori_loop(0, heads, one_head, 0)

        head_line = lax.broadcasted_iota(jnp.int32, (HEAD_ROWS, full), 0)

        def with_keys(count):
            def one_head(h, carry):
                top = peak[pl.ds(h, 1), :]
                query = jnp.where(
                    head_line == HEAD_DIM, -top, queries[r, h].astype(F32)
                ).astype(BF16)
                exponent = jnp.exp2(product(key_rows[h, :count, :], query)).astype(BF16)
                blend = product(values[r, h, :, :count], exponent)
                total = blend[HEAD_DIM : HEAD_DIM + 1, :]
                logsum[r, pl.ds(h, 1), :] = top + jnp.log2(total)
                mixed_turned[r, pl.ds(pl.multiple_of(h * HEAD_DIM, 8), HEAD_DIM), :] = blend[
                    :HEAD_DIM
                ] * (1.0 / total)
                return carry

            lax.fori_loop(0, heads, one_head, 0, unroll=True)

        blocks = jnp.maximum((length + KEY_STEP - 1) // KEY_STEP, 1)
        for b in range(1, full // KEY_STEP + 1):
            pl.when(blocks == b)(lambda b=b: with_keys(b * KEY_STEP))
        mixed_turned[r, span:, :] = jnp.zeros((mixed_turned.shape[1] - span, full), F32)
        own_out[r] = mixed_turned[r, :, at_block(position, chunk)].astype(BF16)
        near_out[r] = mixed_turned[r, :, at_block(position ^ 1, chunk)].astype(BF16)
        cross_out[r, 0] = mixed_turned[r, :, at_block(position ^ 2, chunk)].astype(BF16)
        cross_out[r, 1] = mixed_turned[r, :, at_block(position ^ 3, chunk)].astype(BF16)
        return carry

    lax.fori_loop(0, rows, one_row, 0)
    for r in range(rows):
        pltpu.make_async_copy(normed.at[r], normed_out.at[r], semaphores.at[r]).wait()


def attend_back_kernel(heads, chunks, chunk, row, local, first, last, info, lengths, *refs):
    upstream_own, upstream_near, upstream_cross, upstream_far = refs[:4]
    queries, keys, values, logsum, mixed_turned, normed_in, weight_turned, inner, outer = refs[
        4:13
    ]
    refs = refs[13:]
    if not first:
        carried = refs[0]
        refs = refs[1:]
    if last:
        out_own, out_near, out_cross, weight, vector_rows = refs[:5]
        refs = refs[5:]
    own_out, near_out, cross_out = refs[:3]
    refs = refs[3:]
    if last:
        even_pieces, odd_pieces, norm_sums = refs[:3]
        refs = refs[3:]
    else:
        running = refs[0]
        refs = refs[1:]
    (
        upstream,
        query_full,
        upstream_full,
        key_rows,
        value_rows,
        grads,
        grad_low,
        packed,
        normed,
        semaphore,
    ) = refs
    fetch = pltpu.make_async_copy(normed_in.at[local], normed, semaphore)
    fetch.start()
    position, index = info[0], info[1]
    length = lengths[row_of(lengths, row, lengths.shape[0])]
    full = chunk * chunks
    span = heads * HEAD_DIM
    upstream[:, at_block(position, chunk)] = upstream_own[local]
    upstream[:, at_block(position ^ 1, chunk)] = upstream_near[local]
    upstream[:, at_block(position ^ 2, chunk)] = upstream_cross[local, 0]
    upstream[:, at_block(position ^ 3, chunk)] = upstream_far[local, 1]
    zeros = jnp.zeros((5, chunk), F32)
    line = lax.broadcasted_iota(jnp.int32, (8, chunk), 0)
    for j in range(chunks):
        at = slice(j * chunk, (j + 1) * chunk)
        turned = upstream[:, at].astype(F32)
        blend = turned * mixed_turned[local, :, at]
        for h in range(heads):
            own = slice(h * HEAD_DIM, (h + 1) * HEAD_DIM)
            high, middle, rest = split_three(-jnp.sum(blend[own], axis=0, keepdims=True))
            extra = jnp.where(
                line == 0, high, jnp.where(line == 1, middle, jnp.where(line == 2, rest, 0.0))
            )
            upstream_full[h, :, at] = jnp.concatenate([turned[own], extra]).astype(BF16)
            high, middle, rest = split_three(-logsum[local, h : h + 1, at])
            extra = jnp.where(
                line == 0,
                high,
                jnp.where(
                    line == 1, middle, jnp.where(line == 2, rest, jnp.where(line == 3, 1.0, 0.0))
                ),
            )
            query = queries[local, h, :, at].astype(F32)[:HEAD_DIM]
            query_full[h, :, at] = jnp.concatenate([query, extra]).astype(BF16)
            key_rows[h, at, :] = keys[local, h, :, at].astype(F32).T.astype(BF16)
            value_rows[h, at, :] = values[local, h, :, at].astype(F32).T.astype(BF16)

    def with_keys(count):
        def one_head(h, carry):
            own = pl.ds(pl.multiple_of(h * HEAD_DIM, 8), HEAD_DIM)
            grad_query = jnp.zeros((HEAD_ROWS, full), F32)
            for place in range(0, count, BLOCK):
                at = slice(place, min(place + BLOCK, count))
                probs = jnp.exp2(product(key_rows[h, at, :], query_full[h])).astype(BF16)
                grad_probs = product(value_rows[h, at, :], upstream_full[h]).astype(BF16)
                grad_scores = probs * grad_probs
                grads[2, own, at] = product(upstream_full[h], probs, NT)[:HEAD_DIM]
                grads[1, own, at] = product(query_full[h], grad_scores, NT)[:HEAD_DIM]
                grad_query += product(keys[local, h, :, at], grad_scores)
            grads[0, own, :] = grad_query[:HEAD_DIM]
            return carry

        lax.fori_loop(0, heads, one_head, 0)
        if count < full:
            grads[1, :, count:] = jnp.zeros((span, full - count), F32)
            grads[2, :, count:] = jnp.zeros((span, full - count), F32)

    blocks = jnp.maximum((length + KEY_STEP - 1) // KEY_STEP, 1)
    for b in range(1, full // KEY_STEP + 1):
        pl.when(blocks == b)(lambda b=b: with_keys(b * KEY_STEP))

    sums = [[jnp.zeros((HEAD_DIM, 128), F32) for _ in range(heads)] for _ in range(3)]
    for j in range(chunks):
        at = slice(j * chunk, (j + 1) * chunk)
        cosine, sine = chunk_tables(inner, outer, j)
        query_cosine, query_sine = cosine * HEAD_DIM**-0.5, sine * HEAD_DIM**-0.5
        key_cosine, key_sine = cosine * (1.0 / LOG2E), sine * (1.0 / LOG2E)
        for h in range(heads):
            own = slice(h * HEAD_DIM, (h + 1) * HEAD_DIM)
            query, key, value = (grads[c, own, at] for c in range(3))
            query = query * query_cosine - swap_halves(query) * query_sine
            key = key * key_cosine - swap_halves(key) * key_sine
            for c, part in enumerate((query, key, value)):
                for piece in range(chunk // 128):
                    sums[c][h] = sums[c][h] + part[:, piece * 128 : (piece + 1) * 128]
                grads[c, own, at] = part
    for c in range(3):
        grad_low[c * span : (c + 1) * span, :] = grads[c].astype(BF16)
    for k in range(chunks):
        result = product(
            weight_turned[...], grad_low[:, at_block(position ^ k, chunk)]
        ).astype(BF16)
        if k == 0:
            own_out[...] = result
        elif k == 2:
            cross_out[...] = result
        else:
            near_out[k // 2] = result
    width = weight_turned.shape[0]
    fetch.wait()
    result = product(grad_low[...], normed[...], NT)
    bias_grad = jnp.concatenate(
        [jnp.sum(part, axis=1, keepdims=True) for group in sums for part in group]
    )
    bias_grad = jnp.broadcast_to(bias_grad, (3 * span, 128))
    if not first:
        result = result + carried[:, :width]
        bias_grad = bias_grad + carried[:, LANES:]
    if not last:
        running[:, :width] = result
        running[:, LANES:] = bias_grad
        return
    packed[: 3 * span, :width] = result
    gain_sum = jnp.zeros((8, width), F32)
    shift_sum = jnp.zeros((8, width), F32)
    gain, shift = vector_rows[0:1, :], vector_rows[1:2, :]
    for place in range(0, 3 * span, 8):
        own = slice(place, place + 8)
        factor = weight[own, :].astype(F32)
        column = bias_grad[own, 0:1]
        gain_sum = gain_sum + factor * (result[own] - shift * column)
        shift_sum = shift_sum + factor * column
    norm_sums[...] = jnp.zeros_like(norm_sums)
    norm_sums[0:1, :] = jnp.sum(gain_sum, axis=0, keepdims=True) / gain
    norm_sums[1:2, :] = jnp.sum(shift_sum, axis=0, keepdims=True)
    lane = lax.broadcasted_iota(jnp.int32, (3 * span, 128), 1)
    packed[: 3 * span, LANES - 128 :] = jnp.where(
        lane >= width - (LANES - 128), bias_grad, packed[: 3 * span, LANES - 128 :]
    )
    shared = (out_own[...].astype(F32) + out_near[0].astype(F32)) + out_cross[...].astype(F32)
    packed[3 * span : 4 * span, :] = shared[:span]
    packed[4 * span : 4 * span + 16, :] = shared[128:144]
    packed[4 * span + 16 :, :] = jnp.zeros((packed.shape[0] - 4 * span - 16, LANES), F32)
    size = packed.shape[0] // 8
    for j in range(8):
        target = odd_pieces if j % 2 else even_pieces
        target[j // 2] = packed[at_block(index ^ j, size), :].astype(BF16)


def gelu_parts(values):
    magnitude = jnp.abs(values) * (0.5**0.5)
    density = jnp.exp2(values * values * (-0.5 * LOG2E))
    divisor = 1.0 + 0.3275911 * magnitude
    step = pl.reciprocal(divisor, approx=True)
    step = step * (2.0 - divisor * step)
    series = 1.061405429 * step - 1.453152027
    series = series * step + 1.421413741
    series = series * step - 0.284496736
    series = series * step + 0.254829592
    tail = 0.5 * series * step * density
    share = jnp.where(values < 0, tail, 1.0 - tail)
    return share, density * (1.0 / math.sqrt(2.0 * math.pi))


def lane_groups(values):
    total = values[:, :128]
    for place in range(128, values.shape[1], 128):
        total = total + values[:, place : place + 128]
    return total


def row_sum(values):
    total = values[:8]
    for place in range(8, values.shape[0], 8):
        total = total + values[place : place + 8]
    return total


def feed_kernel(chunks, blocks, first_row, rows, last, info, lengths, *refs):
    hidden, cotangent, columns, up_bias = refs[:4]
    mixed_own, mixed_near, mixed_cross, mixed_far = refs[4:8]
    out_weight = refs[8 : 8 + chunks]
    refs = refs[8 + chunks :]
    if last:
        weights, carried, out_carried, sums_carried, bias_carried, hidden_before = refs[:6]
        refs = refs[6:]
    else:
        feeds, refs = refs[:12], refs[12:]
    hidden_out, grad_middle_out, grad_own, grad_near, grad_cross = refs[:5]
    refs = refs[5:]
    if last:
        kept_out, sent_out, out_own, out_near, out_cross = refs[:5]
    else:
        weights, carried, out_carried, sums_carried, bias_carried = refs[:5]
    refs = refs[5:]
    (
        out_rows,
        mixed,
        source,
        given,
        low_rows,
        down_total,
        back_total,
        upward,
        upstream,
        active,
        grad_low,
        sums_total,
        bias_total,
        shared,
        semaphores,
    ) = refs
    core, index = info[0] & 1, info[1]
    width, chunk = hidden.shape[1:]
    tokens = rows * chunk
    held = mixed_own.shape[1]
    places = [row_of(lengths, first_row + r, hidden.shape[0]) for r in range(rows)]
    if not last:
        copies = []
        for side in range(2):
            sources = list(feeds[6 * side : 6 * side + 4])
            duo, duo_beside = feeds[6 * side + 4 : 6 * side + 6]
            place = core if side == 0 else 1 - core
            for e in range(2):
                sources += [duo.at[e], duo_beside.at[e]]
            for j in range(blocks):
                copies.append(
                    pltpu.make_async_copy(
                        sources[j],
                        weights.at[place, :, j * BLOCK : (j + 1) * BLOCK],
                        semaphores.at[side, j],
                    )
                )
        for copy in copies:
            copy.start()
    own_rows = (out_weight[0].shape[0] - 2 * width) // 2
    for k in range(chunks):
        base = 2 * width
        at = k * held
        out_rows[at : at + held, :] = jnp.zeros((held, width), BF16)
        out_rows[at : at + own_rows, :chunk] = out_weight[k][base : base + own_rows, :]
        out_rows[at : at + own_rows, chunk:] = out_weight[k][
            base + own_rows : base + 2 * own_rows, : width - chunk
        ]
    for r in range(rows):
        at = slice(r * chunk, (r + 1) * chunk)
        mixed[0 * held : 1 * held, at] = mixed_own[r]
        mixed[1 * held : 2 * held, at] = mixed_near[r]
        mixed[2 * held : 3 * held, at] = mixed_cross[r, 0]
        mixed[3 * held : 4 * held, at] = mixed_far[r, 1]
        given[:, at] = cotangent[places[r]]
    source[...] = product(out_rows[...], mixed[...], TN)
    step = 32
    pieces = [slice(place, place + step) for place in range(0, width, step)]

    total = jnp.zeros((8, tokens), F32)
    for own in pieces:
        entered = jnp.concatenate([hidden[places[r], own, :] for r in range(rows)], axis=1)
        middle = source[own, :] + entered.astype(F32) + columns[own, 2:3]
        source[own, :] = middle
        total = total + row_sum(middle)
    mean = jnp.sum(total, axis=0, keepdims=True) * (1.0 / width)
    total = jnp.zeros((8, tokens), F32)
    for own in pieces:
        centre = source[own, :] - mean
        total = total + row_sum(centre * centre)
    inverse = lax.rsqrt(jnp.sum(total, axis=0, keepdims=True) * (1.0 / width) + EPS)
    for own in pieces:
        middle = source[own, :]
        unit = (middle - mean) * inverse
        low_rows[own, :] = (unit * columns[own, 3:4] + columns[own, 4:5]).astype(BF16)
        down_total[own, :] = middle + columns[own, 5:6]
        source[own, :] = unit
    back_total[...] = jnp.zeros_like(back_total)
    if not last:
        for copy in copies:
            copy.wait()

    pair = 2 * BLOCK

    def enter(i, slot):
        at = at_block(i, pair)
        upward[slot] = product(weights[0, :, at], low_rows[...], TN)
        upstream[slot] = product(weights[1, :, at], given[...], TN)

    lane = lax.broadcasted_iota(jnp.int32, (step, 128), 1)

    def bend(i, slot):
        for place in range(0, pair, step):
            own = slice(place, place + step)
            j = 2 * i + place // BLOCK
            inside = slice(place % BLOCK, place % BLOCK + step)
            bias = jnp.sum(
                jnp.where(lane == j, up_bias[inside, :], 0.0), axis=1, keepdims=True
            )
            values = upward[slot, own, :] + bias
            share, density = gelu_parts(values)
            active[slot, own, :] = (values * share).astype(BF16)
            grad_up = upstream[slot, own, :] * (share + values * density)
            grad_low[slot, own, :] = grad_up.astype(BF16)
            bias_sum = lane_groups(grad_up)
            if last:
                bias_total[j, inside, :] = bias_sum + bias_carried[j, inside, :]
            else:
                bias_carried[j, inside, :] = bias_sum

    def leave(i, slot):
        at = at_block(i, pair)
        down_total[...] += product(weights[1, :, at], active[slot])
        back_total[...] += product(weights[0, :, at], grad_low[slot])
        up_grad = product(low_rows[...], grad_low[slot], NT)
        down_grad = product(given[...], active[slot], NT)
        if not last:
            carried[0, :, at] = up_grad
            carried[1, :, at] = down_grad
            return
        up_grad = up_grad + carried[0, :, at]
        down_grad = down_grad + carried[1, :, at]
        kept = jnp.where(core == 0, up_grad, down_grad).astype(BF16)
        sent = jnp.where(core == 0, down_grad, up_grad).astype(BF16)
        for odd in range(2):
            kept_out[odd, i] = kept[:, odd * BLOCK : (odd + 1) * BLOCK]
            sent_out[odd, i] = sent[:, odd * BLOCK : (odd + 1) * BLOCK]

    def two_pairs(n, carry):
        i = 2 * n
        enter(i + 1, 1)
        bend(i, 0)
        leave(i, 0)
        enter(lax.rem(i + 2, blocks // 2), 0)
        bend(i + 1, 1)
        leave(i + 1, 1)
        return carry

    enter(0, 0)
    lax.fori_loop(0, blocks // 4, two_pairs, 0)
    if last:
        for r in range(first_row):
            hidden_out[row_of(lengths, r, hidden.shape[0])] = hidden_before[r]
    for r in range(rows):
        place = places[r] if last else r
        hidden_out[place] = down_total[:, r * chunk : (r + 1) * chunk].astype(BF16)
    scaled_total = jnp.zeros((8, tokens), F32)
    unit_total = jnp.zeros((8, tokens), F32)
    for own in pieces:
        scaled = back_total[own, :] * columns[own, 3:4]
        scaled_total = scaled_total + row_sum(scaled)
        unit_total = unit_total + row_sum(scaled * source[own, :])
    scaled_mean = jnp.sum(scaled_total, axis=0, keepdims=True) * (1.0 / width)
    unit_mean = jnp.sum(unit_total, axis=0, keepdims=True) * (1.0 / width)
    for own in pieces:
        back, unit = back_total[own, :], source[own, :]
        given_wide = given[own, :].astype(F32)
        scaled = back * columns[own, 3:4]
        grad_middle = given_wide + inverse * (scaled - scaled_mean - unit * unit_mean)
        for r in range(rows):
            grad_middle_out[r, own, :] = grad_middle[:, r * chunk : (r + 1) * chunk]
        low_rows[own, :] = grad_middle.astype(BF16)
        for place, part in enumerate((back * unit, back, grad_middle, given_wide)):
            part = lane_groups(part)
            if last:
                sums_total[place, own, :] = part + sums_carried[place, own, :]
            else:
                sums_carried[place, own, :] = part
    mixed_grad = product(out_rows[...], low_rows[...]).astype(BF16)
    for r in range(rows):
        at = slice(r * chunk, (r + 1) * chunk)
        grad_own[r] = mixed_grad[:held, at]
        grad_near[r] = mixed_grad[held : 2 * held, at]
        grad_cross[r, 0] = mixed_grad[2 * held : 3 * held, at]
        grad_cross[r, 1] = mixed_grad[3 * held :, at]
    out_part = product(mixed[...], low_rows[...], NT)
    if not last:
        out_carried[...] = out_part
        return
    out_part = (out_part + out_carried[...]).astype(BF16)
    shared[...] = jnp.zeros_like(shared)
    for place in range(4):
        line = row_sum(sums_total[place].T)
        shared[place : place + 1, :width] = jnp.sum(line, axis=0, keepdims=True)
    for j in range(blocks):
        line = row_sum(bias_total[j].T)
        shared[pl.ds(4 + (index ^ j), 1), :BLOCK] = jnp.sum(line, axis=0, keepdims=True)
    shared_low = shared[...].astype(BF16)
    for k, target in enumerate((out_own, out_near.at[0], out_cross, out_near.at[1])):
        target[:held, 384:] = jnp.zeros((held, LANES - 384), BF16)
        target[:held, :width] = out_part[k * held : (k + 1) * held]
        target[held:, :] = shared_low


def norm_back_kernel(rows, lengths, hidden, columns, *refs):
    middle_grads, refs = refs[:2], refs[2:]
    own_parts, near_parts = refs[0 : 2 * rows : 2], refs[1 : 2 * rows : 2]
    crossed, (out,) = refs[2 * rows : 2 * rows + rows // 2], refs[2 * rows + rows // 2 :]
    cross_parts = [part.at[place] for part in crossed for place in range(2)]
    gain = columns[:, 0:1]
    for row in range(rows):
        place = row_of(lengths, row, rows)
        unit, inverse = norm_columns(hidden[place].astype(F32))
        grad = (
            own_parts[row][...].astype(F32)
            + near_parts[row][0].astype(F32)
            + cross_parts[row][...].astype(F32)
        )
        half = rows // 2
        result = middle_grads[row // half][row % half] + norm_columns_back(
            grad, unit, inverse, gain
        )
        out[place] = result.astype(BF16)


def add_pieces_kernel(even, beside, *outs):
    for i, out in enumerate(outs):
        out[...] = (even[i].astype(F32) + beside[i].astype(F32)).astype(BF16)


def own_piece_kernel(first, second, fourth, sixth, norm_sums, out):
    size = first.shape[0]
    total = first[...].astype(F32) + second[...].astype(F32)
    total = total + fourth[...].astype(F32) + sixth[...].astype(F32)
    out[:size, :] = total.astype(BF16)
    width = norm_sums.shape[1]
    values = norm_sums[...]
    high = values.astype(BF16)
    rest = (values - high.astype(F32)).astype(BF16)
    out[size:, 384:] = jnp.zeros((16, LANES - 384), BF16)
    out[size:, :width] = jnp.concatenate([high.astype(F32), rest.astype(F32)]).astype(BF16)


def feed_sum_kernel(info, first, second, fourth, sixth, keep, send, rows):
    total = first[...].astype(F32) + second[...].astype(F32)
    rows[...] = total + fourth[...].astype(F32) + sixth[...].astype(F32)
    size = keep.shape[0]
    chip = info[0] >> 1
    keep[...] = rows[at_block(chip, size), :].astype(BF16)
    send[...] = rows[at_block(1 - chip, size), :].astype(BF16)


def feed_pair_kernel(info, kept, came, mine, other, rows):
    rows[...] = kept[...].astype(F32) + came[...].astype(F32)
    size = mine.shape[0]
    core = info[0] & 1
    mine[...] = rows[at_block(core, size), :].astype(BF16)
    other[...] = rows[at_block(1 - core, size), :].astype(BF16)


def unpack_kernel(info, *refs):
    evens, beside = refs[:4], refs[4]
    refs = refs[5:]
    if len(refs) > 12:
        mine, came, refs = refs[0], refs[1], refs[2:]
        up_grad, down_grad = refs[10:12]
        refs = refs[:10] + refs[12:]
        count = up_grad.shape[1]

        def write(up, down):
            up_grad[...] = up[:, :count].astype(F32)
            down_grad[...] = down[...].astype(F32).T[:count, :]

        pl.when(info[0] & 1 == 0)(lambda: write(mine, came))
        pl.when(info[0] & 1 == 1)(lambda: write(came, mine))
    weight_grad, bias_grad, out_grad, gain, shift, out_bias, down_bias, up_bias = refs[:8]
    norm_gain, norm_shift, whole, line = refs[8:]
    size = whole.shape[0] // 8
    width = weight_grad.shape[1]
    norms = [evens[0][size:, :].astype(F32) + beside[0, size:, :].astype(F32)]
    for i in range(4):
        whole[at_block(info[1] ^ (2 * i), size), :] = evens[i][:size, :].astype(F32)
        whole[at_block(info[1] ^ (2 * i + 1), size), :] = beside[i, :size, :].astype(F32)
        if i > 0:
            norms.append(evens[i][size:, :].astype(F32) + beside[i, size:, :].astype(F32))
    norms = (norms[0] + norms[1]) + (norms[2] + norms[3])
    norms = norms[:8] + norms[8:16]
    norm_gain[...] = norms[0:1, :width]
    norm_shift[...] = norms[1:2, :width]
    columns = weight_grad.shape[2]
    for c in range(3):
        turned = whole[c * columns : (c + 1) * columns, :].T
        weight_grad[c] = turned[:width, :]
        bias_grad[c : c + 1, :] = turned[width : width + 1, :]
    out_grad[...] = whole[3 * columns : 4 * columns, :width]
    for place, target in enumerate((gain, shift, out_bias, down_bias)):
        target[...] = whole[4 * columns + place : 4 * columns + place + 1, :width]
    block = up_bias.shape[0] // 8
    for j in range(8):
        line[:, j * block : (j + 1) * block] = whole[
            4 * columns + 4 + j : 4 * columns + 5 + j, :block
        ]
    up_bias[...] = line[0, :]


def swap(values, axis, bit):
    size = lax.axis_size(axis)
    return lax.ppermute(values, axis, [(i, i ^ bit) for i in range(size)])


def gather_four(own, *others):
    beside = swap(own, "tensor", 1)
    across = swap(own, "tensor", 2)
    return [own, beside, across, swap(after(across, *others), "tensor", 1)]


def spread_four(own, near, cross, *others):
    beside = swap(near, "tensor", 1)
    across = swap(cross, "tensor", 2)
    return [own, beside, across, swap(after(across, *others), "tensor", 1)]


def add_low(*parts):
    total = parts[0].astype(F32)
    for part in parts[1:]:
        total = total + part.astype(F32)
    return total.astype(BF16)


def gather_feed_plain(up, down, core):
    pair = jnp.stack([up, down.T])
    pair = lax.all_gather(pair, "tensor", axis=1, tiled=True)
    pair = lax.all_gather(pair, "dp", axis=2, tiled=True)
    pair = pair.reshape(2, pair.shape[1], 8, -1).transpose(0, 2, 1, 3)
    pair = jnp.pad(pair, ((0, 0), (0, 0), (0, 0), (0, BLOCK - pair.shape[3])))
    pair = jnp.where(core == 0, pair, pair[::-1])
    feeds = []
    for half in (pair[0], pair[1]):
        feeds += [half[0], half[1], half[2], half[3], half[4::2], half[5::2]]
    return feeds


def scatter_feed_plain(kept, sent, core, hidden_count):
    grads = jnp.stack([kept, sent]).swapaxes(1, 2).reshape(2, 8, *kept.shape[2:])
    grads = jnp.where(core == 0, grads, grads[::-1]).astype(F32)
    grads = grads[:, :, :, : hidden_count * lax.axis_size("dp") // 8]
    grads = grads.transpose(0, 2, 1, 3).reshape(2, grads.shape[2], -1)
    grads = lax.psum_scatter(grads, "dp", scatter_dimension=2, tiled=True)
    grads = lax.psum_scatter(grads, "tensor", scatter_dimension=1, tiled=True)
    return grads[0], grads[1].T


def sum_pieces(even, beside, norm_sums):
    parts = call(
        add_pieces_kernel,
        (even, beside),
        [shape(even.shape[1:], BF16)] * 4,
        limit=4,
    )
    parts = [parts[0]] + [swap(parts[i], "dp", 2 * i) for i in (1, 2, 3)]
    norm_sums = norm_sums + swap(norm_sums, "tensor", 1)
    (own,) = call(
        own_piece_kernel,
        (*parts, norm_sums),
        [shape((even.shape[1] + 16, LANES), BF16)],
        limit=4,
    )
    back = [own] + [swap(own, "dp", e) for e in (2, 4, 6)]
    return back + [swap(jnp.stack(back), "dp", 1)], own


def sum_pieces_plain(even, odd, norm_sums):
    even, odd = (lax.psum(part.astype(F32), "dp").astype(BF16) for part in (even, odd))
    norm_sums = lax.psum(norm_sums, ("dp", "tensor"))
    high = norm_sums.astype(BF16)
    rest = (norm_sums - high.astype(F32)).astype(BF16)
    rows = jnp.concatenate([high, rest])
    rows = jnp.pad(rows, ((0, 0), (0, LANES - rows.shape[1])))
    even = jnp.concatenate([even, jnp.stack([rows] + [jnp.zeros_like(rows)] * 3)], axis=1)
    odd = jnp.concatenate([odd, jnp.zeros((4, *rows.shape), BF16)], axis=1)
    return [even[i] for i in range(4)] + [odd]


def shards(
    hidden_in,
    attn_gain,
    attn_shift,
    query_key_value_weight,
    query_key_value_bias,
    attention_output_weight,
    out_bias,
    ffn_gain,
    ffn_shift,
    up_projection_weight,
    up_projection_bias,
    down_projection_weight,
    down_bias,
    lengths,
    cotangent,
):
    chunks = lax.axis_size("tensor")
    ring = lax.axis_size("dp") == 8
    position = lax.axis_index("tensor")
    index = lax.axis_index("dp") if ring else jnp.int32(0)
    core = position & 1
    rows, chunk, width = hidden_in.shape
    full = chunk * chunks
    columns = query_key_value_weight.shape[2]
    heads = columns // HEAD_DIM
    hidden_count = up_projection_weight.shape[1]
    blocks = 8
    half = rows // 2

    info = jnp.stack([position, index]).astype(jnp.int32)
    lengths = lengths.astype(jnp.int32)
    inner_table, outer_table = (jnp.asarray(table) for table in rotary_constants(chunk, chunks))
    hidden = hidden_in.transpose(0, 2, 1)
    given = cotangent.transpose(0, 2, 1)

    if ring:
        inputs = (info, up_projection_weight, down_projection_weight)
        (pair,) = call(
            pair_kernel,
            inputs,
            [shape((columns, 2 * BLOCK), BF16)],
            scratch=[pltpu.VMEM(part.shape, part.dtype) for part in inputs[1:]]
            + [pltpu.SemaphoreType.DMA((2,))],
            in_specs=[smem()] + hbm(2),
            limit=4,
            tiles=20,
        )
        pair_across = swap(pair, "tensor", 2)
    inputs = (
        lengths,
        after(hidden, pair) if ring else hidden,
        attn_gain[None],
        attn_shift[None],
        attention_output_weight,
    )
    first, second = call(
        norm_kernel,
        inputs,
        [
            shape((half * width, chunk), BF16),
            shape((half * width + 2 * columns, chunk), BF16),
        ],
        scratch=[pltpu.VMEM(part.shape, part.dtype) for part in inputs[1:]]
        + [pltpu.VMEM((128, width), F32), pltpu.SemaphoreType.DMA((8,))],
        in_specs=[smem()] + hbm(4),
        limit=8,
        tiles=80,
    )
    inputs = (
        info,
        attn_gain[None],
        attn_shift[None],
        out_bias[None],
        ffn_gain[None],
        ffn_shift[None],
        down_bias[None],
        up_projection_bias[None],
        query_key_value_weight,
        query_key_value_bias,
    )
    weight, weight_turned, vectors, bias, up_bias, vector_rows = call(
        lambda *refs: prepare_kernel(heads, *refs),
        inputs,
        [
            shape((3 * columns, width), BF16),
            shape((width, 3 * columns), BF16),
            shape((width, 128), F32),
            shape((3 * columns, 128), F32),
            shape((BLOCK, 128), F32),
            shape((8, width), F32),
        ],
        scratch=[
            pltpu.VMEM((3 * columns, width), F32),
            pltpu.VMEM((128, BLOCK), F32),
        ]
        + [pltpu.VMEM(part.shape, part.dtype) for part in inputs[1:]]
        + [pltpu.SemaphoreType.DMA((9,))],
        in_specs=[smem()] + hbm(len(inputs) - 1),
        limit=8,
        tiles=60,
    )
    if ring:
        parts = [
            pair,
            swap(pair, "tensor", 1),
            pair_across,
            swap(after(pair_across, first), "tensor", 1),
        ]
        (own_feed,) = call(
            lambda *refs: assemble_kernel(chunks, *refs),
            (info, *parts),
            [shape((width, BLOCK), BF16)],
            scratch=[pltpu.VMEM((width, BLOCK), F32)],
            in_specs=[smem()] + vmem(chunks),
            limit=6,
            tiles=20,
        )
        came = [swap(own_feed, "dp", e) for e in (2, 4, 6)]
        beside = swap(own_feed, "dp", 1)
        second_beside = swap(came[0], "dp", 1)
        gathered = [
            gather_four(after(first, pair_across), own_feed, came[0], beside, weight)
        ]
    else:
        gathered = [gather_four(first)]

    kept = []
    mixed = []
    for g in range(2):
        if g == 1 and ring:
            gathered[1][0] = after(gathered[1][0], duo, beside, second_beside)
        inputs = (info, lengths, *gathered[g], weight, bias, inner_table, outer_table)
        outs = call(
            lambda *refs, g=g: attend_kernel(heads, chunks, chunk, g * half, half, *refs),
            inputs,
            [
                shape((half, 128, chunk), BF16),
                shape((half, 128, chunk), BF16),
                shape((half, 2, 128, chunk), BF16),
            ]
            + [shape((half, heads, HEAD_ROWS, full), BF16)] * 3
            + [
                shape((half, 8, full), F32),
                shape((half, 128, full), F32),
                shape((half, width, full), BF16),
            ],
            scratch=[
                pltpu.VMEM((heads, full, HEAD_ROWS), BF16),
                pltpu.VMEM((8, full), F32),
                pltpu.VMEM((3 * columns, full), F32),
                pltpu.VMEM((half, width, full), BF16),
                pltpu.SemaphoreType.DMA((half,)),
            ],
            in_specs=[smem(), smem()] + vmem(len(inputs) - 2),
            out_specs=vmem(8) + hbm(),
            limit=14,
            tiles=400,
        )
        kept.append(outs[3:])
        mixed.append(outs[:3])
        if g == 0:
            gathered.append(gather_four(second, outs[0]))
            if ring:
                duo = jnp.stack([after(part, outs[0], second_beside) for part in came[1:]])
                duo_beside = swap(duo, "dp", 1)
            else:
                feeds = gather_feed_plain(up_projection_weight, down_projection_weight, core)

    if ring:
        duo_beside = after(duo_beside, kept[1][0])
        feeds = [own_feed, beside, came[0], second_beside, duo, duo_beside]
        feeds += [swap(part, "tensor", 1) for part in feeds]
    feed_outs = []
    for g in range(2):
        last = g == 1
        others = (kept[1][0],) if g == 0 else (feed_outs[0][2],)
        inputs = (
            info,
            lengths,
            hidden,
            given,
            vectors,
            up_bias,
            *spread_four(*mixed[g], *others),
            *gathered[1],
        )
        if last:
            inputs = inputs + tuple(feed_outs[0][5:]) + (feed_outs[0][0],)
        else:
            inputs = inputs + tuple(feeds)
        carried = [
            shape((2, width, blocks * BLOCK), BF16),
            shape((2, width, blocks * BLOCK), F32),
            shape((chunks * 128, width), F32),
            shape((4, width, 128), F32),
            shape((blocks, BLOCK, 128), F32),
        ]
        sent = [
            shape((2, blocks // 2, width, BLOCK), BF16),
            shape((2, blocks // 2, width, BLOCK), BF16),
            shape((144, LANES), BF16),
            shape((2, 144, LANES), BF16),
            shape((144, LANES), BF16),
        ]
        tokens = half * chunk
        outs = call(
            lambda *refs, g=g, last=last: feed_kernel(
                chunks, blocks, g * half, half, last, *refs
            ),
            inputs,
            [
                shape((rows if last else half, width, chunk), BF16),
                shape((half, width, chunk), F32),
                shape((half, 128, chunk), BF16),
                shape((half, 128, chunk), BF16),
                shape((half, 2, 128, chunk), BF16),
            ]
            + (sent if last else carried),
            scratch=[
                pltpu.VMEM((chunks * 128, width), BF16),
                pltpu.VMEM((chunks * 128, tokens), BF16),
                pltpu.VMEM((width, tokens), F32),
                pltpu.VMEM((width, tokens), BF16),
                pltpu.VMEM((width, tokens), BF16),
                pltpu.VMEM((width, tokens), F32),
                pltpu.VMEM((width, tokens), F32),
                pltpu.VMEM((2, 2 * BLOCK, tokens), F32),
                pltpu.VMEM((2, 2 * BLOCK, tokens), F32),
                pltpu.VMEM((2, 2 * BLOCK, tokens), BF16),
                pltpu.VMEM((2, 2 * BLOCK, tokens), BF16),
                pltpu.VMEM((4, width, 128), F32),
                pltpu.VMEM((blocks, BLOCK, 128), F32),
                pltpu.VMEM((16, LANES), F32),
                pltpu.SemaphoreType.DMA((2, blocks)),
            ],
            in_specs=[smem(), smem()]
            + (
                vmem(len(inputs) - 2)
                if last
                else vmem(len(inputs) - 2 - len(feeds)) + [pl.BlockSpec(memory_space=pl.ANY)] * len(feeds)
            ),
            limit=22,
            tiles=500,
        )
        feed_outs.append(outs)
    hidden_out = feed_outs[1][0]
    middle_grads = [outs[1] for outs in feed_outs]
    feed_kept, feed_sent, out_own, out_near, out_cross = feed_outs[1][5:]

    mixed_grads = [spread_four(*feed_outs[0][2:5], feed_outs[1][2])]
    feed_sent, out_near = after((feed_sent, out_near), mixed_grads[0][2])
    out_came = swap(out_near, "tensor", 1)
    feed_came = swap(feed_sent, "tensor", 1)
    running = None
    reduced = []
    crossing = []
    for r in range(rows):
        last = r == rows - 1
        g = r // half
        inputs = (
            info,
            lengths,
            *mixed_grads[g],
            *kept[g],
            weight_turned,
            inner_table,
            outer_table,
        )
        if last and ring:
            running = after(running, *evens)
        if r > 0:
            inputs = inputs + (running,)
        if last:
            inputs = inputs + (out_own, out_came, out_across, weight, vector_rows)
        outs = call(
            lambda *refs, r=r, last=last: attend_back_kernel(
                heads, chunks, chunk, r, r % half, r == 0, last, *refs
            ),
            inputs,
            [
                shape((width, chunk), BF16),
                shape((2, width, chunk), BF16),
                shape((width, chunk), BF16),
            ]
            + (
                [shape((4, 64, LANES), BF16)] * 2 + [shape((8, width), F32)]
                if last
                else [shape((3 * columns, LANES + 128), F32)]
            ),
            scratch=[
                pltpu.VMEM((128, full), BF16),
                pltpu.VMEM((heads, HEAD_ROWS, full), BF16),
                pltpu.VMEM((heads, HEAD_ROWS, full), BF16),
                pltpu.VMEM((heads, full, HEAD_ROWS), BF16),
                pltpu.VMEM((heads, full, HEAD_ROWS), BF16),
                pltpu.VMEM((3, columns, full), F32),
                pltpu.VMEM((3 * columns, full), BF16),
                pltpu.VMEM((512, LANES), F32),
                pltpu.VMEM((width, full), BF16),
                pltpu.SemaphoreType.DMA(()),
            ],
            in_specs=[smem(), smem()] + vmem(9) + hbm() + vmem(len(inputs) - 12),
            limit=12,
            tiles=420,
        )
        if last:
            outs = list(outs)
            even, odd, norm_sums = outs[3:]
            if ring:
                odd = after(odd, reduced[5], *feed_came)
                beside_pieces = swap(odd, "dp", 1)
                norm_sums = norm_sums + swap(norm_sums, "tensor", 2)
                outs[1] = after(outs[1], beside_pieces, norm_sums)
        near = swap(outs[1], "tensor", 1)
        reduced += [outs[0], near, None]
        crossing.append((outs[2], near))
        if r >= 2:
            pair_sum = jnp.stack(
                [
                    add_low(after(cross, outs[0], out_across), near[1])
                    for cross, near in crossing[2 * r - 4 : 2 * r - 2]
                ]
            )
            reduced[3 * (2 * r - 3) + 2] = swap(pair_sum, "tensor", 2)
        if not last:
            running = outs[3]
        if r == 1:
            mixed_grads.append(spread_four(*feed_outs[1][2:5], outs[0]))
        if r == 0:
            out_across = swap(
                add_low(after(out_cross, outs[0]), out_came[1]), "tensor", 2
            )
            if ring:
                feed_odd = add_low(after(feed_kept[1], outs[0]), feed_came[1])
                running = after(running, feed_odd)
                feed_odd = swap(feed_odd, "dp", 1)
        if r == 2 and ring:
            feed_kept = after(feed_kept, outs[0])
            evens = [
                add_low(feed_kept[0, i], feed_came[0, i], feed_odd[i]) for i in range(4)
            ]
            feed_came = [swap(evens[i], "dp", 2 * i) for i in (1, 2, 3)]
    own_parts = [part for place, part in enumerate(reduced) if place % 3 < 2]
    cross_parts = [part for part in reduced[2::3] if part is not None]
    inputs = (lengths, hidden, vectors, *middle_grads, *own_parts, *cross_parts)
    (grad_hidden,) = call(
        lambda *refs: norm_back_kernel(rows, *refs),
        inputs,
        [shape((rows, width, chunk), BF16)],
        in_specs=[smem()] + vmem(len(inputs) - 1),
        limit=12,
        tiles=120,
    )
    if ring:
        parts, own = sum_pieces(even, beside_pieces, norm_sums)
    else:
        parts = sum_pieces_plain(even, odd, norm_sums)
    if ring:
        keep, send = call(
            feed_sum_kernel,
            (info, after(evens[0], own), *feed_came),
            [shape((width // 2, BLOCK), BF16)] * 2,
            scratch=[pltpu.VMEM((width, BLOCK), F32)],
            in_specs=[smem()] + vmem(4),
            limit=4,
            tiles=20,
        )
        mine, other = call(
            feed_pair_kernel,
            (info, keep, after(swap(send, "tensor", 2), grad_hidden)),
            [shape((columns, BLOCK), BF16)] * 2,
            scratch=[pltpu.VMEM((width // 2, BLOCK), F32)],
            in_specs=[smem()] + vmem(2),
            limit=4,
            tiles=20,
        )
        feed_parts = (mine, swap(other, "tensor", 1))
    else:
        grad_up_weight, grad_down_weight = scatter_feed_plain(
            feed_kept, feed_sent, core, hidden_count
        )

    inputs = (info, *parts) + (feed_parts if ring else ())
    outs = [
        shape((3, width, columns), F32),
        shape((3, columns), F32),
        shape((columns, width), F32),
    ]
    outs += [shape((1, width), F32)] * 4
    outs += [shape(up_projection_bias.shape, F32)]
    outs += [shape((1, width), F32)] * 2
    if ring:
        outs += [shape((columns, hidden_count), F32), shape((hidden_count, columns), F32)]
    outs = call(
        unpack_kernel,
        inputs,
        outs,
        scratch=[
            pltpu.VMEM((512, LANES), F32),
            pltpu.VMEM((1, up_projection_bias.shape[0]), F32),
        ],
        in_specs=[smem()] + vmem(len(inputs) - 1),
        limit=8,
        tiles=60,
    )
    grad_qkv_weight, grad_qkv_bias, grad_out_weight = outs[:3]
    grad_ffn_gain, grad_ffn_shift, grad_out_bias, grad_down_bias, grad_up_bias = outs[3:8]
    grad_attn_gain, grad_attn_shift = outs[8:10]
    if ring:
        grad_up_weight, grad_down_weight = outs[10:]
    return (
        hidden_out.transpose(0, 2, 1),
        grad_hidden.transpose(0, 2, 1),
        grad_attn_gain[0],
        grad_attn_shift[0],
        grad_qkv_weight,
        grad_qkv_bias,
        grad_out_weight,
        grad_out_bias[0],
        grad_ffn_gain[0],
        grad_ffn_shift[0],
        grad_up_weight,
        grad_up_bias,
        grad_down_weight,
        grad_down_bias[0],
    )


def solution(mesh):
    return jax.shard_map(
        shards,
        mesh=mesh,
        in_specs=(
            P("dp", "tensor", None),
            P(),
            P(),
            P(None, None, "tensor"),
            P(None, "tensor"),
            P("tensor", None),
            P(),
            P(),
            P(),
            P("tensor", "dp"),
            P(),
            P("dp", "tensor"),
            P(),
            P("dp"),
            P("dp", "tensor", None),
        ),
        out_specs=(
            P("dp", "tensor", None),
            P("dp", "tensor", None),
            P(),
            P(),
            P(None, None, "tensor"),
            P(None, "tensor"),
            P("tensor", None),
            P(),
            P(),
            P(),
            P("tensor", "dp"),
            P(),
            P("dp", "tensor"),
            P(),
        ),
        check_vma=False,
    )
```

```python
import math

import jax
import jax.numpy as jnp
import numpy as np
from jax import lax
from jax.experimental import pallas as pl
from jax.experimental.pallas import tpu as pltpu
from jax.sharding import PartitionSpec as P

HEAD_DIM = 24
HEAD_ROWS = 32
EPS = 1e-05
MASK_FILL = -1000000000.0
LOG2E = math.log2(math.e)
SAFE_SCORE = 85.0
WORK_SCALE = 0.01
BLOCK = 256
KEY_STEP = 256
LANES = 512
BF16 = jnp.bfloat16
F32 = jnp.float32

NN = (((1,), (0,)), ((), ()))
NT = (((1,), (1,)), ((), ()))
TN = (((0,), (0,)), ((), ()))


def product(left, right, dims=NN):
    return lax.dot_general(left, right, dims, preferred_element_type=F32)


def vmem(count):
    return [pl.BlockSpec(memory_space=pltpu.VMEM)] * count


def smem():
    return pl.BlockSpec(memory_space=pltpu.SMEM)


def hbm(count=1):
    return [pl.BlockSpec(memory_space=pltpu.HBM)] * count


def call(kernel, inputs, outs, scratch=(), in_specs=None, out_specs=None, limit=40, tiles=0):
    flops = int(2 * 256**3 * tiles * WORK_SCALE)
    in_specs = vmem(len(inputs)) if in_specs is None else in_specs
    inputs = [
        pltpu.with_memory_space_constraint(part, pltpu.HBM)
        if spec.memory_space is pltpu.HBM
        else part
        for part, spec in zip(inputs, in_specs)
    ]
    out_specs = vmem(len(outs)) if out_specs is None else out_specs
    outs = [
        pltpu.HBM(part.shape, part.dtype) if spec.memory_space is pltpu.HBM else part
        for part, spec in zip(outs, out_specs)
    ]
    return pl.pallas_call(
        kernel,
        out_shape=outs,
        in_specs=in_specs,
        out_specs=out_specs,
        scratch_shapes=list(scratch),
        compiler_params=pltpu.CompilerParams(vmem_limit_bytes=limit << 20),
        cost_estimate=pl.CostEstimate(flops=flops, transcendentals=0, bytes_accessed=0),
    )(*inputs)


def shape(dims, dtype):
    return jax.ShapeDtypeStruct(dims, dtype)


def at_block(index, size):
    return pl.ds(pl.multiple_of(index * size, size), size)


def split_three(values):
    high = values.astype(BF16).astype(F32)
    rest = values - high
    middle = rest.astype(BF16).astype(F32)
    return high, middle, rest - middle


def row_of(lengths, slot, rows):
    slot = jnp.where(slot == 0, 0, jnp.where(slot == 1, rows - 1, slot - 1))
    chosen = jnp.int32(0)
    for i in range(rows):
        rank = jnp.int32(0)
        for j in range(rows):
            if j < i:
                rank += jnp.where(lengths[j] <= lengths[i], 1, 0)
            elif j > i:
                rank += jnp.where(lengths[j] < lengths[i], 1, 0)
        chosen += jnp.where(rank == slot, i, 0)
    return chosen


def after(values, *others):
    return lax.optimization_barrier((values, *others))[0]


def norm_columns(values):
    centre = values - jnp.mean(values, axis=0, keepdims=True)
    inverse = lax.rsqrt(jnp.mean(centre * centre, axis=0, keepdims=True) + EPS)
    return centre * inverse, inverse


def norm_columns_back(upstream, unit, inverse, gain):
    scaled = upstream * gain
    centred = scaled - jnp.mean(scaled, axis=0, keepdims=True)
    return inverse * (centred - unit * jnp.mean(scaled * unit, axis=0, keepdims=True))


def pair_kernel(info, up, down, pair, up_inside, down_inside, semaphores):
    copies = [
        pltpu.make_async_copy(up, up_inside, semaphores.at[0]),
        pltpu.make_async_copy(down, down_inside, semaphores.at[1]),
    ]
    for copy in copies:
        copy.start()
    pair[...] = jnp.zeros_like(pair)
    for copy in copies:
        copy.wait()
    size = up.shape[1]
    up_half = up_inside[...]
    down_half = down_inside[...].astype(F32).T.astype(BF16)

    @pl.when(info[0] & 1 == 0)
    def _():
        pair[:, :size] = up_half
        pair[:, BLOCK : BLOCK + size] = down_half

    @pl.when(info[0] & 1 == 1)
    def _():
        pair[:, :size] = down_half
        pair[:, BLOCK : BLOCK + size] = up_half


def norm_kernel(
    lengths,
    hidden_in,
    gain,
    shift,
    out_weight_in,
    first_out,
    second_out,
    hidden,
    gain_inside,
    shift_inside,
    out_weight,
    rows_scratch,
    semaphores,
):
    rows, width, chunk = hidden.shape
    copies = [
        pltpu.make_async_copy(
            hidden_in.at[row_of(lengths, slot, rows)], hidden.at[slot], semaphores.at[slot]
        )
        for slot in range(rows)
    ]
    others = [
        pltpu.make_async_copy(gain, gain_inside, semaphores.at[4]),
        pltpu.make_async_copy(shift, shift_inside, semaphores.at[5]),
        pltpu.make_async_copy(out_weight_in, out_weight, semaphores.at[6]),
    ]
    for copy in others[:2] + copies + others[2:]:
        copy.start()
    rows_scratch[...] = jnp.zeros_like(rows_scratch)
    others[0].wait()
    others[1].wait()
    rows_scratch[0:1, :] = gain_inside[...]
    rows_scratch[1:2, :] = shift_inside[...]
    columns = rows_scratch[...].T
    half = rows // 2
    for row in range(rows):
        copies[row].wait()
        unit, _ = norm_columns(hidden[row].astype(F32))
        target = first_out if row < half else second_out
        place = row % half * width
        target[place : place + width, :] = (unit * columns[:, 0:1] + columns[:, 1:2]).astype(
            BF16
        )
    others[2].wait()
    own = out_weight.shape[0]
    second_out[half * width : half * width + own, :] = out_weight[:, :chunk]
    rest = width - chunk
    second_out[half * width + own : half * width + 2 * own, :] = jnp.zeros((own, chunk), BF16)
    second_out[half * width + own : half * width + 2 * own, :rest] = out_weight[:, chunk:]


def prepare_kernel(heads, info, *refs):
    outside, refs = refs[:9], refs[9:]
    weight_out, weight_turned_out, columns_out, bias_out, up_bias_out, vector_rows = refs[:6]
    weight_scratch, bias_rows = refs[6:8]
    inside, semaphores = refs[8:17], refs[17]
    copies = [
        pltpu.make_async_copy(source, target, semaphores.at[place])
        for place, (source, target) in enumerate(zip(outside, inside))
    ]
    for copy in copies:
        copy.start()
    vectors, (up_bias, weight, bias) = inside[:6], inside[6:]
    width = weight.shape[1]
    vector_rows[...] = jnp.zeros_like(vector_rows)
    for copy in copies:
        copy.wait()
    for place, vector in enumerate(vectors):
        vector_rows[place : place + 1, :] = vector[...]
    columns_out[...] = jnp.concatenate([vector_rows[...], jnp.zeros((120, width), F32)]).T
    span = heads * HEAD_DIM
    for c in range(3):
        own = slice(c * span, (c + 1) * span)
        weight_scratch[own, :] = weight[c].astype(F32).T
        bias_out[own, :] = jnp.broadcast_to(bias[c : c + 1, :], (128, span)).T
    weight_out[...] = weight_scratch[...].astype(BF16)
    weight_turned_out[...] = weight_scratch[...].T.astype(BF16)
    bias_rows[...] = jnp.zeros_like(bias_rows)
    count = up_bias.shape[1]
    block = count // 8
    spread = jnp.broadcast_to(up_bias[...], (8, count))
    for j in range(8):
        moved = pltpu.roll(spread, lax.rem(count - (info[1] ^ j) * block, count), 1)
        bias_rows[j : j + 1, :block] = moved[0:1, :block]
    up_bias_out[...] = bias_rows[...].T


def assemble_kernel(chunks, info, *refs):
    parts, (out, rows) = refs[:chunks], refs[chunks:]
    size = parts[0].shape[0]
    for k in range(chunks):
        half = parts[k][:, (k & 1) * BLOCK : ((k & 1) + 1) * BLOCK]
        rows[at_block(info[0] ^ k, size), :] = half.astype(F32)
    out[...] = rows[...].astype(BF16)


def rotary_constants(chunk, chunks):
    half = HEAD_DIM // 2
    element = np.arange(HEAD_DIM)
    frequency = (1.0 / 10000.0 ** (np.arange(0, HEAD_DIM, 2).astype(np.float32) / HEAD_DIM)).astype(
        np.float32
    )
    per_row = frequency[element % half].astype(np.float64)
    inner = per_row[:, None] * np.arange(chunk)[None, :]
    outer = per_row[:, None] * (np.arange(chunks) * chunk)[None, :]
    outer = np.repeat(outer[:, :, None], chunk, axis=2).transpose(1, 0, 2)
    inner_pair = np.stack([np.cos(inner), np.sin(inner)]).astype(np.float32)
    outer_pair = np.stack([np.cos(outer), np.sin(outer)]).astype(np.float32)
    return inner_pair, outer_pair


def chunk_tables(inner, outer, index):
    cos_in, sin_in = inner[0], inner[1]
    cos_out, sin_out = outer[0, index], outer[1, index]
    element = lax.broadcasted_iota(jnp.int32, cos_in.shape, 0)
    sine = sin_in * cos_out + cos_in * sin_out
    return cos_in * cos_out - sin_in * sin_out, jnp.where(
        element < HEAD_DIM // 2, -sine, sine
    )


def swap_halves(values):
    return pltpu.roll(values, HEAD_DIM // 2, 0)


def attend_kernel(heads, chunks, chunk, first_row, rows, info, lengths, *refs):
    parts = refs[:chunks]
    weight, bias, inner, outer, own_out, near_out, cross_out = refs[chunks : chunks + 7]
    queries, keys, values, logsum, mixed_turned, normed_out, key_rows, peak, flat = refs[
        chunks + 7 : chunks + 16
    ]
    normed, semaphores = refs[chunks + 16 :]
    position = info[0]
    width = normed.shape[1]
    full = chunk * chunks
    span = heads * HEAD_DIM
    scale = LOG2E * HEAD_DIM**-0.5

    def one_row(r, carry):
        length = lengths[row_of(lengths, first_row + r, lengths.shape[0])]
        for k in range(chunks):
            normed[r, :, at_block(position ^ k, chunk)] = parts[k][at_block(r, width), :]
        pltpu.make_async_copy(normed.at[r], normed_out.at[r], semaphores.at[r]).start()
        flat[...] = product(weight[...], normed[r])
        line = lax.broadcasted_iota(jnp.int32, (8, chunk), 0)
        ones = jnp.where(line < 3, 1.0, 0.0)
        query_line = jnp.where(line == 3, 1.0, 0.0)
        query_top = [jnp.zeros((1, chunk), F32) for _ in range(heads)]
        key_top = [jnp.zeros((1, chunk), F32) for _ in range(heads)]
        for j in range(chunks):
            at = slice(j * chunk, (j + 1) * chunk)
            cosine, sine = chunk_tables(inner, outer, j)
            query_cosine, query_sine = cosine * scale, sine * scale
            place = lax.broadcasted_iota(jnp.int32, (8, chunk), 1) + j * chunk
            key_line = jnp.where((line == 3) & (place >= length), MASK_FILL, ones)
            for h in range(heads):
                here = h * HEAD_DIM
                query, key, value = (
                    flat[c * span + here : c * span + here + HEAD_DIM, at]
                    + jnp.concatenate(
                        [bias[c * span + here : c * span + here + HEAD_DIM, :]] * (chunk // 128),
                        axis=1,
                    )
                    for c in range(3)
                )
                query = query * query_cosine + swap_halves(query) * query_sine
                key = key * cosine + swap_halves(key) * sine
                query_top[h] = jnp.maximum(
                    query_top[h], jnp.sum(query * query, axis=0, keepdims=True)
                )
                key_top[h] = jnp.maximum(key_top[h], jnp.sum(key * key, axis=0, keepdims=True))
                key_full = jnp.concatenate([key, key_line])
                queries[r, h, :, at] = jnp.concatenate([query, query_line]).astype(BF16)
                keys[r, h, :, at] = key_full.astype(BF16)
                values[r, h, :, at] = jnp.concatenate([value, ones]).astype(BF16)
                key_rows[h, at, :] = key_full.T.astype(BF16)
        bound = jnp.zeros((1, 1), F32)
        for h in range(heads):
            bound = jnp.maximum(
                bound,
                jnp.max(query_top[h], axis=-1, keepdims=True)
                * jnp.max(key_top[h], axis=-1, keepdims=True),
            )
        safe = jnp.max(bound) <= SAFE_SCORE * SAFE_SCORE
        peak[...] = jnp.zeros_like(peak)

        @pl.when(jnp.logical_not(safe))
        def _():
            def one_head(h, carry):
                scores = product(key_rows[h], queries[r, h])
                peak[pl.ds(h, 1), :] = (
                    jnp.max(scores, axis=0, keepdims=True).astype(BF16).astype(F32)
                )
                return carry

            lax.fori_loop(0, heads, one_head, 0)

        head_line = lax.broadcasted_iota(jnp.int32, (HEAD_ROWS, full), 0)

        def with_keys(count):
            def one_head(h, carry):
                top = peak[pl.ds(h, 1), :]
                query = jnp.where(
                    head_line == HEAD_DIM, -top, queries[r, h].astype(F32)
                ).astype(BF16)
                exponent = jnp.exp2(product(key_rows[h, :count, :], query)).astype(BF16)
                blend = product(values[r, h, :, :count], exponent)
                total = blend[HEAD_DIM : HEAD_DIM + 1, :]
                logsum[r, pl.ds(h, 1), :] = top + jnp.log2(total)
                mixed_turned[r, pl.ds(pl.multiple_of(h * HEAD_DIM, 8), HEAD_DIM), :] = blend[
                    :HEAD_DIM
                ] * (1.0 / total)
                return carry

            lax.fori_loop(0, heads, one_head, 0, unroll=True)

        blocks = jnp.maximum((length + KEY_STEP - 1) // KEY_STEP, 1)
        for b in range(1, full // KEY_STEP + 1):
            pl.when(blocks == b)(lambda b=b: with_keys(b * KEY_STEP))
        mixed_turned[r, span:, :] = jnp.zeros((mixed_turned.shape[1] - span, full), F32)
        own_out[r] = mixed_turned[r, :, at_block(position, chunk)].astype(BF16)
        near_out[r] = mixed_turned[r, :, at_block(position ^ 1, chunk)].astype(BF16)
        cross_out[r, 0] = mixed_turned[r, :, at_block(position ^ 2, chunk)].astype(BF16)
        cross_out[r, 1] = mixed_turned[r, :, at_block(position ^ 3, chunk)].astype(BF16)
        return carry

    lax.fori_loop(0, rows, one_row, 0)
    for r in range(rows):
        pltpu.make_async_copy(normed.at[r], normed_out.at[r], semaphores.at[r]).wait()


def attend_back_kernel(heads, chunks, chunk, row, local, first, last, info, lengths, *refs):
    upstream_own, upstream_near, upstream_cross, upstream_far = refs[:4]
    queries, keys, values, logsum, mixed_turned, normed_in, weight_turned, inner, outer = refs[
        4:13
    ]
    refs = refs[13:]
    if not first:
        carried = refs[0]
        refs = refs[1:]
    if last:
        out_own, out_near, out_cross, weight, vector_rows = refs[:5]
        refs = refs[5:]
    own_out, near_out, cross_out = refs[:3]
    refs = refs[3:]
    if last:
        even_pieces, odd_pieces, norm_sums = refs[:3]
        refs = refs[3:]
    else:
        running = refs[0]
        refs = refs[1:]
    (
        upstream,
        query_full,
        upstream_full,
        key_rows,
        value_rows,
        grads,
        grad_low,
        packed,
        normed,
        semaphore,
    ) = refs
    fetch = pltpu.make_async_copy(normed_in.at[local], normed, semaphore)
    fetch.start()
    position, index = info[0], info[1]
    length = lengths[row_of(lengths, row, lengths.shape[0])]
    full = chunk * chunks
    span = heads * HEAD_DIM
    upstream[:, at_block(position, chunk)] = upstream_own[local]
    upstream[:, at_block(position ^ 1, chunk)] = upstream_near[local]
    upstream[:, at_block(position ^ 2, chunk)] = upstream_cross[local, 0]
    upstream[:, at_block(position ^ 3, chunk)] = upstream_far[local, 1]
    zeros = jnp.zeros((5, chunk), F32)
    line = lax.broadcasted_iota(jnp.int32, (8, chunk), 0)
    for j in range(chunks):
        at = slice(j * chunk, (j + 1) * chunk)
        turned = upstream[:, at].astype(F32)
        blend = turned * mixed_turned[local, :, at]
        for h in range(heads):
            own = slice(h * HEAD_DIM, (h + 1) * HEAD_DIM)
            high, middle, rest = split_three(-jnp.sum(blend[own], axis=0, keepdims=True))
            extra = jnp.where(
                line == 0, high, jnp.where(line == 1, middle, jnp.where(line == 2, rest, 0.0))
            )
            upstream_full[h, :, at] = jnp.concatenate([turned[own], extra]).astype(BF16)
            high, middle, rest = split_three(-logsum[local, h : h + 1, at])
            extra = jnp.where(
                line == 0,
                high,
                jnp.where(
                    line == 1, middle, jnp.where(line == 2, rest, jnp.where(line == 3, 1.0, 0.0))
                ),
            )
            query = queries[local, h, :, at].astype(F32)[:HEAD_DIM]
            query_full[h, :, at] = jnp.concatenate([query, extra]).astype(BF16)
            key_rows[h, at, :] = keys[local, h, :, at].astype(F32).T.astype(BF16)
            value_rows[h, at, :] = values[local, h, :, at].astype(F32).T.astype(BF16)

    def with_keys(count):
        def one_head(h, carry):
            own = pl.ds(pl.multiple_of(h * HEAD_DIM, 8), HEAD_DIM)
            grad_query = jnp.zeros((HEAD_ROWS, full), F32)
            for place in range(0, count, BLOCK):
                at = slice(place, min(place + BLOCK, count))
                probs = jnp.exp2(product(key_rows[h, at, :], query_full[h])).astype(BF16)
                grad_probs = product(value_rows[h, at, :], upstream_full[h]).astype(BF16)
                grad_scores = probs * grad_probs
                grads[2, own, at] = product(upstream_full[h], probs, NT)[:HEAD_DIM]
                grads[1, own, at] = product(query_full[h], grad_scores, NT)[:HEAD_DIM]
                grad_query += product(keys[local, h, :, at], grad_scores)
            grads[0, own, :] = grad_query[:HEAD_DIM]
            return carry

        lax.fori_loop(0, heads, one_head, 0)
        if count < full:
            grads[1, :, count:] = jnp.zeros((span, full - count), F32)
            grads[2, :, count:] = jnp.zeros((span, full - count), F32)

    blocks = jnp.maximum((length + KEY_STEP - 1) // KEY_STEP, 1)
    for b in range(1, full // KEY_STEP + 1):
        pl.when(blocks == b)(lambda b=b: with_keys(b * KEY_STEP))

    sums = [[jnp.zeros((HEAD_DIM, 128), F32) for _ in range(heads)] for _ in range(3)]
    for j in range(chunks):
        at = slice(j * chunk, (j + 1) * chunk)
        cosine, sine = chunk_tables(inner, outer, j)
        query_cosine, query_sine = cosine * HEAD_DIM**-0.5, sine * HEAD_DIM**-0.5
        key_cosine, key_sine = cosine * (1.0 / LOG2E), sine * (1.0 / LOG2E)
        for h in range(heads):
            own = slice(h * HEAD_DIM, (h + 1) * HEAD_DIM)
            query, key, value = (grads[c, own, at] for c in range(3))
            query = query * query_cosine - swap_halves(query) * query_sine
            key = key * key_cosine - swap_halves(key) * key_sine
            for c, part in enumerate((query, key, value)):
                for piece in range(chunk // 128):
                    sums[c][h] = sums[c][h] + part[:, piece * 128 : (piece + 1) * 128]
                grads[c, own, at] = part
    for c in range(3):
        grad_low[c * span : (c + 1) * span, :] = grads[c].astype(BF16)
    for k in range(chunks):
        result = product(
            weight_turned[...], grad_low[:, at_block(position ^ k, chunk)]
        ).astype(BF16)
        if k == 0:
            own_out[...] = result
        elif k == 2:
            cross_out[...] = result
        else:
            near_out[k // 2] = result
    width = weight_turned.shape[0]
    fetch.wait()
    result = product(grad_low[...], normed[...], NT)
    bias_grad = jnp.concatenate(
        [jnp.sum(part, axis=1, keepdims=True) for group in sums for part in group]
    )
    bias_grad = jnp.broadcast_to(bias_grad, (3 * span, 128))
    if not first:
        result = result + carried[:, :width]
        bias_grad = bias_grad + carried[:, LANES:]
    if not last:
        running[:, :width] = result
        running[:, LANES:] = bias_grad
        return
    packed[: 3 * span, :width] = result
    gain_sum = jnp.zeros((8, width), F32)
    shift_sum = jnp.zeros((8, width), F32)
    gain, shift = vector_rows[0:1, :], vector_rows[1:2, :]
    for place in range(0, 3 * span, 8):
        own = slice(place, place + 8)
        factor = weight[own, :].astype(F32)
        column = bias_grad[own, 0:1]
        gain_sum = gain_sum + factor * (result[own] - shift * column)
        shift_sum = shift_sum + factor * column
    norm_sums[...] = jnp.zeros_like(norm_sums)
    norm_sums[0:1, :] = jnp.sum(gain_sum, axis=0, keepdims=True) / gain
    norm_sums[1:2, :] = jnp.sum(shift_sum, axis=0, keepdims=True)
    lane = lax.broadcasted_iota(jnp.int32, (3 * span, 128), 1)
    packed[: 3 * span, LANES - 128 :] = jnp.where(
        lane >= width - (LANES - 128), bias_grad, packed[: 3 * span, LANES - 128 :]
    )
    shared = (out_own[...].astype(F32) + out_near[0].astype(F32)) + out_cross[...].astype(F32)
    packed[3 * span : 4 * span, :] = shared[:span]
    packed[4 * span : 4 * span + 16, :] = shared[128:144]
    packed[4 * span + 16 :, :] = jnp.zeros((packed.shape[0] - 4 * span - 16, LANES), F32)
    size = packed.shape[0] // 8
    for j in range(8):
        target = odd_pieces if j % 2 else even_pieces
        target[j // 2] = packed[at_block(index ^ j, size), :].astype(BF16)


def gelu_parts(values):
    magnitude = jnp.abs(values) * (0.5**0.5)
    density = jnp.exp2(values * values * (-0.5 * LOG2E))
    divisor = 1.0 + 0.3275911 * magnitude
    step = pl.reciprocal(divisor, approx=True)
    step = step * (2.0 - divisor * step)
    series = 1.061405429 * step - 1.453152027
    series = series * step + 1.421413741
    series = series * step - 0.284496736
    series = series * step + 0.254829592
    tail = 0.5 * series * step * density
    share = jnp.where(values < 0, tail, 1.0 - tail)
    return share, density * (1.0 / math.sqrt(2.0 * math.pi))


def lane_groups(values):
    total = values[:, :128]
    for place in range(128, values.shape[1], 128):
        total = total + values[:, place : place + 128]
    return total


def row_sum(values):
    total = values[:8]
    for place in range(8, values.shape[0], 8):
        total = total + values[place : place + 8]
    return total


def feed_kernel(chunks, blocks, first_row, rows, last, info, lengths, *refs):
    hidden, cotangent, columns, up_bias = refs[:4]
    mixed_own, mixed_near, mixed_cross, mixed_far = refs[4:8]
    out_weight = refs[8 : 8 + chunks]
    refs = refs[8 + chunks :]
    if last:
        weights, carried, out_carried, sums_carried, bias_carried, hidden_before = refs[:6]
        refs = refs[6:]
    else:
        feeds, refs = refs[:12], refs[12:]
    hidden_out, grad_middle_out, grad_own, grad_near, grad_cross = refs[:5]
    refs = refs[5:]
    if last:
        kept_out, sent_out, out_own, out_near, out_cross = refs[:5]
    else:
        weights, carried, out_carried, sums_carried, bias_carried = refs[:5]
    refs = refs[5:]
    (
        out_rows,
        mixed,
        source,
        given,
        low_rows,
        down_total,
        back_total,
        upward,
        upstream,
        active,
        grad_low,
        sums_total,
        bias_total,
        shared,
        semaphores,
    ) = refs
    core, index = info[0] & 1, info[1]
    width, chunk = hidden.shape[1:]
    tokens = rows * chunk
    held = mixed_own.shape[1]
    places = [row_of(lengths, first_row + r, hidden.shape[0]) for r in range(rows)]
    if not last:
        copies = []
        for side in range(2):
            sources = list(feeds[6 * side : 6 * side + 4])
            duo, duo_beside = feeds[6 * side + 4 : 6 * side + 6]
            place = core if side == 0 else 1 - core
            for e in range(2):
                sources += [duo.at[e], duo_beside.at[e]]
            for j in range(blocks):
                copies.append(
                    pltpu.make_async_copy(
                        sources[j],
                        weights.at[place, :, j * BLOCK : (j + 1) * BLOCK],
                        semaphores.at[side, j],
                    )
                )
        for copy in copies:
            copy.start()
    own_rows = (out_weight[0].shape[0] - 2 * width) // 2
    for k in range(chunks):
        base = 2 * width
        at = k * held
        out_rows[at : at + held, :] = jnp.zeros((held, width), BF16)
        out_rows[at : at + own_rows, :chunk] = out_weight[k][base : base + own_rows, :]
        out_rows[at : at + own_rows, chunk:] = out_weight[k][
            base + own_rows : base + 2 * own_rows, : width - chunk
        ]
    for r in range(rows):
        at = slice(r * chunk, (r + 1) * chunk)
        mixed[0 * held : 1 * held, at] = mixed_own[r]
        mixed[1 * held : 2 * held, at] = mixed_near[r]
        mixed[2 * held : 3 * held, at] = mixed_cross[r, 0]
        mixed[3 * held : 4 * held, at] = mixed_far[r, 1]
        given[:, at] = cotangent[places[r]]
    source[...] = product(out_rows[...], mixed[...], TN)
    step = 32
    pieces = [slice(place, place + step) for place in range(0, width, step)]

    total = jnp.zeros((8, tokens), F32)
    for own in pieces:
        entered = jnp.concatenate([hidden[places[r], own, :] for r in range(rows)], axis=1)
        middle = source[own, :] + entered.astype(F32) + columns[own, 2:3]
        source[own, :] = middle
        total = total + row_sum(middle)
    mean = jnp.sum(total, axis=0, keepdims=True) * (1.0 / width)
    total = jnp.zeros((8, tokens), F32)
    for own in pieces:
        centre = source[own, :] - mean
        total = total + row_sum(centre * centre)
    inverse = lax.rsqrt(jnp.sum(total, axis=0, keepdims=True) * (1.0 / width) + EPS)
    for own in pieces:
        middle = source[own, :]
        unit = (middle - mean) * inverse
        low_rows[own, :] = (unit * columns[own, 3:4] + columns[own, 4:5]).astype(BF16)
        down_total[own, :] = middle + columns[own, 5:6]
        source[own, :] = unit
    back_total[...] = jnp.zeros_like(back_total)
    if not last:
        for copy in copies:
            copy.wait()

    pair = 2 * BLOCK

    def enter(i, slot):
        at = at_block(i, pair)
        upward[slot] = product(weights[0, :, at], low_rows[...], TN)
        upstream[slot] = product(weights[1, :, at], given[...], TN)

    lane = lax.broadcasted_iota(jnp.int32, (step, 128), 1)

    def bend(i, slot):
        for place in range(0, pair, step):
            own = slice(place, place + step)
            j = 2 * i + place // BLOCK
            inside = slice(place % BLOCK, place % BLOCK + step)
            bias = jnp.sum(
                jnp.where(lane == j, up_bias[inside, :], 0.0), axis=1, keepdims=True
            )
            values = upward[slot, own, :] + bias
            share, density = gelu_parts(values)
            active[slot, own, :] = (values * share).astype(BF16)
            grad_up = upstream[slot, own, :] * (share + values * density)
            grad_low[slot, own, :] = grad_up.astype(BF16)
            bias_sum = lane_groups(grad_up)
            if last:
                bias_total[j, inside, :] = bias_sum + bias_carried[j, inside, :]
            else:
                bias_carried[j, inside, :] = bias_sum

    def leave(i, slot):
        at = at_block(i, pair)
        down_total[...] += product(weights[1, :, at], active[slot])
        back_total[...] += product(weights[0, :, at], grad_low[slot])
        up_grad = product(low_rows[...], grad_low[slot], NT)
        down_grad = product(given[...], active[slot], NT)
        if not last:
            carried[0, :, at] = up_grad
            carried[1, :, at] = down_grad
            return
        up_grad = up_grad + carried[0, :, at]
        down_grad = down_grad + carried[1, :, at]
        kept = jnp.where(core == 0, up_grad, down_grad).astype(BF16)
        sent = jnp.where(core == 0, down_grad, up_grad).astype(BF16)
        for odd in range(2):
            kept_out[odd, i] = kept[:, odd * BLOCK : (odd + 1) * BLOCK]
            sent_out[odd, i] = sent[:, odd * BLOCK : (odd + 1) * BLOCK]

    def two_pairs(n, carry):
        i = 2 * n
        enter(i + 1, 1)
        bend(i, 0)
        leave(i, 0)
        enter(lax.rem(i + 2, blocks // 2), 0)
        bend(i + 1, 1)
        leave(i + 1, 1)
        return carry

    enter(0, 0)
    lax.fori_loop(0, blocks // 4, two_pairs, 0)
    if last:
        for r in range(first_row):
            hidden_out[row_of(lengths, r, hidden.shape[0])] = hidden_before[r]
    for r in range(rows):
        place = places[r] if last else r
        hidden_out[place] = down_total[:, r * chunk : (r + 1) * chunk].astype(BF16)
    scaled_total = jnp.zeros((8, tokens), F32)
    unit_total = jnp.zeros((8, tokens), F32)
    for own in pieces:
        scaled = back_total[own, :] * columns[own, 3:4]
        scaled_total = scaled_total + row_sum(scaled)
        unit_total = unit_total + row_sum(scaled * source[own, :])
    scaled_mean = jnp.sum(scaled_total, axis=0, keepdims=True) * (1.0 / width)
    unit_mean = jnp.sum(unit_total, axis=0, keepdims=True) * (1.0 / width)
    for own in pieces:
        back, unit = back_total[own, :], source[own, :]
        given_wide = given[own, :].astype(F32)
        scaled = back * columns[own, 3:4]
        grad_middle = given_wide + inverse * (scaled - scaled_mean - unit * unit_mean)
        for r in range(rows):
            grad_middle_out[r, own, :] = grad_middle[:, r * chunk : (r + 1) * chunk]
        low_rows[own, :] = grad_middle.astype(BF16)
        for place, part in enumerate((back * unit, back, grad_middle, given_wide)):
            part = lane_groups(part)
            if last:
                sums_total[place, own, :] = part + sums_carried[place, own, :]
            else:
                sums_carried[place, own, :] = part
    mixed_grad = product(out_rows[...], low_rows[...]).astype(BF16)
    for r in range(rows):
        at = slice(r * chunk, (r + 1) * chunk)
        grad_own[r] = mixed_grad[:held, at]
        grad_near[r] = mixed_grad[held : 2 * held, at]
        grad_cross[r, 0] = mixed_grad[2 * held : 3 * held, at]
        grad_cross[r, 1] = mixed_grad[3 * held :, at]
    out_part = product(mixed[...], low_rows[...], NT)
    if not last:
        out_carried[...] = out_part
        return
    out_part = (out_part + out_carried[...]).astype(BF16)
    shared[...] = jnp.zeros_like(shared)
    for place in range(4):
        line = row_sum(sums_total[place].T)
        shared[place : place + 1, :width] = jnp.sum(line, axis=0, keepdims=True)
    for j in range(blocks):
        line = row_sum(bias_total[j].T)
        shared[pl.ds(4 + (index ^ j), 1), :BLOCK] = jnp.sum(line, axis=0, keepdims=True)
    shared_low = shared[...].astype(BF16)
    for k, target in enumerate((out_own, out_near.at[0], out_cross, out_near.at[1])):
        target[:held, 384:] = jnp.zeros((held, LANES - 384), BF16)
        target[:held, :width] = out_part[k * held : (k + 1) * held]
        target[held:, :] = shared_low


def norm_back_kernel(rows, lengths, hidden, columns, *refs):
    middle_grads, refs = refs[:2], refs[2:]
    own_parts, near_parts = refs[0 : 2 * rows : 2], refs[1 : 2 * rows : 2]
    crossed, (out,) = refs[2 * rows : 2 * rows + rows // 2], refs[2 * rows + rows // 2 :]
    cross_parts = [part.at[place] for part in crossed for place in range(2)]
    gain = columns[:, 0:1]
    for row in range(rows):
        place = row_of(lengths, row, rows)
        unit, inverse = norm_columns(hidden[place].astype(F32))
        grad = (
            own_parts[row][...].astype(F32)
            + near_parts[row][0].astype(F32)
            + cross_parts[row][...].astype(F32)
        )
        half = rows // 2
        result = middle_grads[row // half][row % half] + norm_columns_back(
            grad, unit, inverse, gain
        )
        out[place] = result.astype(BF16)


def add_pieces_kernel(even, beside, *outs):
    for i, out in enumerate(outs):
        out[...] = (even[i].astype(F32) + beside[i].astype(F32)).astype(BF16)


def own_piece_kernel(first, second, fourth, sixth, norm_sums, out):
    size = first.shape[0]
    total = first[...].astype(F32) + second[...].astype(F32)
    total = total + fourth[...].astype(F32) + sixth[...].astype(F32)
    out[:size, :] = total.astype(BF16)
    width = norm_sums.shape[1]
    values = norm_sums[...]
    high = values.astype(BF16)
    rest = (values - high.astype(F32)).astype(BF16)
    out[size:, 384:] = jnp.zeros((16, LANES - 384), BF16)
    out[size:, :width] = jnp.concatenate([high.astype(F32), rest.astype(F32)]).astype(BF16)


def feed_sum_kernel(info, first, second, fourth, sixth, keep, send, rows):
    total = first[...].astype(F32) + second[...].astype(F32)
    rows[...] = total + fourth[...].astype(F32) + sixth[...].astype(F32)
    size = keep.shape[0]
    chip = info[0] >> 1
    keep[...] = rows[at_block(chip, size), :].astype(BF16)
    send[...] = rows[at_block(1 - chip, size), :].astype(BF16)


def feed_pair_kernel(info, kept, came, mine, other, rows):
    rows[...] = kept[...].astype(F32) + came[...].astype(F32)
    size = mine.shape[0]
    core = info[0] & 1
    mine[...] = rows[at_block(core, size), :].astype(BF16)
    other[...] = rows[at_block(1 - core, size), :].astype(BF16)


def unpack_kernel(info, *refs):
    evens, beside = refs[:4], refs[4]
    refs = refs[5:]
    if len(refs) > 12:
        mine, came, refs = refs[0], refs[1], refs[2:]
        up_grad, down_grad = refs[10:12]
        refs = refs[:10] + refs[12:]
        count = up_grad.shape[1]

        def write(up, down):
            up_grad[...] = up[:, :count].astype(F32)
            down_grad[...] = down[...].astype(F32).T[:count, :]

        pl.when(info[0] & 1 == 0)(lambda: write(mine, came))
        pl.when(info[0] & 1 == 1)(lambda: write(came, mine))
    weight_grad, bias_grad, out_grad, gain, shift, out_bias, down_bias, up_bias = refs[:8]
    norm_gain, norm_shift, whole, line = refs[8:]
    size = whole.shape[0] // 8
    width = weight_grad.shape[1]
    norms = [evens[0][size:, :].astype(F32) + beside[0, size:, :].astype(F32)]
    for i in range(4):
        whole[at_block(info[1] ^ (2 * i), size), :] = evens[i][:size, :].astype(F32)
        whole[at_block(info[1] ^ (2 * i + 1), size), :] = beside[i, :size, :].astype(F32)
        if i > 0:
            norms.append(evens[i][size:, :].astype(F32) + beside[i, size:, :].astype(F32))
    norms = (norms[0] + norms[1]) + (norms[2] + norms[3])
    norms = norms[:8] + norms[8:16]
    norm_gain[...] = norms[0:1, :width]
    norm_shift[...] = norms[1:2, :width]
    columns = weight_grad.shape[2]
    for c in range(3):
        turned = whole[c * columns : (c + 1) * columns, :].T
        weight_grad[c] = turned[:width, :]
        bias_grad[c : c + 1, :] = turned[width : width + 1, :]
    out_grad[...] = whole[3 * columns : 4 * columns, :width]
    for place, target in enumerate((gain, shift, out_bias, down_bias)):
        target[...] = whole[4 * columns + place : 4 * columns + place + 1, :width]
    block = up_bias.shape[0] // 8
    for j in range(8):
        line[:, j * block : (j + 1) * block] = whole[
            4 * columns + 4 + j : 4 * columns + 5 + j, :block
        ]
    up_bias[...] = line[0, :]


def swap(values, axis, bit):
    size = lax.axis_size(axis)
    return lax.ppermute(values, axis, [(i, i ^ bit) for i in range(size)])


def gather_four(own, *others):
    beside = swap(own, "tensor", 1)
    across = swap(own, "tensor", 2)
    return [own, beside, across, swap(after(across, *others), "tensor", 1)]


def spread_four(own, near, cross, beside, *others):
    across = swap(cross, "tensor", 2)
    return [own, beside, across, swap(after(across, *others), "tensor", 1)]


def add_low(*parts):
    total = parts[0].astype(F32)
    for part in parts[1:]:
        total = total + part.astype(F32)
    return total.astype(BF16)


def gather_feed_plain(up, down, core):
    pair = jnp.stack([up, down.T])
    pair = lax.all_gather(pair, "tensor", axis=1, tiled=True)
    pair = lax.all_gather(pair, "dp", axis=2, tiled=True)
    pair = pair.reshape(2, pair.shape[1], 8, -1).transpose(0, 2, 1, 3)
    pair = jnp.pad(pair, ((0, 0), (0, 0), (0, 0), (0, BLOCK - pair.shape[3])))
    pair = jnp.where(core == 0, pair, pair[::-1])
    feeds = []
    for half in (pair[0], pair[1]):
        feeds += [half[0], half[1], half[2], half[3], half[4::2], half[5::2]]
    return feeds


def scatter_feed_plain(kept, sent, core, hidden_count):
    grads = jnp.stack([kept, sent]).swapaxes(1, 2).reshape(2, 8, *kept.shape[2:])
    grads = jnp.where(core == 0, grads, grads[::-1]).astype(F32)
    grads = grads[:, :, :, : hidden_count * lax.axis_size("dp") // 8]
    grads = grads.transpose(0, 2, 1, 3).reshape(2, grads.shape[2], -1)
    grads = lax.psum_scatter(grads, "dp", scatter_dimension=2, tiled=True)
    grads = lax.psum_scatter(grads, "tensor", scatter_dimension=1, tiled=True)
    return grads[0], grads[1].T


def sum_pieces(even, beside, norm_sums):
    parts = call(
        add_pieces_kernel,
        (even, beside),
        [shape(even.shape[1:], BF16)] * 4,
        limit=4,
    )
    parts = [parts[0]] + [swap(parts[i], "dp", 2 * i) for i in (1, 2, 3)]
    norm_sums = norm_sums + swap(norm_sums, "tensor", 1)
    (own,) = call(
        own_piece_kernel,
        (*parts, norm_sums),
        [shape((even.shape[1] + 16, LANES), BF16)],
        limit=4,
    )
    back = [own] + [swap(own, "dp", e) for e in (2, 4, 6)]
    return back + [swap(jnp.stack(back), "dp", 1)], own


def sum_pieces_plain(even, odd, norm_sums):
    even, odd = (lax.psum(part.astype(F32), "dp").astype(BF16) for part in (even, odd))
    norm_sums = lax.psum(norm_sums, ("dp", "tensor"))
    high = norm_sums.astype(BF16)
    rest = (norm_sums - high.astype(F32)).astype(BF16)
    rows = jnp.concatenate([high, rest])
    rows = jnp.pad(rows, ((0, 0), (0, LANES - rows.shape[1])))
    even = jnp.concatenate([even, jnp.stack([rows] + [jnp.zeros_like(rows)] * 3)], axis=1)
    odd = jnp.concatenate([odd, jnp.zeros((4, *rows.shape), BF16)], axis=1)
    return [even[i] for i in range(4)] + [odd]


def shards(
    hidden_in,
    attn_gain,
    attn_shift,
    query_key_value_weight,
    query_key_value_bias,
    attention_output_weight,
    out_bias,
    ffn_gain,
    ffn_shift,
    up_projection_weight,
    up_projection_bias,
    down_projection_weight,
    down_bias,
    lengths,
    cotangent,
):
    chunks = lax.axis_size("tensor")
    ring = lax.axis_size("dp") == 8
    position = lax.axis_index("tensor")
    index = lax.axis_index("dp") if ring else jnp.int32(0)
    core = position & 1
    rows, chunk, width = hidden_in.shape
    full = chunk * chunks
    columns = query_key_value_weight.shape[2]
    heads = columns // HEAD_DIM
    hidden_count = up_projection_weight.shape[1]
    blocks = 8
    half = rows // 2

    info = jnp.stack([position, index]).astype(jnp.int32)
    lengths = lengths.astype(jnp.int32)
    inner_table, outer_table = (jnp.asarray(table) for table in rotary_constants(chunk, chunks))
    hidden = hidden_in.transpose(0, 2, 1)
    given = cotangent.transpose(0, 2, 1)

    if ring:
        inputs = (info, up_projection_weight, down_projection_weight)
        (pair,) = call(
            pair_kernel,
            inputs,
            [shape((columns, 2 * BLOCK), BF16)],
            scratch=[pltpu.VMEM(part.shape, part.dtype) for part in inputs[1:]]
            + [pltpu.SemaphoreType.DMA((2,))],
            in_specs=[smem()] + hbm(2),
            limit=4,
            tiles=20,
        )
        pair_across = swap(pair, "tensor", 2)
    inputs = (
        lengths,
        after(hidden, pair) if ring else hidden,
        attn_gain[None],
        attn_shift[None],
        attention_output_weight,
    )
    first, second = call(
        norm_kernel,
        inputs,
        [
            shape((half * width, chunk), BF16),
            shape((half * width + 2 * columns, chunk), BF16),
        ],
        scratch=[pltpu.VMEM(part.shape, part.dtype) for part in inputs[1:]]
        + [pltpu.VMEM((128, width), F32), pltpu.SemaphoreType.DMA((8,))],
        in_specs=[smem()] + hbm(4),
        limit=8,
        tiles=80,
    )
    inputs = (
        info,
        attn_gain[None],
        attn_shift[None],
        out_bias[None],
        ffn_gain[None],
        ffn_shift[None],
        down_bias[None],
        up_projection_bias[None],
        query_key_value_weight,
        query_key_value_bias,
    )
    weight, weight_turned, vectors, bias, up_bias, vector_rows = call(
        lambda *refs: prepare_kernel(heads, *refs),
        inputs,
        [
            shape((3 * columns, width), BF16),
            shape((width, 3 * columns), BF16),
            shape((width, 128), F32),
            shape((3 * columns, 128), F32),
            shape((BLOCK, 128), F32),
            shape((8, width), F32),
        ],
        scratch=[
            pltpu.VMEM((3 * columns, width), F32),
            pltpu.VMEM((128, BLOCK), F32),
        ]
        + [pltpu.VMEM(part.shape, part.dtype) for part in inputs[1:]]
        + [pltpu.SemaphoreType.DMA((9,))],
        in_specs=[smem()] + hbm(len(inputs) - 1),
        limit=8,
        tiles=60,
    )
    if ring:
        parts = [
            pair,
            swap(pair, "tensor", 1),
            pair_across,
            swap(after(pair_across, first), "tensor", 1),
        ]
        (own_feed,) = call(
            lambda *refs: assemble_kernel(chunks, *refs),
            (info, *parts),
            [shape((width, BLOCK), BF16)],
            scratch=[pltpu.VMEM((width, BLOCK), F32)],
            in_specs=[smem()] + vmem(chunks),
            limit=6,
            tiles=20,
        )
        came = [swap(own_feed, "dp", e) for e in (2, 4, 6)]
        beside = swap(own_feed, "dp", 1)
        second_beside = swap(came[0], "dp", 1)
        gathered = [
            gather_four(after(first, pair_across), own_feed, came[0], beside, weight)
        ]
    else:
        gathered = [gather_four(first)]

    kept = []
    mixed = []
    for g in range(2):
        if g == 1 and ring:
            gathered[1][0] = after(gathered[1][0], duo, beside, second_beside, mixed[0][3])
        inputs = (info, lengths, *gathered[g], weight, bias, inner_table, outer_table)
        outs = call(
            lambda *refs, g=g: attend_kernel(heads, chunks, chunk, g * half, half, *refs),
            inputs,
            [
                shape((half, 128, chunk), BF16),
                shape((half, 128, chunk), BF16),
                shape((half, 2, 128, chunk), BF16),
            ]
            + [shape((half, heads, HEAD_ROWS, full), BF16)] * 3
            + [
                shape((half, 8, full), F32),
                shape((half, 128, full), F32),
                shape((half, width, full), BF16),
            ],
            scratch=[
                pltpu.VMEM((heads, full, HEAD_ROWS), BF16),
                pltpu.VMEM((8, full), F32),
                pltpu.VMEM((3 * columns, full), F32),
                pltpu.VMEM((half, width, full), BF16),
                pltpu.SemaphoreType.DMA((half,)),
            ],
            in_specs=[smem(), smem()] + vmem(len(inputs) - 2),
            out_specs=vmem(8) + hbm(),
            limit=14,
            tiles=400,
        )
        kept.append(outs[3:])
        mixed.append(list(outs[:3]) + [swap(outs[1], "tensor", 1)])
        if g == 0:
            gathered.append(gather_four(after(second, gathered[0][2]), outs[0]))
            if ring:
                duo = jnp.stack([after(part, mixed[0][3], second_beside) for part in came[1:]])
                duo_beside = swap(duo, "dp", 1)
            else:
                feeds = gather_feed_plain(up_projection_weight, down_projection_weight, core)

    if ring:
        duo_beside = after(duo_beside, kept[1][0])
        feeds = [own_feed, beside, came[0], second_beside, duo, duo_beside]
        feeds += [swap(part, "tensor", 1) for part in feeds]
    feed_outs = []
    for g in range(2):
        last = g == 1
        others = (kept[1][0],) if g == 0 else (feed_outs[0][2],)
        ready = (mixed[1][3],) if g == 0 else (mixed_near,)
        inputs = (
            info,
            lengths,
            hidden,
            after(given, *ready),
            vectors,
            up_bias,
            *spread_four(*mixed[g], *others),
            *gathered[1],
        )
        if last:
            inputs = inputs + tuple(feed_outs[0][5:]) + (feed_outs[0][0],)
        else:
            inputs = inputs + tuple(feeds)
        carried = [
            shape((2, width, blocks * BLOCK), BF16),
            shape((2, width, blocks * BLOCK), F32),
            shape((chunks * 128, width), F32),
            shape((4, width, 128), F32),
            shape((blocks, BLOCK, 128), F32),
        ]
        sent = [
            shape((2, blocks // 2, width, BLOCK), BF16),
            shape((2, blocks // 2, width, BLOCK), BF16),
            shape((144, LANES), BF16),
            shape((2, 144, LANES), BF16),
            shape((144, LANES), BF16),
        ]
        tokens = half * chunk
        outs = call(
            lambda *refs, g=g, last=last: feed_kernel(
                chunks, blocks, g * half, half, last, *refs
            ),
            inputs,
            [
                shape((rows if last else half, width, chunk), BF16),
                shape((half, width, chunk), F32),
                shape((half, 128, chunk), BF16),
                shape((half, 128, chunk), BF16),
                shape((half, 2, 128, chunk), BF16),
            ]
            + (sent if last else carried),
            scratch=[
                pltpu.VMEM((chunks * 128, width), BF16),
                pltpu.VMEM((chunks * 128, tokens), BF16),
                pltpu.VMEM((width, tokens), F32),
                pltpu.VMEM((width, tokens), BF16),
                pltpu.VMEM((width, tokens), BF16),
                pltpu.VMEM((width, tokens), F32),
                pltpu.VMEM((width, tokens), F32),
                pltpu.VMEM((2, 2 * BLOCK, tokens), F32),
                pltpu.VMEM((2, 2 * BLOCK, tokens), F32),
                pltpu.VMEM((2, 2 * BLOCK, tokens), BF16),
                pltpu.VMEM((2, 2 * BLOCK, tokens), BF16),
                pltpu.VMEM((4, width, 128), F32),
                pltpu.VMEM((blocks, BLOCK, 128), F32),
                pltpu.VMEM((16, LANES), F32),
                pltpu.SemaphoreType.DMA((2, blocks)),
            ],
            in_specs=[smem(), smem()]
            + (
                vmem(len(inputs) - 2)
                if last
                else vmem(len(inputs) - 2 - len(feeds)) + [pl.BlockSpec(memory_space=pl.ANY)] * len(feeds)
            ),
            limit=22,
            tiles=500,
        )
        feed_outs.append(outs)
        if g == 0:
            mixed_near = swap(outs[3], "tensor", 1)
    hidden_out = feed_outs[1][0]
    middle_grads = [outs[1] for outs in feed_outs]
    feed_kept, feed_sent, out_own, out_near, out_cross = feed_outs[1][5:]

    mixed_grads = [spread_four(*feed_outs[0][2:5], mixed_near, feed_outs[1][2])]
    feed_sent, out_near = after((feed_sent, out_near), mixed_grads[0][3])
    out_came = swap(out_near, "tensor", 1)
    feed_came = swap(feed_sent, "tensor", 1)
    running = None
    reduced = []
    crossing = []
    for r in range(rows):
        last = r == rows - 1
        g = r // half
        inputs = (
            info,
            lengths,
            *mixed_grads[g],
            *kept[g],
            weight_turned,
            inner_table,
            outer_table,
        )
        if last and ring:
            running = after(running, *evens)
        if r > 0:
            inputs = inputs + (running,)
        if last:
            inputs = inputs + (out_own, out_came, out_across, weight, vector_rows)
        outs = call(
            lambda *refs, r=r, last=last: attend_back_kernel(
                heads, chunks, chunk, r, r % half, r == 0, last, *refs
            ),
            inputs,
            [
                shape((width, chunk), BF16),
                shape((2, width, chunk), BF16),
                shape((width, chunk), BF16),
            ]
            + (
                [shape((4, 64, LANES), BF16)] * 2 + [shape((8, width), F32)]
                if last
                else [shape((3 * columns, LANES + 128), F32)]
            ),
            scratch=[
                pltpu.VMEM((128, full), BF16),
                pltpu.VMEM((heads, HEAD_ROWS, full), BF16),
                pltpu.VMEM((heads, HEAD_ROWS, full), BF16),
                pltpu.VMEM((heads, full, HEAD_ROWS), BF16),
                pltpu.VMEM((heads, full, HEAD_ROWS), BF16),
                pltpu.VMEM((3, columns, full), F32),
                pltpu.VMEM((3 * columns, full), BF16),
                pltpu.VMEM((512, LANES), F32),
                pltpu.VMEM((width, full), BF16),
                pltpu.SemaphoreType.DMA(()),
            ],
            in_specs=[smem(), smem()] + vmem(9) + hbm() + vmem(len(inputs) - 12),
            limit=12,
            tiles=420,
        )
        if last:
            outs = list(outs)
            even, odd, norm_sums = outs[3:]
            if ring:
                odd = after(odd, reduced[5], *feed_came)
                beside_pieces = swap(odd, "dp", 1)
                norm_sums = norm_sums + swap(norm_sums, "tensor", 2)
                outs[1] = after(outs[1], beside_pieces, norm_sums)
        near = swap(outs[1], "tensor", 1)
        reduced += [outs[0], near, None]
        crossing.append((outs[2], near))
        if r >= 2:
            pair_sum = jnp.stack(
                [
                    add_low(after(cross, outs[0], out_across), near[1])
                    for cross, near in crossing[2 * r - 4 : 2 * r - 2]
                ]
            )
            reduced[3 * (2 * r - 3) + 2] = swap(pair_sum, "tensor", 2)
        if not last:
            running = outs[3]
        if r == 1:
            mixed_near = swap(feed_outs[1][3], "tensor", 1)
            mixed_grads.append(spread_four(*feed_outs[1][2:5], mixed_near, outs[0]))
        if r == 0:
            out_across = swap(
                add_low(after(out_cross, outs[0]), out_came[1]), "tensor", 2
            )
            if ring:
                feed_odd = add_low(after(feed_kept[1], outs[0]), feed_came[1])
                running = after(running, feed_odd)
                feed_odd = swap(feed_odd, "dp", 1)
        if r == 2 and ring:
            feed_kept = after(feed_kept, outs[0])
            evens = [
                add_low(feed_kept[0, i], feed_came[0, i], feed_odd[i]) for i in range(4)
            ]
            feed_came = [swap(evens[i], "dp", 2 * i) for i in (1, 2, 3)]
    own_parts = [part for place, part in enumerate(reduced) if place % 3 < 2]
    cross_parts = [part for part in reduced[2::3] if part is not None]
    inputs = (lengths, hidden, vectors, *middle_grads, *own_parts, *cross_parts)
    (grad_hidden,) = call(
        lambda *refs: norm_back_kernel(rows, *refs),
        inputs,
        [shape((rows, width, chunk), BF16)],
        in_specs=[smem()] + vmem(len(inputs) - 1),
        limit=12,
        tiles=120,
    )
    if ring:
        parts, own = sum_pieces(even, beside_pieces, norm_sums)
    else:
        parts = sum_pieces_plain(even, odd, norm_sums)
    if ring:
        keep, send = call(
            feed_sum_kernel,
            (info, after(evens[0], own), *feed_came),
            [shape((width // 2, BLOCK), BF16)] * 2,
            scratch=[pltpu.VMEM((width, BLOCK), F32)],
            in_specs=[smem()] + vmem(4),
            limit=4,
            tiles=20,
        )
        mine, other = call(
            feed_pair_kernel,
            (info, keep, after(swap(send, "tensor", 2), grad_hidden)),
            [shape((columns, BLOCK), BF16)] * 2,
            scratch=[pltpu.VMEM((width // 2, BLOCK), F32)],
            in_specs=[smem()] + vmem(2),
            limit=4,
            tiles=20,
        )
        feed_parts = (mine, swap(other, "tensor", 1))
    else:
        grad_up_weight, grad_down_weight = scatter_feed_plain(
            feed_kept, feed_sent, core, hidden_count
        )

    inputs = (info, *parts) + (feed_parts if ring else ())
    outs = [
        shape((3, width, columns), F32),
        shape((3, columns), F32),
        shape((columns, width), F32),
    ]
    outs += [shape((1, width), F32)] * 4
    outs += [shape(up_projection_bias.shape, F32)]
    outs += [shape((1, width), F32)] * 2
    if ring:
        outs += [shape((columns, hidden_count), F32), shape((hidden_count, columns), F32)]
    outs = call(
        unpack_kernel,
        inputs,
        outs,
        scratch=[
            pltpu.VMEM((512, LANES), F32),
            pltpu.VMEM((1, up_projection_bias.shape[0]), F32),
        ],
        in_specs=[smem()] + vmem(len(inputs) - 1),
        limit=8,
        tiles=60,
    )
    grad_qkv_weight, grad_qkv_bias, grad_out_weight = outs[:3]
    grad_ffn_gain, grad_ffn_shift, grad_out_bias, grad_down_bias, grad_up_bias = outs[3:8]
    grad_attn_gain, grad_attn_shift = outs[8:10]
    if ring:
        grad_up_weight, grad_down_weight = outs[10:]
    return (
        hidden_out.transpose(0, 2, 1),
        grad_hidden.transpose(0, 2, 1),
        grad_attn_gain[0],
        grad_attn_shift[0],
        grad_qkv_weight,
        grad_qkv_bias,
        grad_out_weight,
        grad_out_bias[0],
        grad_ffn_gain[0],
        grad_ffn_shift[0],
        grad_up_weight,
        grad_up_bias,
        grad_down_weight,
        grad_down_bias[0],
    )


def solution(mesh):
    return jax.shard_map(
        shards,
        mesh=mesh,
        in_specs=(
            P("dp", "tensor", None),
            P(),
            P(),
            P(None, None, "tensor"),
            P(None, "tensor"),
            P("tensor", None),
            P(),
            P(),
            P(),
            P("tensor", "dp"),
            P(),
            P("dp", "tensor"),
            P(),
            P("dp"),
            P("dp", "tensor", None),
        ),
        out_specs=(
            P("dp", "tensor", None),
            P("dp", "tensor", None),
            P(),
            P(),
            P(None, None, "tensor"),
            P(None, "tensor"),
            P("tensor", None),
            P(),
            P(),
            P(),
            P("tensor", "dp"),
            P(),
            P("dp", "tensor"),
            P(),
        ),
        check_vma=False,
    )
```

```python
import math

import jax
import jax.numpy as jnp
import numpy as np
from jax import lax
from jax.experimental import pallas as pl
from jax.experimental.pallas import tpu as pltpu
from jax.sharding import PartitionSpec as P

HEAD_DIM = 24
HEAD_ROWS = 32
EPS = 1e-05
MASK_FILL = -1000000000.0
LOG2E = math.log2(math.e)
SAFE_SCORE = 58.0
WORK_SCALE = 0.01
BLOCK = 256
KEY_STEP = 256
LANES = 512
BF16 = jnp.bfloat16
F32 = jnp.float32

NN = (((1,), (0,)), ((), ()))
NT = (((1,), (1,)), ((), ()))
TN = (((0,), (0,)), ((), ()))


def product(left, right, dims=NN):
    return lax.dot_general(left, right, dims, preferred_element_type=F32)


def vmem(count):
    return [pl.BlockSpec(memory_space=pltpu.VMEM)] * count


def smem():
    return pl.BlockSpec(memory_space=pltpu.SMEM)


def hbm(count=1):
    return [pl.BlockSpec(memory_space=pltpu.HBM)] * count


def call(kernel, inputs, outs, scratch=(), in_specs=None, out_specs=None, limit=40, tiles=0):
    flops = int(2 * 256**3 * tiles * WORK_SCALE)
    in_specs = vmem(len(inputs)) if in_specs is None else in_specs
    inputs = [
        pltpu.with_memory_space_constraint(part, pltpu.HBM)
        if spec.memory_space is pltpu.HBM
        else part
        for part, spec in zip(inputs, in_specs)
    ]
    out_specs = vmem(len(outs)) if out_specs is None else out_specs
    outs = [
        pltpu.HBM(part.shape, part.dtype) if spec.memory_space is pltpu.HBM else part
        for part, spec in zip(outs, out_specs)
    ]
    return pl.pallas_call(
        kernel,
        out_shape=outs,
        in_specs=in_specs,
        out_specs=out_specs,
        scratch_shapes=list(scratch),
        compiler_params=pltpu.CompilerParams(vmem_limit_bytes=limit << 20),
        cost_estimate=pl.CostEstimate(flops=flops, transcendentals=0, bytes_accessed=0),
    )(*inputs)


def shape(dims, dtype):
    return jax.ShapeDtypeStruct(dims, dtype)


def at_block(index, size):
    return pl.ds(pl.multiple_of(index * size, size), size)


def split_three(values):
    high = values.astype(BF16).astype(F32)
    rest = values - high
    middle = rest.astype(BF16).astype(F32)
    return high, middle, rest - middle


def row_of(lengths, slot, rows):
    slot = jnp.where(slot == 0, 0, jnp.where(slot == 1, rows - 1, slot - 1))
    chosen = jnp.int32(0)
    for i in range(rows):
        rank = jnp.int32(0)
        for j in range(rows):
            if j < i:
                rank += jnp.where(lengths[j] <= lengths[i], 1, 0)
            elif j > i:
                rank += jnp.where(lengths[j] < lengths[i], 1, 0)
        chosen += jnp.where(rank == slot, i, 0)
    return chosen


def after(values, *others):
    return lax.optimization_barrier((values, *others))[0]


def norm_columns(values):
    centre = values - jnp.mean(values, axis=0, keepdims=True)
    inverse = lax.rsqrt(jnp.mean(centre * centre, axis=0, keepdims=True) + EPS)
    return centre * inverse, inverse


def norm_columns_back(upstream, unit, inverse, gain):
    scaled = upstream * gain
    centred = scaled - jnp.mean(scaled, axis=0, keepdims=True)
    return inverse * (centred - unit * jnp.mean(scaled * unit, axis=0, keepdims=True))


def pair_kernel(info, up, down, pair, up_inside, down_inside, semaphores):
    copies = [
        pltpu.make_async_copy(up, up_inside, semaphores.at[0]),
        pltpu.make_async_copy(down, down_inside, semaphores.at[1]),
    ]
    for copy in copies:
        copy.start()
    pair[...] = jnp.zeros_like(pair)
    for copy in copies:
        copy.wait()
    size = up.shape[1]
    up_half = up_inside[...]
    down_half = down_inside[...].astype(F32).T.astype(BF16)

    @pl.when(info[0] & 1 == 0)
    def _():
        pair[:, :size] = up_half
        pair[:, BLOCK : BLOCK + size] = down_half

    @pl.when(info[0] & 1 == 1)
    def _():
        pair[:, :size] = down_half
        pair[:, BLOCK : BLOCK + size] = up_half


def norm_kernel(
    lengths,
    hidden_in,
    gain,
    shift,
    out_weight_in,
    first_out,
    second_out,
    hidden,
    gain_inside,
    shift_inside,
    out_weight,
    rows_scratch,
    semaphores,
):
    rows, width, chunk = hidden.shape
    copies = [
        pltpu.make_async_copy(
            hidden_in.at[row_of(lengths, slot, rows)], hidden.at[slot], semaphores.at[slot]
        )
        for slot in range(rows)
    ]
    others = [
        pltpu.make_async_copy(gain, gain_inside, semaphores.at[4]),
        pltpu.make_async_copy(shift, shift_inside, semaphores.at[5]),
        pltpu.make_async_copy(out_weight_in, out_weight, semaphores.at[6]),
    ]
    for copy in others[:2] + copies + others[2:]:
        copy.start()
    rows_scratch[...] = jnp.zeros_like(rows_scratch)
    others[0].wait()
    others[1].wait()
    rows_scratch[0:1, :] = gain_inside[...]
    rows_scratch[1:2, :] = shift_inside[...]
    columns = rows_scratch[...].T
    half = rows // 2
    for row in range(rows):
        copies[row].wait()
        unit, _ = norm_columns(hidden[row].astype(F32))
        target = first_out if row < half else second_out
        place = row % half * width
        target[place : place + width, :] = (unit * columns[:, 0:1] + columns[:, 1:2]).astype(
            BF16
        )
    others[2].wait()
    own = out_weight.shape[0]
    second_out[half * width : half * width + own, :] = out_weight[:, :chunk]
    rest = width - chunk
    second_out[half * width + own : half * width + 2 * own, :] = jnp.zeros((own, chunk), BF16)
    second_out[half * width + own : half * width + 2 * own, :rest] = out_weight[:, chunk:]


def prepare_kernel(heads, info, *refs):
    outside, refs = refs[:9], refs[9:]
    weight_out, weight_turned_out, columns_out, bias_out, up_bias_out, vector_rows = refs[:6]
    weight_scratch, bias_rows = refs[6:8]
    inside, semaphores = refs[8:17], refs[17]
    copies = [
        pltpu.make_async_copy(source, target, semaphores.at[place])
        for place, (source, target) in enumerate(zip(outside, inside))
    ]
    for copy in copies:
        copy.start()
    vectors, (up_bias, weight, bias) = inside[:6], inside[6:]
    width = weight.shape[1]
    vector_rows[...] = jnp.zeros_like(vector_rows)
    for copy in copies:
        copy.wait()
    for place, vector in enumerate(vectors):
        vector_rows[place : place + 1, :] = vector[...]
    columns_out[...] = jnp.concatenate([vector_rows[...], jnp.zeros((120, width), F32)]).T
    span = heads * HEAD_DIM
    for c in range(3):
        own = slice(c * span, (c + 1) * span)
        weight_scratch[own, :] = weight[c].astype(F32).T
        bias_out[own, :] = jnp.broadcast_to(bias[c : c + 1, :], (128, span)).T
    weight_out[...] = weight_scratch[...].astype(BF16)
    weight_turned_out[...] = weight_scratch[...].T.astype(BF16)
    bias_rows[...] = jnp.zeros_like(bias_rows)
    count = up_bias.shape[1]
    block = count // 8
    spread = jnp.broadcast_to(up_bias[...], (8, count))
    for j in range(8):
        moved = pltpu.roll(spread, lax.rem(count - (info[1] ^ j) * block, count), 1)
        bias_rows[j : j + 1, :block] = moved[0:1, :block]
    up_bias_out[...] = bias_rows[...].T


def assemble_kernel(chunks, info, *refs):
    parts, (out, rows) = refs[:chunks], refs[chunks:]
    size = parts[0].shape[0]
    for k in range(chunks):
        half = parts[k][:, (k & 1) * BLOCK : ((k & 1) + 1) * BLOCK]
        rows[at_block(info[0] ^ k, size), :] = half.astype(F32)
    out[...] = rows[...].astype(BF16)


def rotary_constants(chunk, chunks):
    half = HEAD_DIM // 2
    element = np.arange(HEAD_DIM)
    frequency = (1.0 / 10000.0 ** (np.arange(0, HEAD_DIM, 2).astype(np.float32) / HEAD_DIM)).astype(
        np.float32
    )
    per_row = frequency[element % half].astype(np.float64)
    inner = per_row[:, None] * np.arange(chunk)[None, :]
    outer = per_row[:, None] * (np.arange(chunks) * chunk)[None, :]
    outer = np.repeat(outer[:, :, None], chunk, axis=2).transpose(1, 0, 2)
    inner_pair = np.stack([np.cos(inner), np.sin(inner)]).astype(np.float32)
    outer_pair = np.stack([np.cos(outer), np.sin(outer)]).astype(np.float32)
    return inner_pair, outer_pair


def chunk_tables(inner, outer, index):
    cos_in, sin_in = inner[0], inner[1]
    cos_out, sin_out = outer[0, index], outer[1, index]
    element = lax.broadcasted_iota(jnp.int32, cos_in.shape, 0)
    sine = sin_in * cos_out + cos_in * sin_out
    return cos_in * cos_out - sin_in * sin_out, jnp.where(
        element < HEAD_DIM // 2, -sine, sine
    )


def swap_halves(values):
    return pltpu.roll(values, HEAD_DIM // 2, 0)


def attend_kernel(heads, chunks, chunk, first_row, rows, info, lengths, *refs):
    parts = refs[:chunks]
    weight, bias, inner, outer, own_out, near_out, cross_out = refs[chunks : chunks + 7]
    queries, keys, values, logsum, mixed_turned, normed_out, key_rows, peak, flat = refs[
        chunks + 7 : chunks + 16
    ]
    normed, semaphores = refs[chunks + 16 :]
    position = info[0]
    width = normed.shape[1]
    full = chunk * chunks
    span = heads * HEAD_DIM
    scale = HEAD_DIM**-0.5

    def one_row(r, carry):
        length = lengths[row_of(lengths, first_row + r, lengths.shape[0])]
        for k in range(chunks):
            normed[r, :, at_block(position ^ k, chunk)] = parts[k][at_block(r, width), :]
        pltpu.make_async_copy(normed.at[r], normed_out.at[r], semaphores.at[r]).start()
        flat[...] = product(weight[...], normed[r])
        line = lax.broadcasted_iota(jnp.int32, (8, chunk), 0)
        ones = jnp.where(line < 3, 1.0, 0.0)
        query_line = jnp.where(line == 3, 1.0, 0.0)
        query_top = [jnp.zeros((1, chunk), F32) for _ in range(heads)]
        key_top = [jnp.zeros((1, chunk), F32) for _ in range(heads)]
        for j in range(chunks):
            at = slice(j * chunk, (j + 1) * chunk)
            cosine, sine = chunk_tables(inner, outer, j)
            query_cosine, query_sine = cosine * scale, sine * scale
            place = lax.broadcasted_iota(jnp.int32, (8, chunk), 1) + j * chunk
            key_line = jnp.where((line == 3) & (place >= length), MASK_FILL, ones)
            for h in range(heads):
                here = h * HEAD_DIM
                query, key, value = (
                    flat[c * span + here : c * span + here + HEAD_DIM, at]
                    + jnp.concatenate(
                        [bias[c * span + here : c * span + here + HEAD_DIM, :]] * (chunk // 128),
                        axis=1,
                    )
                    for c in range(3)
                )
                query = query * query_cosine + swap_halves(query) * query_sine
                key = key * cosine + swap_halves(key) * sine
                query_top[h] = jnp.maximum(
                    query_top[h], jnp.sum(query * query, axis=0, keepdims=True)
                )
                key_top[h] = jnp.maximum(key_top[h], jnp.sum(key * key, axis=0, keepdims=True))
                key_full = jnp.concatenate([key, key_line])
                queries[r, h, :, at] = jnp.concatenate([query, query_line]).astype(BF16)
                keys[r, h, :, at] = key_full.astype(BF16)
                values[r, h, :, at] = jnp.concatenate([value, ones]).astype(BF16)
                key_rows[h, at, :] = key_full.T.astype(BF16)
        bound = jnp.zeros((1, 1), F32)
        for h in range(heads):
            bound = jnp.maximum(
                bound,
                jnp.max(query_top[h], axis=-1, keepdims=True)
                * jnp.max(key_top[h], axis=-1, keepdims=True),
            )
        safe = jnp.max(bound) <= SAFE_SCORE * SAFE_SCORE
        peak[...] = jnp.zeros_like(peak)

        @pl.when(jnp.logical_not(safe))
        def _():
            def one_head(h, carry):
                scores = product(key_rows[h], queries[r, h])
                peak[pl.ds(h, 1), :] = (
                    jnp.max(scores, axis=0, keepdims=True).astype(BF16).astype(F32)
                )
                return carry

            lax.fori_loop(0, heads, one_head, 0)

        head_line = lax.broadcasted_iota(jnp.int32, (HEAD_ROWS, full), 0)

        def with_keys(count):
            def one_head(h, carry):
                top = peak[pl.ds(h, 1), :]
                query = jnp.where(
                    head_line == HEAD_DIM, -top, queries[r, h].astype(F32)
                ).astype(BF16)
                exponent = jnp.exp(product(key_rows[h, :count, :], query)).astype(BF16)
                blend = product(values[r, h, :, :count], exponent)
                total = blend[HEAD_DIM : HEAD_DIM + 1, :]
                logsum[r, pl.ds(h, 1), :] = top + jnp.log(total)
                mixed_turned[r, pl.ds(pl.multiple_of(h * HEAD_DIM, 8), HEAD_DIM), :] = blend[
                    :HEAD_DIM
                ] * (1.0 / total)
                return carry

            lax.fori_loop(0, heads, one_head, 0, unroll=True)

        blocks = jnp.maximum((length + KEY_STEP - 1) // KEY_STEP, 1)
        for b in range(1, full // KEY_STEP + 1):
            pl.when(blocks == b)(lambda b=b: with_keys(b * KEY_STEP))
        mixed_turned[r, span:, :] = jnp.zeros((mixed_turned.shape[1] - span, full), F32)
        own_out[r] = mixed_turned[r, :, at_block(position, chunk)].astype(BF16)
        near_out[r] = mixed_turned[r, :, at_block(position ^ 1, chunk)].astype(BF16)
        cross_out[r, 0] = mixed_turned[r, :, at_block(position ^ 2, chunk)].astype(BF16)
        cross_out[r, 1] = mixed_turned[r, :, at_block(position ^ 3, chunk)].astype(BF16)
        return carry

    lax.fori_loop(0, rows, one_row, 0)
    for r in range(rows):
        pltpu.make_async_copy(normed.at[r], normed_out.at[r], semaphores.at[r]).wait()


def attend_back_kernel(heads, chunks, chunk, row, local, first, last, info, lengths, *refs):
    upstream_own, upstream_near, upstream_cross, upstream_far = refs[:4]
    queries, keys, values, logsum, mixed_turned, normed_in, weight_turned, inner, outer = refs[
        4:13
    ]
    refs = refs[13:]
    if not first:
        carried = refs[0]
        refs = refs[1:]
    if last:
        out_own, out_near, out_cross, weight, vector_rows = refs[:5]
        refs = refs[5:]
    own_out, near_out, cross_out = refs[:3]
    refs = refs[3:]
    if last:
        even_pieces, odd_pieces, norm_sums = refs[:3]
        refs = refs[3:]
    else:
        running = refs[0]
        refs = refs[1:]
    (
        upstream,
        query_full,
        upstream_full,
        key_rows,
        value_rows,
        grads,
        grad_low,
        packed,
        normed,
        semaphore,
    ) = refs
    fetch = pltpu.make_async_copy(normed_in.at[local], normed, semaphore)
    fetch.start()
    position, index = info[0], info[1]
    length = lengths[row_of(lengths, row, lengths.shape[0])]
    full = chunk * chunks
    span = heads * HEAD_DIM
    upstream[:, at_block(position, chunk)] = upstream_own[local]
    upstream[:, at_block(position ^ 1, chunk)] = upstream_near[local]
    upstream[:, at_block(position ^ 2, chunk)] = upstream_cross[local, 0]
    upstream[:, at_block(position ^ 3, chunk)] = upstream_far[local, 1]
    zeros = jnp.zeros((5, chunk), F32)
    line = lax.broadcasted_iota(jnp.int32, (8, chunk), 0)
    for j in range(chunks):
        at = slice(j * chunk, (j + 1) * chunk)
        turned = upstream[:, at].astype(F32)
        blend = turned * mixed_turned[local, :, at]
        for h in range(heads):
            own = slice(h * HEAD_DIM, (h + 1) * HEAD_DIM)
            high, middle, rest = split_three(-jnp.sum(blend[own], axis=0, keepdims=True))
            extra = jnp.where(
                line == 0, high, jnp.where(line == 1, middle, jnp.where(line == 2, rest, 0.0))
            )
            upstream_full[h, :, at] = jnp.concatenate([turned[own], extra]).astype(BF16)
            high, middle, rest = split_three(-logsum[local, h : h + 1, at])
            extra = jnp.where(
                line == 0,
                high,
                jnp.where(
                    line == 1, middle, jnp.where(line == 2, rest, jnp.where(line == 3, 1.0, 0.0))
                ),
            )
            query = queries[local, h, :, at].astype(F32)[:HEAD_DIM]
            query_full[h, :, at] = jnp.concatenate([query, extra]).astype(BF16)
            key_rows[h, at, :] = keys[local, h, :, at].astype(F32).T.astype(BF16)
            value_rows[h, at, :] = values[local, h, :, at].astype(F32).T.astype(BF16)

    def with_keys(count):
        def one_head(h, carry):
            own = pl.ds(pl.multiple_of(h * HEAD_DIM, 8), HEAD_DIM)
            grad_query = jnp.zeros((HEAD_ROWS, full), F32)
            for place in range(0, count, BLOCK):
                at = slice(place, min(place + BLOCK, count))
                probs = jnp.exp(product(key_rows[h, at, :], query_full[h])).astype(BF16)
                grad_probs = product(value_rows[h, at, :], upstream_full[h]).astype(BF16)
                grad_scores = probs * grad_probs
                grads[2, own, at] = product(upstream_full[h], probs, NT)[:HEAD_DIM]
                grads[1, own, at] = product(query_full[h], grad_scores, NT)[:HEAD_DIM]
                grad_query += product(keys[local, h, :, at], grad_scores)
            grads[0, own, :] = grad_query[:HEAD_DIM]
            return carry

        lax.fori_loop(0, heads, one_head, 0)
        if count < full:
            grads[1, :, count:] = jnp.zeros((span, full - count), F32)
            grads[2, :, count:] = jnp.zeros((span, full - count), F32)

    blocks = jnp.maximum((length + KEY_STEP - 1) // KEY_STEP, 1)
    for b in range(1, full // KEY_STEP + 1):
        pl.when(blocks == b)(lambda b=b: with_keys(b * KEY_STEP))

    sums = [[jnp.zeros((HEAD_DIM, 128), F32) for _ in range(heads)] for _ in range(3)]
    for j in range(chunks):
        at = slice(j * chunk, (j + 1) * chunk)
        cosine, sine = chunk_tables(inner, outer, j)
        query_cosine, query_sine = cosine * HEAD_DIM**-0.5, sine * HEAD_DIM**-0.5
        for h in range(heads):
            own = slice(h * HEAD_DIM, (h + 1) * HEAD_DIM)
            query, key, value = (grads[c, own, at] for c in range(3))
            query = query * query_cosine - swap_halves(query) * query_sine
            key = key * cosine - swap_halves(key) * sine
            for c, part in enumerate((query, key, value)):
                for piece in range(chunk // 128):
                    sums[c][h] = sums[c][h] + part[:, piece * 128 : (piece + 1) * 128]
                grads[c, own, at] = part
    for c in range(3):
        grad_low[c * span : (c + 1) * span, :] = grads[c].astype(BF16)
    for k in range(chunks):
        result = product(
            weight_turned[...], grad_low[:, at_block(position ^ k, chunk)]
        ).astype(BF16)
        if k == 0:
            own_out[...] = result
        elif k == 2:
            cross_out[...] = result
        else:
            near_out[k // 2] = result
    width = weight_turned.shape[0]
    fetch.wait()
    result = product(grad_low[...], normed[...], NT)
    bias_grad = jnp.concatenate(
        [jnp.sum(part, axis=1, keepdims=True) for group in sums for part in group]
    )
    bias_grad = jnp.broadcast_to(bias_grad, (3 * span, 128))
    if not first:
        result = result + carried[:, :width]
        bias_grad = bias_grad + carried[:, LANES:]
    if not last:
        running[:, :width] = result
        running[:, LANES:] = bias_grad
        return
    packed[: 3 * span, :width] = result
    gain_sum = jnp.zeros((8, width), F32)
    shift_sum = jnp.zeros((8, width), F32)
    gain, shift = vector_rows[0:1, :], vector_rows[1:2, :]
    for place in range(0, 3 * span, 8):
        own = slice(place, place + 8)
        factor = weight[own, :].astype(F32)
        column = bias_grad[own, 0:1]
        gain_sum = gain_sum + factor * (result[own] - shift * column)
        shift_sum = shift_sum + factor * column
    norm_sums[...] = jnp.zeros_like(norm_sums)
    norm_sums[0:1, :] = jnp.sum(gain_sum, axis=0, keepdims=True) / gain
    norm_sums[1:2, :] = jnp.sum(shift_sum, axis=0, keepdims=True)
    lane = lax.broadcasted_iota(jnp.int32, (3 * span, 128), 1)
    packed[: 3 * span, LANES - 128 :] = jnp.where(
        lane >= width - (LANES - 128), bias_grad, packed[: 3 * span, LANES - 128 :]
    )
    shared = (out_own[...].astype(F32) + out_near[0].astype(F32)) + out_cross[...].astype(F32)
    packed[3 * span : 4 * span, :] = shared[:span]
    packed[4 * span : 4 * span + 16, :] = shared[128:144]
    packed[4 * span + 16 :, :] = jnp.zeros((packed.shape[0] - 4 * span - 16, LANES), F32)
    size = packed.shape[0] // 8
    for j in range(8):
        target = odd_pieces if j % 2 else even_pieces
        target[j // 2] = packed[at_block(index ^ j, size), :].astype(BF16)


def gelu_parts(values):
    magnitude = jnp.abs(values) * (0.5**0.5)
    density = jnp.exp2(values * values * (-0.5 * LOG2E))
    divisor = 1.0 + 0.3275911 * magnitude
    step = pl.reciprocal(divisor, approx=True)
    step = step * (2.0 - divisor * step)
    series = 1.061405429 * step - 1.453152027
    series = series * step + 1.421413741
    series = series * step - 0.284496736
    series = series * step + 0.254829592
    tail = 0.5 * series * step * density
    share = jnp.where(values < 0, tail, 1.0 - tail)
    return share, density * (1.0 / math.sqrt(2.0 * math.pi))


def lane_groups(values):
    total = values[:, :128]
    for place in range(128, values.shape[1], 128):
        total = total + values[:, place : place + 128]
    return total


def row_sum(values):
    total = values[:8]
    for place in range(8, values.shape[0], 8):
        total = total + values[place : place + 8]
    return total


def feed_kernel(chunks, blocks, first_row, rows, last, info, lengths, *refs):
    hidden, cotangent, columns, up_bias = refs[:4]
    mixed_own, mixed_near, mixed_cross, mixed_far = refs[4:8]
    out_weight = refs[8 : 8 + chunks]
    refs = refs[8 + chunks :]
    if last:
        weights, carried, out_carried, sums_carried, bias_carried, hidden_before = refs[:6]
        refs = refs[6:]
    else:
        feeds, refs = refs[:12], refs[12:]
    hidden_out, grad_middle_out, grad_own, grad_near, grad_cross = refs[:5]
    refs = refs[5:]
    if last:
        kept_out, sent_out, out_own, out_near, out_cross = refs[:5]
    else:
        weights, carried, out_carried, sums_carried, bias_carried = refs[:5]
    refs = refs[5:]
    (
        out_rows,
        mixed,
        source,
        given,
        low_rows,
        down_total,
        back_total,
        upward,
        upstream,
        active,
        grad_low,
        sums_total,
        bias_total,
        shared,
        semaphores,
    ) = refs
    core, index = info[0] & 1, info[1]
    width, chunk = hidden.shape[1:]
    tokens = rows * chunk
    held = mixed_own.shape[1]
    places = [row_of(lengths, first_row + r, hidden.shape[0]) for r in range(rows)]
    if not last:
        copies = []
        for side in range(2):
            sources = list(feeds[6 * side : 6 * side + 4])
            duo, duo_beside = feeds[6 * side + 4 : 6 * side + 6]
            place = core if side == 0 else 1 - core
            for e in range(2):
                sources += [duo.at[e], duo_beside.at[e]]
            for j in range(blocks):
                copies.append(
                    pltpu.make_async_copy(
                        sources[j],
                        weights.at[place, :, j * BLOCK : (j + 1) * BLOCK],
                        semaphores.at[side, j],
                    )
                )
        for copy in copies:
            copy.start()
    own_rows = (out_weight[0].shape[0] - 2 * width) // 2
    for k in range(chunks):
        base = 2 * width
        at = k * held
        out_rows[at : at + held, :] = jnp.zeros((held, width), BF16)
        out_rows[at : at + own_rows, :chunk] = out_weight[k][base : base + own_rows, :]
        out_rows[at : at + own_rows, chunk:] = out_weight[k][
            base + own_rows : base + 2 * own_rows, : width - chunk
        ]
    for r in range(rows):
        at = slice(r * chunk, (r + 1) * chunk)
        mixed[0 * held : 1 * held, at] = mixed_own[r]
        mixed[1 * held : 2 * held, at] = mixed_near[r]
        mixed[2 * held : 3 * held, at] = mixed_cross[r, 0]
        mixed[3 * held : 4 * held, at] = mixed_far[r, 1]
        given[:, at] = cotangent[places[r]]
    source[...] = product(out_rows[...], mixed[...], TN)
    step = 32
    pieces = [slice(place, place + step) for place in range(0, width, step)]

    total = jnp.zeros((8, tokens), F32)
    for own in pieces:
        entered = jnp.concatenate([hidden[places[r], own, :] for r in range(rows)], axis=1)
        middle = source[own, :] + entered.astype(F32) + columns[own, 2:3]
        source[own, :] = middle
        total = total + row_sum(middle)
    mean = jnp.sum(total, axis=0, keepdims=True) * (1.0 / width)
    total = jnp.zeros((8, tokens), F32)
    for own in pieces:
        centre = source[own, :] - mean
        total = total + row_sum(centre * centre)
    inverse = lax.rsqrt(jnp.sum(total, axis=0, keepdims=True) * (1.0 / width) + EPS)
    for own in pieces:
        middle = source[own, :]
        unit = (middle - mean) * inverse
        low_rows[own, :] = (unit * columns[own, 3:4] + columns[own, 4:5]).astype(BF16)
        down_total[own, :] = middle + columns[own, 5:6]
        source[own, :] = unit
    back_total[...] = jnp.zeros_like(back_total)
    if not last:
        for copy in copies:
            copy.wait()

    pair = 2 * BLOCK

    def enter(i, slot):
        at = at_block(i, pair)
        upward[slot] = product(weights[0, :, at], low_rows[...], TN)
        upstream[slot] = product(weights[1, :, at], given[...], TN)

    lane = lax.broadcasted_iota(jnp.int32, (step, 128), 1)

    def bend(i, slot):
        for place in range(0, pair, step):
            own = slice(place, place + step)
            j = 2 * i + place // BLOCK
            inside = slice(place % BLOCK, place % BLOCK + step)
            bias = jnp.sum(
                jnp.where(lane == j, up_bias[inside, :], 0.0), axis=1, keepdims=True
            )
            values = upward[slot, own, :] + bias
            share, density = gelu_parts(values)
            active[slot, own, :] = (values * share).astype(BF16)
            grad_up = upstream[slot, own, :] * (share + values * density)
            grad_low[slot, own, :] = grad_up.astype(BF16)
            bias_sum = lane_groups(grad_up)
            if last:
                bias_total[j, inside, :] = bias_sum + bias_carried[j, inside, :]
            else:
                bias_carried[j, inside, :] = bias_sum

    def leave(i, slot):
        at = at_block(i, pair)
        down_total[...] += product(weights[1, :, at], active[slot])
        back_total[...] += product(weights[0, :, at], grad_low[slot])
        up_grad = product(low_rows[...], grad_low[slot], NT)
        down_grad = product(given[...], active[slot], NT)
        if not last:
            carried[0, :, at] = up_grad
            carried[1, :, at] = down_grad
            return
        up_grad = up_grad + carried[0, :, at]
        down_grad = down_grad + carried[1, :, at]
        kept = jnp.where(core == 0, up_grad, down_grad).astype(BF16)
        sent = jnp.where(core == 0, down_grad, up_grad).astype(BF16)
        for odd in range(2):
            kept_out[odd, i] = kept[:, odd * BLOCK : (odd + 1) * BLOCK]
            sent_out[odd, i] = sent[:, odd * BLOCK : (odd + 1) * BLOCK]

    def two_pairs(n, carry):
        i = 2 * n
        enter(i + 1, 1)
        bend(i, 0)
        leave(i, 0)
        enter(lax.rem(i + 2, blocks // 2), 0)
        bend(i + 1, 1)
        leave(i + 1, 1)
        return carry

    enter(0, 0)
    lax.fori_loop(0, blocks // 4, two_pairs, 0)
    if last:
        for r in range(first_row):
            hidden_out[row_of(lengths, r, hidden.shape[0])] = hidden_before[r]
    for r in range(rows):
        place = places[r] if last else r
        hidden_out[place] = down_total[:, r * chunk : (r + 1) * chunk].astype(BF16)
    scaled_total = jnp.zeros((8, tokens), F32)
    unit_total = jnp.zeros((8, tokens), F32)
    for own in pieces:
        scaled = back_total[own, :] * columns[own, 3:4]
        scaled_total = scaled_total + row_sum(scaled)
        unit_total = unit_total + row_sum(scaled * source[own, :])
    scaled_mean = jnp.sum(scaled_total, axis=0, keepdims=True) * (1.0 / width)
    unit_mean = jnp.sum(unit_total, axis=0, keepdims=True) * (1.0 / width)
    for own in pieces:
        back, unit = back_total[own, :], source[own, :]
        given_wide = given[own, :].astype(F32)
        scaled = back * columns[own, 3:4]
        grad_middle = given_wide + inverse * (scaled - scaled_mean - unit * unit_mean)
        for r in range(rows):
            grad_middle_out[r, own, :] = grad_middle[:, r * chunk : (r + 1) * chunk]
        low_rows[own, :] = grad_middle.astype(BF16)
        for place, part in enumerate((back * unit, back, grad_middle, given_wide)):
            part = lane_groups(part)
            if last:
                sums_total[place, own, :] = part + sums_carried[place, own, :]
            else:
                sums_carried[place, own, :] = part
    mixed_grad = product(out_rows[...], low_rows[...]).astype(BF16)
    for r in range(rows):
        at = slice(r * chunk, (r + 1) * chunk)
        grad_own[r] = mixed_grad[:held, at]
        grad_near[r] = mixed_grad[held : 2 * held, at]
        grad_cross[r, 0] = mixed_grad[2 * held : 3 * held, at]
        grad_cross[r, 1] = mixed_grad[3 * held :, at]
    out_part = product(mixed[...], low_rows[...], NT)
    if not last:
        out_carried[...] = out_part
        return
    out_part = (out_part + out_carried[...]).astype(BF16)
    shared[...] = jnp.zeros_like(shared)
    for place in range(4):
        line = row_sum(sums_total[place].T)
        shared[place : place + 1, :width] = jnp.sum(line, axis=0, keepdims=True)
    for j in range(blocks):
        line = row_sum(bias_total[j].T)
        shared[pl.ds(4 + (index ^ j), 1), :BLOCK] = jnp.sum(line, axis=0, keepdims=True)
    shared_low = shared[...].astype(BF16)
    for k, target in enumerate((out_own, out_near.at[0], out_cross, out_near.at[1])):
        target[:held, 384:] = jnp.zeros((held, LANES - 384), BF16)
        target[:held, :width] = out_part[k * held : (k + 1) * held]
        target[held:, :] = shared_low


def norm_back_kernel(rows, lengths, hidden, columns, *refs):
    middle_grads, refs = refs[:2], refs[2:]
    own_parts, near_parts = refs[0 : 2 * rows : 2], refs[1 : 2 * rows : 2]
    crossed, (out,) = refs[2 * rows : 2 * rows + rows // 2], refs[2 * rows + rows // 2 :]
    cross_parts = [part.at[place] for part in crossed for place in range(2)]
    gain = columns[:, 0:1]
    for row in range(rows):
        place = row_of(lengths, row, rows)
        unit, inverse = norm_columns(hidden[place].astype(F32))
        grad = (
            own_parts[row][...].astype(F32)
            + near_parts[row][0].astype(F32)
            + cross_parts[row][...].astype(F32)
        )
        half = rows // 2
        result = middle_grads[row // half][row % half] + norm_columns_back(
            grad, unit, inverse, gain
        )
        out[place] = result.astype(BF16)


def add_pieces_kernel(even, beside, *outs):
    for i, out in enumerate(outs):
        out[...] = (even[i].astype(F32) + beside[i].astype(F32)).astype(BF16)


def own_piece_kernel(first, second, fourth, sixth, norm_sums, out):
    size = first.shape[0]
    total = first[...].astype(F32) + second[...].astype(F32)
    total = total + fourth[...].astype(F32) + sixth[...].astype(F32)
    out[:size, :] = total.astype(BF16)
    width = norm_sums.shape[1]
    values = norm_sums[...]
    high = values.astype(BF16)
    rest = (values - high.astype(F32)).astype(BF16)
    out[size:, 384:] = jnp.zeros((16, LANES - 384), BF16)
    out[size:, :width] = jnp.concatenate([high.astype(F32), rest.astype(F32)]).astype(BF16)


def feed_sum_kernel(info, first, second, fourth, sixth, keep, send, rows):
    total = first[...].astype(F32) + second[...].astype(F32)
    rows[...] = total + fourth[...].astype(F32) + sixth[...].astype(F32)
    size = keep.shape[0]
    chip = info[0] >> 1
    keep[...] = rows[at_block(chip, size), :].astype(BF16)
    send[...] = rows[at_block(1 - chip, size), :].astype(BF16)


def feed_pair_kernel(info, kept, came, mine, other, rows):
    rows[...] = kept[...].astype(F32) + came[...].astype(F32)
    size = mine.shape[0]
    core = info[0] & 1
    mine[...] = rows[at_block(core, size), :].astype(BF16)
    other[...] = rows[at_block(1 - core, size), :].astype(BF16)


def unpack_kernel(info, *refs):
    evens, beside = refs[:4], refs[4]
    refs = refs[5:]
    if len(refs) > 12:
        mine, came, refs = refs[0], refs[1], refs[2:]
        up_grad, down_grad = refs[10:12]
        refs = refs[:10] + refs[12:]
        count = up_grad.shape[1]

        def write(up, down):
            up_grad[...] = up[:, :count].astype(F32)
            down_grad[...] = down[...].astype(F32).T[:count, :]

        pl.when(info[0] & 1 == 0)(lambda: write(mine, came))
        pl.when(info[0] & 1 == 1)(lambda: write(came, mine))
    weight_grad, bias_grad, out_grad, gain, shift, out_bias, down_bias, up_bias = refs[:8]
    norm_gain, norm_shift, whole, line = refs[8:]
    size = whole.shape[0] // 8
    width = weight_grad.shape[1]
    norms = [evens[0][size:, :].astype(F32) + beside[0, size:, :].astype(F32)]
    for i in range(4):
        whole[at_block(info[1] ^ (2 * i), size), :] = evens[i][:size, :].astype(F32)
        whole[at_block(info[1] ^ (2 * i + 1), size), :] = beside[i, :size, :].astype(F32)
        if i > 0:
            norms.append(evens[i][size:, :].astype(F32) + beside[i, size:, :].astype(F32))
    norms = (norms[0] + norms[1]) + (norms[2] + norms[3])
    norms = norms[:8] + norms[8:16]
    norm_gain[...] = norms[0:1, :width]
    norm_shift[...] = norms[1:2, :width]
    columns = weight_grad.shape[2]
    for c in range(3):
        turned = whole[c * columns : (c + 1) * columns, :].T
        weight_grad[c] = turned[:width, :]
        bias_grad[c : c + 1, :] = turned[width : width + 1, :]
    out_grad[...] = whole[3 * columns : 4 * columns, :width]
    for place, target in enumerate((gain, shift, out_bias, down_bias)):
        target[...] = whole[4 * columns + place : 4 * columns + place + 1, :width]
    block = up_bias.shape[0] // 8
    for j in range(8):
        line[:, j * block : (j + 1) * block] = whole[
            4 * columns + 4 + j : 4 * columns + 5 + j, :block
        ]
    up_bias[...] = line[0, :]


def swap(values, axis, bit):
    size = lax.axis_size(axis)
    return lax.ppermute(values, axis, [(i, i ^ bit) for i in range(size)])


def gather_four(own, *others):
    beside = swap(own, "tensor", 1)
    across = swap(own, "tensor", 2)
    return [own, beside, across, swap(after(across, *others), "tensor", 1)]


def spread_four(own, near, cross, beside, *others):
    across = swap(cross, "tensor", 2)
    return [own, beside, across, swap(after(across, *others), "tensor", 1)]


def add_low(*parts):
    total = parts[0].astype(F32)
    for part in parts[1:]:
        total = total + part.astype(F32)
    return total.astype(BF16)


def gather_feed_plain(up, down, core):
    pair = jnp.stack([up, down.T])
    pair = lax.all_gather(pair, "tensor", axis=1, tiled=True)
    pair = lax.all_gather(pair, "dp", axis=2, tiled=True)
    pair = pair.reshape(2, pair.shape[1], 8, -1).transpose(0, 2, 1, 3)
    pair = jnp.pad(pair, ((0, 0), (0, 0), (0, 0), (0, BLOCK - pair.shape[3])))
    pair = jnp.where(core == 0, pair, pair[::-1])
    feeds = []
    for half in (pair[0], pair[1]):
        feeds += [half[0], half[1], half[2], half[3], half[4::2], half[5::2]]
    return feeds


def scatter_feed_plain(kept, sent, core, hidden_count):
    grads = jnp.stack([kept, sent]).swapaxes(1, 2).reshape(2, 8, *kept.shape[2:])
    grads = jnp.where(core == 0, grads, grads[::-1]).astype(F32)
    grads = grads[:, :, :, : hidden_count * lax.axis_size("dp") // 8]
    grads = grads.transpose(0, 2, 1, 3).reshape(2, grads.shape[2], -1)
    grads = lax.psum_scatter(grads, "dp", scatter_dimension=2, tiled=True)
    grads = lax.psum_scatter(grads, "tensor", scatter_dimension=1, tiled=True)
    return grads[0], grads[1].T


def sum_pieces(even, beside, norm_sums):
    parts = call(
        add_pieces_kernel,
        (even, beside),
        [shape(even.shape[1:], BF16)] * 4,
        limit=4,
    )
    parts = [parts[0]] + [swap(parts[i], "dp", 2 * i) for i in (1, 2, 3)]
    norm_sums = norm_sums + swap(norm_sums, "tensor", 1)
    (own,) = call(
        own_piece_kernel,
        (*parts, norm_sums),
        [shape((even.shape[1] + 16, LANES), BF16)],
        limit=4,
    )
    back = [own] + [swap(own, "dp", e) for e in (2, 4, 6)]
    return back + [swap(jnp.stack(back), "dp", 1)], own


def sum_pieces_plain(even, odd, norm_sums):
    even, odd = (lax.psum(part.astype(F32), "dp").astype(BF16) for part in (even, odd))
    norm_sums = lax.psum(norm_sums, ("dp", "tensor"))
    high = norm_sums.astype(BF16)
    rest = (norm_sums - high.astype(F32)).astype(BF16)
    rows = jnp.concatenate([high, rest])
    rows = jnp.pad(rows, ((0, 0), (0, LANES - rows.shape[1])))
    even = jnp.concatenate([even, jnp.stack([rows] + [jnp.zeros_like(rows)] * 3)], axis=1)
    odd = jnp.concatenate([odd, jnp.zeros((4, *rows.shape), BF16)], axis=1)
    return [even[i] for i in range(4)] + [odd]


def shards(
    hidden_in,
    attn_gain,
    attn_shift,
    query_key_value_weight,
    query_key_value_bias,
    attention_output_weight,
    out_bias,
    ffn_gain,
    ffn_shift,
    up_projection_weight,
    up_projection_bias,
    down_projection_weight,
    down_bias,
    lengths,
    cotangent,
):
    chunks = lax.axis_size("tensor")
    ring = lax.axis_size("dp") == 8
    position = lax.axis_index("tensor")
    index = lax.axis_index("dp") if ring else jnp.int32(0)
    core = position & 1
    rows, chunk, width = hidden_in.shape
    full = chunk * chunks
    columns = query_key_value_weight.shape[2]
    heads = columns // HEAD_DIM
    hidden_count = up_projection_weight.shape[1]
    blocks = 8
    half = rows // 2

    info = jnp.stack([position, index]).astype(jnp.int32)
    lengths = lengths.astype(jnp.int32)
    inner_table, outer_table = (jnp.asarray(table) for table in rotary_constants(chunk, chunks))
    hidden = hidden_in.transpose(0, 2, 1)
    given = cotangent.transpose(0, 2, 1)

    if ring:
        inputs = (info, up_projection_weight, down_projection_weight)
        (pair,) = call(
            pair_kernel,
            inputs,
            [shape((columns, 2 * BLOCK), BF16)],
            scratch=[pltpu.VMEM(part.shape, part.dtype) for part in inputs[1:]]
            + [pltpu.SemaphoreType.DMA((2,))],
            in_specs=[smem()] + hbm(2),
            limit=4,
            tiles=20,
        )
        pair_across = swap(pair, "tensor", 2)
    inputs = (
        lengths,
        after(hidden, pair) if ring else hidden,
        attn_gain[None],
        attn_shift[None],
        attention_output_weight,
    )
    first, second = call(
        norm_kernel,
        inputs,
        [
            shape((half * width, chunk), BF16),
            shape((half * width + 2 * columns, chunk), BF16),
        ],
        scratch=[pltpu.VMEM(part.shape, part.dtype) for part in inputs[1:]]
        + [pltpu.VMEM((128, width), F32), pltpu.SemaphoreType.DMA((8,))],
        in_specs=[smem()] + hbm(4),
        limit=8,
        tiles=80,
    )
    inputs = (
        info,
        attn_gain[None],
        attn_shift[None],
        out_bias[None],
        ffn_gain[None],
        ffn_shift[None],
        down_bias[None],
        up_projection_bias[None],
        query_key_value_weight,
        query_key_value_bias,
    )
    weight, weight_turned, vectors, bias, up_bias, vector_rows = call(
        lambda *refs: prepare_kernel(heads, *refs),
        inputs,
        [
            shape((3 * columns, width), BF16),
            shape((width, 3 * columns), BF16),
            shape((width, 128), F32),
            shape((3 * columns, 128), F32),
            shape((BLOCK, 128), F32),
            shape((8, width), F32),
        ],
        scratch=[
            pltpu.VMEM((3 * columns, width), F32),
            pltpu.VMEM((128, BLOCK), F32),
        ]
        + [pltpu.VMEM(part.shape, part.dtype) for part in inputs[1:]]
        + [pltpu.SemaphoreType.DMA((9,))],
        in_specs=[smem()] + hbm(len(inputs) - 1),
        limit=8,
        tiles=60,
    )
    if ring:
        parts = [
            pair,
            swap(pair, "tensor", 1),
            pair_across,
            swap(after(pair_across, first), "tensor", 1),
        ]
        (own_feed,) = call(
            lambda *refs: assemble_kernel(chunks, *refs),
            (info, *parts),
            [shape((width, BLOCK), BF16)],
            scratch=[pltpu.VMEM((width, BLOCK), F32)],
            in_specs=[smem()] + vmem(chunks),
            limit=6,
            tiles=20,
        )
        came = [swap(own_feed, "dp", e) for e in (2, 4, 6)]
        beside = swap(own_feed, "dp", 1)
        second_beside = swap(came[0], "dp", 1)
        gathered = [
            gather_four(after(first, pair_across), own_feed, came[0], beside, weight)
        ]
    else:
        gathered = [gather_four(first)]

    kept = []
    mixed = []
    for g in range(2):
        if g == 1 and ring:
            gathered[1][0] = after(gathered[1][0], duo, beside, second_beside, mixed[0][3])
        inputs = (info, lengths, *gathered[g], weight, bias, inner_table, outer_table)
        outs = call(
            lambda *refs, g=g: attend_kernel(heads, chunks, chunk, g * half, half, *refs),
            inputs,
            [
                shape((half, 128, chunk), BF16),
                shape((half, 128, chunk), BF16),
                shape((half, 2, 128, chunk), BF16),
            ]
            + [shape((half, heads, HEAD_ROWS, full), BF16)] * 3
            + [
                shape((half, 8, full), F32),
                shape((half, 128, full), F32),
                shape((half, width, full), BF16),
            ],
            scratch=[
                pltpu.VMEM((heads, full, HEAD_ROWS), BF16),
                pltpu.VMEM((8, full), F32),
                pltpu.VMEM((3 * columns, full), F32),
                pltpu.VMEM((half, width, full), BF16),
                pltpu.SemaphoreType.DMA((half,)),
            ],
            in_specs=[smem(), smem()] + vmem(len(inputs) - 2),
            out_specs=vmem(8) + hbm(),
            limit=14,
            tiles=400,
        )
        kept.append(outs[3:])
        mixed.append(list(outs[:3]) + [swap(outs[1], "tensor", 1)])
        if g == 0:
            gathered.append(gather_four(after(second, gathered[0][2]), outs[0]))
            if ring:
                duo = jnp.stack([after(part, mixed[0][3], second_beside) for part in came[1:]])
                duo_beside = swap(duo, "dp", 1)
            else:
                feeds = gather_feed_plain(up_projection_weight, down_projection_weight, core)

    if ring:
        duo_beside = after(duo_beside, kept[1][0])
        feeds = [own_feed, beside, came[0], second_beside, duo, duo_beside]
        feeds += [swap(part, "tensor", 1) for part in feeds]
    feed_outs = []
    for g in range(2):
        last = g == 1
        others = (kept[1][0],) if g == 0 else (feed_outs[0][2],)
        ready = (mixed[1][3],) if g == 0 else (mixed_near,)
        inputs = (
            info,
            lengths,
            hidden,
            after(given, *ready),
            vectors,
            up_bias,
            *spread_four(*mixed[g], *others),
            *gathered[1],
        )
        if last:
            inputs = inputs + tuple(feed_outs[0][5:]) + (feed_outs[0][0],)
        else:
            inputs = inputs + tuple(feeds)
        carried = [
            shape((2, width, blocks * BLOCK), BF16),
            shape((2, width, blocks * BLOCK), F32),
            shape((chunks * 128, width), F32),
            shape((4, width, 128), F32),
            shape((blocks, BLOCK, 128), F32),
        ]
        sent = [
            shape((2, blocks // 2, width, BLOCK), BF16),
            shape((2, blocks // 2, width, BLOCK), BF16),
            shape((144, LANES), BF16),
            shape((2, 144, LANES), BF16),
            shape((144, LANES), BF16),
        ]
        tokens = half * chunk
        outs = call(
            lambda *refs, g=g, last=last: feed_kernel(
                chunks, blocks, g * half, half, last, *refs
            ),
            inputs,
            [
                shape((rows if last else half, width, chunk), BF16),
                shape((half, width, chunk), F32),
                shape((half, 128, chunk), BF16),
                shape((half, 128, chunk), BF16),
                shape((half, 2, 128, chunk), BF16),
            ]
            + (sent if last else carried),
            scratch=[
                pltpu.VMEM((chunks * 128, width), BF16),
                pltpu.VMEM((chunks * 128, tokens), BF16),
                pltpu.VMEM((width, tokens), F32),
                pltpu.VMEM((width, tokens), BF16),
                pltpu.VMEM((width, tokens), BF16),
                pltpu.VMEM((width, tokens), F32),
                pltpu.VMEM((width, tokens), F32),
                pltpu.VMEM((2, 2 * BLOCK, tokens), F32),
                pltpu.VMEM((2, 2 * BLOCK, tokens), F32),
                pltpu.VMEM((2, 2 * BLOCK, tokens), BF16),
                pltpu.VMEM((2, 2 * BLOCK, tokens), BF16),
                pltpu.VMEM((4, width, 128), F32),
                pltpu.VMEM((blocks, BLOCK, 128), F32),
                pltpu.VMEM((16, LANES), F32),
                pltpu.SemaphoreType.DMA((2, blocks)),
            ],
            in_specs=[smem(), smem()]
            + (
                vmem(len(inputs) - 2)
                if last
                else vmem(len(inputs) - 2 - len(feeds)) + [pl.BlockSpec(memory_space=pl.ANY)] * len(feeds)
            ),
            limit=22,
            tiles=500,
        )
        feed_outs.append(outs)
        if g == 0:
            mixed_near = swap(outs[3], "tensor", 1)
    hidden_out = feed_outs[1][0]
    middle_grads = [outs[1] for outs in feed_outs]
    feed_kept, feed_sent, out_own, out_near, out_cross = feed_outs[1][5:]

    mixed_grads = [spread_four(*feed_outs[0][2:5], mixed_near, feed_outs[1][2])]
    feed_sent, out_near = after((feed_sent, out_near), mixed_grads[0][3])
    out_came = swap(out_near, "tensor", 1)
    feed_came = swap(feed_sent, "tensor", 1)
    running = None
    reduced = []
    crossing = []
    for r in range(rows):
        last = r == rows - 1
        g = r // half
        inputs = (
            info,
            lengths,
            *mixed_grads[g],
            *kept[g],
            weight_turned,
            inner_table,
            outer_table,
        )
        if last and ring:
            running = after(running, *evens)
        if r > 0:
            inputs = inputs + (running,)
        if last:
            inputs = inputs + (out_own, out_came, out_across, weight, vector_rows)
        outs = call(
            lambda *refs, r=r, last=last: attend_back_kernel(
                heads, chunks, chunk, r, r % half, r == 0, last, *refs
            ),
            inputs,
            [
                shape((width, chunk), BF16),
                shape((2, width, chunk), BF16),
                shape((width, chunk), BF16),
            ]
            + (
                [shape((4, 64, LANES), BF16)] * 2 + [shape((8, width), F32)]
                if last
                else [shape((3 * columns, LANES + 128), F32)]
            ),
            scratch=[
                pltpu.VMEM((128, full), BF16),
                pltpu.VMEM((heads, HEAD_ROWS, full), BF16),
                pltpu.VMEM((heads, HEAD_ROWS, full), BF16),
                pltpu.VMEM((heads, full, HEAD_ROWS), BF16),
                pltpu.VMEM((heads, full, HEAD_ROWS), BF16),
                pltpu.VMEM((3, columns, full), F32),
                pltpu.VMEM((3 * columns, full), BF16),
                pltpu.VMEM((512, LANES), F32),
                pltpu.VMEM((width, full), BF16),
                pltpu.SemaphoreType.DMA(()),
            ],
            in_specs=[smem(), smem()] + vmem(9) + hbm() + vmem(len(inputs) - 12),
            limit=12,
            tiles=420,
        )
        if last:
            outs = list(outs)
            even, odd, norm_sums = outs[3:]
            if ring:
                odd = after(odd, reduced[5], *feed_came)
                beside_pieces = swap(odd, "dp", 1)
                norm_sums = norm_sums + swap(norm_sums, "tensor", 2)
                outs[1] = after(outs[1], beside_pieces, norm_sums)
        near = swap(outs[1], "tensor", 1)
        reduced += [outs[0], near, None]
        crossing.append((outs[2], near))
        if r >= 2:
            pair_sum = jnp.stack(
                [
                    add_low(after(cross, outs[0], out_across), near[1])
                    for cross, near in crossing[2 * r - 4 : 2 * r - 2]
                ]
            )
            reduced[3 * (2 * r - 3) + 2] = swap(pair_sum, "tensor", 2)
        if not last:
            running = outs[3]
        if r == 1:
            mixed_near = swap(feed_outs[1][3], "tensor", 1)
            mixed_grads.append(spread_four(*feed_outs[1][2:5], mixed_near, outs[0]))
        if r == 0:
            out_across = swap(
                add_low(after(out_cross, outs[0]), out_came[1]), "tensor", 2
            )
            if ring:
                feed_odd = add_low(after(feed_kept[1], outs[0]), feed_came[1])
                running = after(running, feed_odd)
                feed_odd = swap(feed_odd, "dp", 1)
        if r == 2 and ring:
            feed_kept = after(feed_kept, outs[0])
            evens = [
                add_low(feed_kept[0, i], feed_came[0, i], feed_odd[i]) for i in range(4)
            ]
            feed_came = [swap(evens[i], "dp", 2 * i) for i in (1, 2, 3)]
    own_parts = [part for place, part in enumerate(reduced) if place % 3 < 2]
    cross_parts = [part for part in reduced[2::3] if part is not None]
    inputs = (lengths, hidden, vectors, *middle_grads, *own_parts, *cross_parts)
    (grad_hidden,) = call(
        lambda *refs: norm_back_kernel(rows, *refs),
        inputs,
        [shape((rows, width, chunk), BF16)],
        in_specs=[smem()] + vmem(len(inputs) - 1),
        limit=12,
        tiles=120,
    )
    if ring:
        parts, own = sum_pieces(even, beside_pieces, norm_sums)
    else:
        parts = sum_pieces_plain(even, odd, norm_sums)
    if ring:
        keep, send = call(
            feed_sum_kernel,
            (info, after(evens[0], own), *feed_came),
            [shape((width // 2, BLOCK), BF16)] * 2,
            scratch=[pltpu.VMEM((width, BLOCK), F32)],
            in_specs=[smem()] + vmem(4),
            limit=4,
            tiles=20,
        )
        mine, other = call(
            feed_pair_kernel,
            (info, keep, after(swap(send, "tensor", 2), grad_hidden)),
            [shape((columns, BLOCK), BF16)] * 2,
            scratch=[pltpu.VMEM((width // 2, BLOCK), F32)],
            in_specs=[smem()] + vmem(2),
            limit=4,
            tiles=20,
        )
        feed_parts = (mine, swap(other, "tensor", 1))
    else:
        grad_up_weight, grad_down_weight = scatter_feed_plain(
            feed_kept, feed_sent, core, hidden_count
        )

    inputs = (info, *parts) + (feed_parts if ring else ())
    outs = [
        shape((3, width, columns), F32),
        shape((3, columns), F32),
        shape((columns, width), F32),
    ]
    outs += [shape((1, width), F32)] * 4
    outs += [shape(up_projection_bias.shape, F32)]
    outs += [shape((1, width), F32)] * 2
    if ring:
        outs += [shape((columns, hidden_count), F32), shape((hidden_count, columns), F32)]
    outs = call(
        unpack_kernel,
        inputs,
        outs,
        scratch=[
            pltpu.VMEM((512, LANES), F32),
            pltpu.VMEM((1, up_projection_bias.shape[0]), F32),
        ],
        in_specs=[smem()] + vmem(len(inputs) - 1),
        limit=8,
        tiles=60,
    )
    grad_qkv_weight, grad_qkv_bias, grad_out_weight = outs[:3]
    grad_ffn_gain, grad_ffn_shift, grad_out_bias, grad_down_bias, grad_up_bias = outs[3:8]
    grad_attn_gain, grad_attn_shift = outs[8:10]
    if ring:
        grad_up_weight, grad_down_weight = outs[10:]
    return (
        hidden_out.transpose(0, 2, 1),
        grad_hidden.transpose(0, 2, 1),
        grad_attn_gain[0],
        grad_attn_shift[0],
        grad_qkv_weight,
        grad_qkv_bias,
        grad_out_weight,
        grad_out_bias[0],
        grad_ffn_gain[0],
        grad_ffn_shift[0],
        grad_up_weight,
        grad_up_bias,
        grad_down_weight,
        grad_down_bias[0],
    )


def solution(mesh):
    return jax.shard_map(
        shards,
        mesh=mesh,
        in_specs=(
            P("dp", "tensor", None),
            P(),
            P(),
            P(None, None, "tensor"),
            P(None, "tensor"),
            P("tensor", None),
            P(),
            P(),
            P(),
            P("tensor", "dp"),
            P(),
            P("dp", "tensor"),
            P(),
            P("dp"),
            P("dp", "tensor", None),
        ),
        out_specs=(
            P("dp", "tensor", None),
            P("dp", "tensor", None),
            P(),
            P(),
            P(None, None, "tensor"),
            P(None, "tensor"),
            P("tensor", None),
            P(),
            P(),
            P(),
            P("tensor", "dp"),
            P(),
            P("dp", "tensor"),
            P(),
        ),
        check_vma=False,
    )
```

```python
import math

import jax
import jax.numpy as jnp
import numpy as np
from jax import lax
from jax.experimental import pallas as pl
from jax.experimental.pallas import tpu as pltpu
from jax.sharding import PartitionSpec as P

HEAD_DIM = 24
HEAD_ROWS = 32
EPS = 1e-05
MASK_FILL = -1000000000.0
LOG2E = math.log2(math.e)
SAFE_SCORE = 58.0
WORK_SCALE = 0.01
BLOCK = 256
KEY_STEP = 256
LANES = 512
BF16 = jnp.bfloat16
F32 = jnp.float32

NN = (((1,), (0,)), ((), ()))
NT = (((1,), (1,)), ((), ()))
TN = (((0,), (0,)), ((), ()))


def product(left, right, dims=NN):
    return lax.dot_general(left, right, dims, preferred_element_type=F32)


def vmem(count):
    return [pl.BlockSpec(memory_space=pltpu.VMEM)] * count


def smem():
    return pl.BlockSpec(memory_space=pltpu.SMEM)


def hbm(count=1):
    return [pl.BlockSpec(memory_space=pltpu.HBM)] * count


def call(kernel, inputs, outs, scratch=(), in_specs=None, out_specs=None, limit=40, tiles=0):
    flops = int(2 * 256**3 * tiles * WORK_SCALE)
    in_specs = vmem(len(inputs)) if in_specs is None else in_specs
    inputs = [
        pltpu.with_memory_space_constraint(part, pltpu.HBM)
        if spec.memory_space is pltpu.HBM
        else part
        for part, spec in zip(inputs, in_specs)
    ]
    out_specs = vmem(len(outs)) if out_specs is None else out_specs
    outs = [
        pltpu.HBM(part.shape, part.dtype) if spec.memory_space is pltpu.HBM else part
        for part, spec in zip(outs, out_specs)
    ]
    return pl.pallas_call(
        kernel,
        out_shape=outs,
        in_specs=in_specs,
        out_specs=out_specs,
        scratch_shapes=list(scratch),
        compiler_params=pltpu.CompilerParams(vmem_limit_bytes=limit << 20),
        cost_estimate=pl.CostEstimate(flops=flops, transcendentals=0, bytes_accessed=0),
    )(*inputs)


def shape(dims, dtype):
    return jax.ShapeDtypeStruct(dims, dtype)


def at_block(index, size):
    return pl.ds(pl.multiple_of(index * size, size), size)


def split_three(values):
    high = values.astype(BF16).astype(F32)
    rest = values - high
    middle = rest.astype(BF16).astype(F32)
    return high, middle, rest - middle


def row_of(lengths, slot, rows):
    slot = jnp.where(slot == 0, 0, jnp.where(slot == 1, rows - 1, slot - 1))
    chosen = jnp.int32(0)
    for i in range(rows):
        rank = jnp.int32(0)
        for j in range(rows):
            if j < i:
                rank += jnp.where(lengths[j] <= lengths[i], 1, 0)
            elif j > i:
                rank += jnp.where(lengths[j] < lengths[i], 1, 0)
        chosen += jnp.where(rank == slot, i, 0)
    return chosen


def after(values, *others):
    return lax.optimization_barrier((values, *others))[0]


def norm_columns(values):
    centre = values - jnp.mean(values, axis=0, keepdims=True)
    inverse = lax.rsqrt(jnp.mean(centre * centre, axis=0, keepdims=True) + EPS)
    return centre * inverse, inverse


def norm_columns_back(upstream, unit, inverse, gain):
    scaled = upstream * gain
    centred = scaled - jnp.mean(scaled, axis=0, keepdims=True)
    return inverse * (centred - unit * jnp.mean(scaled * unit, axis=0, keepdims=True))


def pair_kernel(info, up, down, pair, up_inside, down_inside, semaphores):
    copies = [
        pltpu.make_async_copy(up, up_inside, semaphores.at[0]),
        pltpu.make_async_copy(down, down_inside, semaphores.at[1]),
    ]
    for copy in copies:
        copy.start()
    pair[...] = jnp.zeros_like(pair)
    for copy in copies:
        copy.wait()
    size = up.shape[1]
    up_half = up_inside[...]
    down_half = down_inside[...].astype(F32).T.astype(BF16)

    @pl.when(info[0] & 1 == 0)
    def _():
        pair[:, :size] = up_half
        pair[:, BLOCK : BLOCK + size] = down_half

    @pl.when(info[0] & 1 == 1)
    def _():
        pair[:, :size] = down_half
        pair[:, BLOCK : BLOCK + size] = up_half


def norm_kernel(
    lengths,
    hidden_in,
    gain,
    shift,
    out_weight_in,
    first_out,
    second_out,
    hidden,
    gain_inside,
    shift_inside,
    out_weight,
    rows_scratch,
    semaphores,
):
    rows, width, chunk = hidden.shape
    copies = [
        pltpu.make_async_copy(
            hidden_in.at[row_of(lengths, slot, rows)], hidden.at[slot], semaphores.at[slot]
        )
        for slot in range(rows)
    ]
    others = [
        pltpu.make_async_copy(gain, gain_inside, semaphores.at[4]),
        pltpu.make_async_copy(shift, shift_inside, semaphores.at[5]),
        pltpu.make_async_copy(out_weight_in, out_weight, semaphores.at[6]),
    ]
    for copy in others[:2] + copies + others[2:]:
        copy.start()
    rows_scratch[...] = jnp.zeros_like(rows_scratch)
    others[0].wait()
    others[1].wait()
    rows_scratch[0:1, :] = gain_inside[...]
    rows_scratch[1:2, :] = shift_inside[...]
    columns = rows_scratch[...].T
    half = rows // 2
    for row in range(rows):
        copies[row].wait()
        unit, _ = norm_columns(hidden[row].astype(F32))
        target = first_out if row < half else second_out
        place = row % half * width
        target[place : place + width, :] = (unit * columns[:, 0:1] + columns[:, 1:2]).astype(
            BF16
        )
    others[2].wait()
    own = out_weight.shape[0]
    second_out[half * width : half * width + own, :] = out_weight[:, :chunk]
    rest = width - chunk
    second_out[half * width + own : half * width + 2 * own, :] = jnp.zeros((own, chunk), BF16)
    second_out[half * width + own : half * width + 2 * own, :rest] = out_weight[:, chunk:]


def prepare_kernel(heads, info, *refs):
    outside, refs = refs[:9], refs[9:]
    weight_out, weight_turned_out, columns_out, bias_out, up_bias_out, vector_rows = refs[:6]
    weight_scratch, bias_rows = refs[6:8]
    inside, semaphores = refs[8:17], refs[17]
    copies = [
        pltpu.make_async_copy(source, target, semaphores.at[place])
        for place, (source, target) in enumerate(zip(outside, inside))
    ]
    for copy in copies:
        copy.start()
    vectors, (up_bias, weight, bias) = inside[:6], inside[6:]
    width = weight.shape[1]
    vector_rows[...] = jnp.zeros_like(vector_rows)
    for copy in copies:
        copy.wait()
    for place, vector in enumerate(vectors):
        vector_rows[place : place + 1, :] = vector[...]
    columns_out[...] = jnp.concatenate([vector_rows[...], jnp.zeros((120, width), F32)]).T
    span = heads * HEAD_DIM
    for c in range(3):
        own = slice(c * span, (c + 1) * span)
        weight_scratch[own, :] = weight[c].astype(F32).T
        bias_out[own, :] = jnp.broadcast_to(bias[c : c + 1, :], (128, span)).T
    weight_out[...] = weight_scratch[...].astype(BF16)
    weight_turned_out[...] = weight_scratch[...].T.astype(BF16)
    bias_rows[...] = jnp.zeros_like(bias_rows)
    count = up_bias.shape[1]
    block = count // 8
    spread = jnp.broadcast_to(up_bias[...], (8, count))
    for j in range(8):
        moved = pltpu.roll(spread, lax.rem(count - (info[1] ^ j) * block, count), 1)
        bias_rows[j : j + 1, :block] = moved[0:1, :block]
    up_bias_out[...] = bias_rows[...].T


def assemble_kernel(chunks, info, *refs):
    parts, (out, rows) = refs[:chunks], refs[chunks:]
    size = parts[0].shape[0]
    for k in range(chunks):
        half = parts[k][:, (k & 1) * BLOCK : ((k & 1) + 1) * BLOCK]
        rows[at_block(info[0] ^ k, size), :] = half.astype(F32)
    out[...] = rows[...].astype(BF16)


def rotary_constants(chunk, chunks):
    half = HEAD_DIM // 2
    element = np.arange(HEAD_DIM)
    frequency = (1.0 / 10000.0 ** (np.arange(0, HEAD_DIM, 2).astype(np.float32) / HEAD_DIM)).astype(
        np.float32
    )
    per_row = frequency[element % half].astype(np.float64)
    inner = per_row[:, None] * np.arange(chunk)[None, :]
    outer = per_row[:, None] * (np.arange(chunks) * chunk)[None, :]
    outer = np.repeat(outer[:, :, None], chunk, axis=2).transpose(1, 0, 2)
    inner_pair = np.stack([np.cos(inner), np.sin(inner)]).astype(np.float32)
    outer_pair = np.stack([np.cos(outer), np.sin(outer)]).astype(np.float32)
    return inner_pair, outer_pair


def chunk_tables(inner, outer, index):
    cos_in, sin_in = inner[0], inner[1]
    cos_out, sin_out = outer[0, index], outer[1, index]
    element = lax.broadcasted_iota(jnp.int32, cos_in.shape, 0)
    sine = sin_in * cos_out + cos_in * sin_out
    return cos_in * cos_out - sin_in * sin_out, jnp.where(
        element < HEAD_DIM // 2, -sine, sine
    )


def swap_halves(values):
    return pltpu.roll(values, HEAD_DIM // 2, 0)


def attend_kernel(heads, chunks, chunk, first_row, rows, info, lengths, *refs):
    parts = refs[:chunks]
    weight, bias, inner, outer, own_out, near_out, cross_out = refs[chunks : chunks + 7]
    queries, keys, values, logsum, mixed_turned, normed_out, key_rows, peak, flat = refs[
        chunks + 7 : chunks + 16
    ]
    normed, semaphores = refs[chunks + 16 :]
    position = info[0]
    width = normed.shape[1]
    full = chunk * chunks
    span = heads * HEAD_DIM
    scale = HEAD_DIM**-0.5

    def one_row(r, carry):
        length = lengths[row_of(lengths, first_row + r, lengths.shape[0])]
        for k in range(chunks):
            normed[r, :, at_block(position ^ k, chunk)] = parts[k][at_block(r, width), :]
        pltpu.make_async_copy(normed.at[r], normed_out.at[r], semaphores.at[r]).start()
        flat[...] = product(weight[...], normed[r])
        line = lax.broadcasted_iota(jnp.int32, (8, chunk), 0)
        ones = jnp.where(line < 3, 1.0, 0.0)
        query_line = jnp.where(line == 3, 1.0, 0.0)
        query_top = [jnp.zeros((1, chunk), F32) for _ in range(heads)]
        key_top = [jnp.zeros((1, chunk), F32) for _ in range(heads)]
        for j in range(chunks):
            at = slice(j * chunk, (j + 1) * chunk)
            cosine, sine = chunk_tables(inner, outer, j)
            query_cosine, query_sine = cosine * scale, sine * scale
            place = lax.broadcasted_iota(jnp.int32, (8, chunk), 1) + j * chunk
            key_line = jnp.where((line == 3) & (place >= length), MASK_FILL, ones)
            for h in range(heads):
                here = h * HEAD_DIM
                query, key, value = (
                    flat[c * span + here : c * span + here + HEAD_DIM, at]
                    + jnp.concatenate(
                        [bias[c * span + here : c * span + here + HEAD_DIM, :]] * (chunk // 128),
                        axis=1,
                    )
                    for c in range(3)
                )
                query = query * query_cosine + swap_halves(query) * query_sine
                key = key * cosine + swap_halves(key) * sine
                query_top[h] = jnp.maximum(
                    query_top[h], jnp.sum(query * query, axis=0, keepdims=True)
                )
                key_top[h] = jnp.maximum(key_top[h], jnp.sum(key * key, axis=0, keepdims=True))
                key_full = jnp.concatenate([key, key_line])
                queries[r, h, :, at] = jnp.concatenate([query, query_line]).astype(BF16)
                keys[r, h, :, at] = key_full.astype(BF16)
                values[r, h, :, at] = jnp.concatenate([value, ones]).astype(BF16)
                key_rows[h, at, :] = key_full.T.astype(BF16)
        bound = jnp.zeros((1, 1), F32)
        for h in range(heads):
            bound = jnp.maximum(
                bound,
                jnp.max(query_top[h], axis=-1, keepdims=True)
                * jnp.max(key_top[h], axis=-1, keepdims=True),
            )
        safe = jnp.max(bound) <= SAFE_SCORE * SAFE_SCORE
        peak[...] = jnp.zeros_like(peak)

        @pl.when(jnp.logical_not(safe))
        def _():
            def one_head(h, carry):
                scores = product(key_rows[h], queries[r, h])
                peak[pl.ds(h, 1), :] = (
                    jnp.max(scores, axis=0, keepdims=True).astype(BF16).astype(F32)
                )
                return carry

            lax.fori_loop(0, heads, one_head, 0)

        head_line = lax.broadcasted_iota(jnp.int32, (HEAD_ROWS, full), 0)

        def with_keys(count):
            def one_head(h, carry):
                top = peak[pl.ds(h, 1), :]
                query = jnp.where(
                    head_line == HEAD_DIM, -top, queries[r, h].astype(F32)
                ).astype(BF16)
                exponent = jnp.exp2(product(key_rows[h, :count, :], query) * LOG2E).astype(BF16)
                blend = product(values[r, h, :, :count], exponent)
                total = blend[HEAD_DIM : HEAD_DIM + 1, :]
                logsum[r, pl.ds(h, 1), :] = top + jnp.log(total)
                mixed_turned[r, pl.ds(pl.multiple_of(h * HEAD_DIM, 8), HEAD_DIM), :] = blend[
                    :HEAD_DIM
                ] * (1.0 / total)
                return carry

            lax.fori_loop(0, heads, one_head, 0, unroll=True)

        blocks = jnp.maximum((length + KEY_STEP - 1) // KEY_STEP, 1)
        for b in range(1, full // KEY_STEP + 1):
            pl.when(blocks == b)(lambda b=b: with_keys(b * KEY_STEP))
        mixed_turned[r, span:, :] = jnp.zeros((mixed_turned.shape[1] - span, full), F32)
        own_out[r] = mixed_turned[r, :, at_block(position, chunk)].astype(BF16)
        near_out[r] = mixed_turned[r, :, at_block(position ^ 1, chunk)].astype(BF16)
        cross_out[r, 0] = mixed_turned[r, :, at_block(position ^ 2, chunk)].astype(BF16)
        cross_out[r, 1] = mixed_turned[r, :, at_block(position ^ 3, chunk)].astype(BF16)
        return carry

    lax.fori_loop(0, rows, one_row, 0)
    for r in range(rows):
        pltpu.make_async_copy(normed.at[r], normed_out.at[r], semaphores.at[r]).wait()


def attend_back_kernel(heads, chunks, chunk, row, local, first, last, info, lengths, *refs):
    upstream_own, upstream_near, upstream_cross, upstream_far = refs[:4]
    queries, keys, values, logsum, mixed_turned, normed_in, weight_turned, inner, outer = refs[
        4:13
    ]
    refs = refs[13:]
    if not first:
        carried = refs[0]
        refs = refs[1:]
    if last:
        out_own, out_near, out_cross, weight, vector_rows = refs[:5]
        refs = refs[5:]
    own_out, near_out, cross_out = refs[:3]
    refs = refs[3:]
    if last:
        even_pieces, odd_pieces, norm_sums = refs[:3]
        refs = refs[3:]
    else:
        running = refs[0]
        refs = refs[1:]
    (
        upstream,
        query_full,
        upstream_full,
        key_rows,
        value_rows,
        grads,
        grad_low,
        packed,
        normed,
        semaphore,
    ) = refs
    fetch = pltpu.make_async_copy(normed_in.at[local], normed, semaphore)
    fetch.start()
    position, index = info[0], info[1]
    length = lengths[row_of(lengths, row, lengths.shape[0])]
    full = chunk * chunks
    span = heads * HEAD_DIM
    upstream[:, at_block(position, chunk)] = upstream_own[local]
    upstream[:, at_block(position ^ 1, chunk)] = upstream_near[local]
    upstream[:, at_block(position ^ 2, chunk)] = upstream_cross[local, 0]
    upstream[:, at_block(position ^ 3, chunk)] = upstream_far[local, 1]
    zeros = jnp.zeros((5, chunk), F32)
    line = lax.broadcasted_iota(jnp.int32, (8, chunk), 0)
    for j in range(chunks):
        at = slice(j * chunk, (j + 1) * chunk)
        turned = upstream[:, at].astype(F32)
        blend = turned * mixed_turned[local, :, at]
        for h in range(heads):
            own = slice(h * HEAD_DIM, (h + 1) * HEAD_DIM)
            high, middle, rest = split_three(-jnp.sum(blend[own], axis=0, keepdims=True))
            extra = jnp.where(
                line == 0, high, jnp.where(line == 1, middle, jnp.where(line == 2, rest, 0.0))
            )
            upstream_full[h, :, at] = jnp.concatenate([turned[own], extra]).astype(BF16)
            high, middle, rest = split_three(-logsum[local, h : h + 1, at])
            extra = jnp.where(
                line == 0,
                high,
                jnp.where(
                    line == 1, middle, jnp.where(line == 2, rest, jnp.where(line == 3, 1.0, 0.0))
                ),
            )
            query = queries[local, h, :, at].astype(F32)[:HEAD_DIM]
            query_full[h, :, at] = jnp.concatenate([query, extra]).astype(BF16)
            key_rows[h, at, :] = keys[local, h, :, at].astype(F32).T.astype(BF16)
            value_rows[h, at, :] = values[local, h, :, at].astype(F32).T.astype(BF16)

    def with_keys(count):
        def one_head(h, carry):
            own = pl.ds(pl.multiple_of(h * HEAD_DIM, 8), HEAD_DIM)
            grad_query = jnp.zeros((HEAD_ROWS, full), F32)
            for place in range(0, count, BLOCK):
                at = slice(place, min(place + BLOCK, count))
                probs = jnp.exp2(product(key_rows[h, at, :], query_full[h]) * LOG2E).astype(BF16)
                grad_probs = product(value_rows[h, at, :], upstream_full[h]).astype(BF16)
                grad_scores = probs * grad_probs
                grads[2, own, at] = product(upstream_full[h], probs, NT)[:HEAD_DIM]
                grads[1, own, at] = product(query_full[h], grad_scores, NT)[:HEAD_DIM]
                grad_query += product(keys[local, h, :, at], grad_scores)
            grads[0, own, :] = grad_query[:HEAD_DIM]
            return carry

        lax.fori_loop(0, heads, one_head, 0)
        if count < full:
            grads[1, :, count:] = jnp.zeros((span, full - count), F32)
            grads[2, :, count:] = jnp.zeros((span, full - count), F32)

    blocks = jnp.maximum((length + KEY_STEP - 1) // KEY_STEP, 1)
    for b in range(1, full // KEY_STEP + 1):
        pl.when(blocks == b)(lambda b=b: with_keys(b * KEY_STEP))

    sums = [[jnp.zeros((HEAD_DIM, 128), F32) for _ in range(heads)] for _ in range(3)]
    for j in range(chunks):
        at = slice(j * chunk, (j + 1) * chunk)
        cosine, sine = chunk_tables(inner, outer, j)
        query_cosine, query_sine = cosine * HEAD_DIM**-0.5, sine * HEAD_DIM**-0.5
        for h in range(heads):
            own = slice(h * HEAD_DIM, (h + 1) * HEAD_DIM)
            query, key, value = (grads[c, own, at] for c in range(3))
            query = query * query_cosine - swap_halves(query) * query_sine
            key = key * cosine - swap_halves(key) * sine
            for c, part in enumerate((query, key, value)):
                for piece in range(chunk // 128):
                    sums[c][h] = sums[c][h] + part[:, piece * 128 : (piece + 1) * 128]
                grads[c, own, at] = part
    for c in range(3):
        grad_low[c * span : (c + 1) * span, :] = grads[c].astype(BF16)
    for k in range(chunks):
        result = product(
            weight_turned[...], grad_low[:, at_block(position ^ k, chunk)]
        ).astype(BF16)
        if k == 0:
            own_out[...] = result
        elif k == 2:
            cross_out[...] = result
        else:
            near_out[k // 2] = result
    width = weight_turned.shape[0]
    fetch.wait()
    result = product(grad_low[...], normed[...], NT)
    bias_grad = jnp.concatenate(
        [jnp.sum(part, axis=1, keepdims=True) for group in sums for part in group]
    )
    bias_grad = jnp.broadcast_to(bias_grad, (3 * span, 128))
    if not first:
        result = result + carried[:, :width]
        bias_grad = bias_grad + carried[:, LANES:]
    if not last:
        running[:, :width] = result
        running[:, LANES:] = bias_grad
        return
    packed[: 3 * span, :width] = result
    gain_sum = jnp.zeros((8, width), F32)
    shift_sum = jnp.zeros((8, width), F32)
    gain, shift = vector_rows[0:1, :], vector_rows[1:2, :]
    for place in range(0, 3 * span, 8):
        own = slice(place, place + 8)
        factor = weight[own, :].astype(F32)
        column = bias_grad[own, 0:1]
        gain_sum = gain_sum + factor * (result[own] - shift * column)
        shift_sum = shift_sum + factor * column
    norm_sums[...] = jnp.zeros_like(norm_sums)
    norm_sums[0:1, :] = jnp.sum(gain_sum, axis=0, keepdims=True) / gain
    norm_sums[1:2, :] = jnp.sum(shift_sum, axis=0, keepdims=True)
    lane = lax.broadcasted_iota(jnp.int32, (3 * span, 128), 1)
    packed[: 3 * span, LANES - 128 :] = jnp.where(
        lane >= width - (LANES - 128), bias_grad, packed[: 3 * span, LANES - 128 :]
    )
    shared = (out_own[...].astype(F32) + out_near[0].astype(F32)) + out_cross[...].astype(F32)
    packed[3 * span : 4 * span, :] = shared[:span]
    packed[4 * span : 4 * span + 16, :] = shared[128:144]
    packed[4 * span + 16 :, :] = jnp.zeros((packed.shape[0] - 4 * span - 16, LANES), F32)
    size = packed.shape[0] // 8
    for j in range(8):
        target = odd_pieces if j % 2 else even_pieces
        target[j // 2] = packed[at_block(index ^ j, size), :].astype(BF16)


def gelu_parts(values):
    magnitude = jnp.abs(values) * (0.5**0.5)
    density = jnp.exp2(values * values * (-0.5 * LOG2E))
    divisor = 1.0 + 0.3275911 * magnitude
    step = pl.reciprocal(divisor, approx=True)
    step = step * (2.0 - divisor * step)
    series = 1.061405429 * step - 1.453152027
    series = series * step + 1.421413741
    series = series * step - 0.284496736
    series = series * step + 0.254829592
    tail = 0.5 * series * step * density
    share = jnp.where(values < 0, tail, 1.0 - tail)
    return share, density * (1.0 / math.sqrt(2.0 * math.pi))


def lane_groups(values):
    total = values[:, :128]
    for place in range(128, values.shape[1], 128):
        total = total + values[:, place : place + 128]
    return total


def row_sum(values):
    total = values[:8]
    for place in range(8, values.shape[0], 8):
        total = total + values[place : place + 8]
    return total


def feed_kernel(chunks, blocks, first_row, rows, last, info, lengths, *refs):
    hidden, cotangent, columns, up_bias = refs[:4]
    mixed_own, mixed_near, mixed_cross, mixed_far = refs[4:8]
    out_weight = refs[8 : 8 + chunks]
    refs = refs[8 + chunks :]
    if last:
        weights, carried, out_carried, sums_carried, bias_carried, hidden_before = refs[:6]
        refs = refs[6:]
    else:
        feeds, refs = refs[:12], refs[12:]
    hidden_out, grad_middle_out, grad_own, grad_near, grad_cross = refs[:5]
    refs = refs[5:]
    if last:
        kept_out, sent_out, out_own, out_near, out_cross = refs[:5]
    else:
        weights, carried, out_carried, sums_carried, bias_carried = refs[:5]
    refs = refs[5:]
    (
        out_rows,
        mixed,
        source,
        given,
        low_rows,
        down_total,
        back_total,
        upward,
        upstream,
        active,
        grad_low,
        sums_total,
        bias_total,
        shared,
        semaphores,
    ) = refs
    core, index = info[0] & 1, info[1]
    width, chunk = hidden.shape[1:]
    tokens = rows * chunk
    held = mixed_own.shape[1]
    places = [row_of(lengths, first_row + r, hidden.shape[0]) for r in range(rows)]
    if not last:
        copies = []
        for side in range(2):
            sources = list(feeds[6 * side : 6 * side + 4])
            duo, duo_beside = feeds[6 * side + 4 : 6 * side + 6]
            place = core if side == 0 else 1 - core
            for e in range(2):
                sources += [duo.at[e], duo_beside.at[e]]
            for j in range(blocks):
                copies.append(
                    pltpu.make_async_copy(
                        sources[j],
                        weights.at[place, :, j * BLOCK : (j + 1) * BLOCK],
                        semaphores.at[side, j],
                    )
                )
        for copy in copies:
            copy.start()
    own_rows = (out_weight[0].shape[0] - 2 * width) // 2
    for k in range(chunks):
        base = 2 * width
        at = k * held
        out_rows[at : at + held, :] = jnp.zeros((held, width), BF16)
        out_rows[at : at + own_rows, :chunk] = out_weight[k][base : base + own_rows, :]
        out_rows[at : at + own_rows, chunk:] = out_weight[k][
            base + own_rows : base + 2 * own_rows, : width - chunk
        ]
    for r in range(rows):
        at = slice(r * chunk, (r + 1) * chunk)
        mixed[0 * held : 1 * held, at] = mixed_own[r]
        mixed[1 * held : 2 * held, at] = mixed_near[r]
        mixed[2 * held : 3 * held, at] = mixed_cross[r, 0]
        mixed[3 * held : 4 * held, at] = mixed_far[r, 1]
        given[:, at] = cotangent[places[r]]
    source[...] = product(out_rows[...], mixed[...], TN)
    step = 32
    pieces = [slice(place, place + step) for place in range(0, width, step)]

    total = jnp.zeros((8, tokens), F32)
    for own in pieces:
        entered = jnp.concatenate([hidden[places[r], own, :] for r in range(rows)], axis=1)
        middle = source[own, :] + entered.astype(F32) + columns[own, 2:3]
        source[own, :] = middle
        total = total + row_sum(middle)
    mean = jnp.sum(total, axis=0, keepdims=True) * (1.0 / width)
    total = jnp.zeros((8, tokens), F32)
    for own in pieces:
        centre = source[own, :] - mean
        total = total + row_sum(centre * centre)
    inverse = lax.rsqrt(jnp.sum(total, axis=0, keepdims=True) * (1.0 / width) + EPS)
    for own in pieces:
        middle = source[own, :]
        unit = (middle - mean) * inverse
        low_rows[own, :] = (unit * columns[own, 3:4] + columns[own, 4:5]).astype(BF16)
        down_total[own, :] = middle + columns[own, 5:6]
        source[own, :] = unit
    back_total[...] = jnp.zeros_like(back_total)
    if not last:
        for copy in copies:
            copy.wait()

    pair = 2 * BLOCK

    def enter(i, slot):
        at = at_block(i, pair)
        upward[slot] = product(weights[0, :, at], low_rows[...], TN)
        upstream[slot] = product(weights[1, :, at], given[...], TN)

    lane = lax.broadcasted_iota(jnp.int32, (step, 128), 1)

    def bend(i, slot):
        for place in range(0, pair, step):
            own = slice(place, place + step)
            j = 2 * i + place // BLOCK
            inside = slice(place % BLOCK, place % BLOCK + step)
            bias = jnp.sum(
                jnp.where(lane == j, up_bias[inside, :], 0.0), axis=1, keepdims=True
            )
            values = upward[slot, own, :] + bias
            share, density = gelu_parts(values)
            active[slot, own, :] = (values * share).astype(BF16)
            grad_up = upstream[slot, own, :] * (share + values * density)
            grad_low[slot, own, :] = grad_up.astype(BF16)
            bias_sum = lane_groups(grad_up)
            if last:
                bias_total[j, inside, :] = bias_sum + bias_carried[j, inside, :]
            else:
                bias_carried[j, inside, :] = bias_sum

    def leave(i, slot):
        at = at_block(i, pair)
        down_total[...] += product(weights[1, :, at], active[slot])
        back_total[...] += product(weights[0, :, at], grad_low[slot])
        up_grad = product(low_rows[...], grad_low[slot], NT)
        down_grad = product(given[...], active[slot], NT)
        if not last:
            carried[0, :, at] = up_grad
            carried[1, :, at] = down_grad
            return
        up_grad = up_grad + carried[0, :, at]
        down_grad = down_grad + carried[1, :, at]
        kept = jnp.where(core == 0, up_grad, down_grad).astype(BF16)
        sent = jnp.where(core == 0, down_grad, up_grad).astype(BF16)
        for odd in range(2):
            kept_out[odd, i] = kept[:, odd * BLOCK : (odd + 1) * BLOCK]
            sent_out[odd, i] = sent[:, odd * BLOCK : (odd + 1) * BLOCK]

    def two_pairs(n, carry):
        i = 2 * n
        enter(i + 1, 1)
        bend(i, 0)
        leave(i, 0)
        enter(lax.rem(i + 2, blocks // 2), 0)
        bend(i + 1, 1)
        leave(i + 1, 1)
        return carry

    enter(0, 0)
    lax.fori_loop(0, blocks // 4, two_pairs, 0)
    if last:
        for r in range(first_row):
            hidden_out[row_of(lengths, r, hidden.shape[0])] = hidden_before[r]
    for r in range(rows):
        place = places[r] if last else r
        hidden_out[place] = down_total[:, r * chunk : (r + 1) * chunk].astype(BF16)
    scaled_total = jnp.zeros((8, tokens), F32)
    unit_total = jnp.zeros((8, tokens), F32)
    for own in pieces:
        scaled = back_total[own, :] * columns[own, 3:4]
        scaled_total = scaled_total + row_sum(scaled)
        unit_total = unit_total + row_sum(scaled * source[own, :])
    scaled_mean = jnp.sum(scaled_total, axis=0, keepdims=True) * (1.0 / width)
    unit_mean = jnp.sum(unit_total, axis=0, keepdims=True) * (1.0 / width)
    for own in pieces:
        back, unit = back_total[own, :], source[own, :]
        given_wide = given[own, :].astype(F32)
        scaled = back * columns[own, 3:4]
        grad_middle = given_wide + inverse * (scaled - scaled_mean - unit * unit_mean)
        for r in range(rows):
            grad_middle_out[r, own, :] = grad_middle[:, r * chunk : (r + 1) * chunk]
        low_rows[own, :] = grad_middle.astype(BF16)
        for place, part in enumerate((back * unit, back, grad_middle, given_wide)):
            part = lane_groups(part)
            if last:
                sums_total[place, own, :] = part + sums_carried[place, own, :]
            else:
                sums_carried[place, own, :] = part
    mixed_grad = product(out_rows[...], low_rows[...]).astype(BF16)
    for r in range(rows):
        at = slice(r * chunk, (r + 1) * chunk)
        grad_own[r] = mixed_grad[:held, at]
        grad_near[r] = mixed_grad[held : 2 * held, at]
        grad_cross[r, 0] = mixed_grad[2 * held : 3 * held, at]
        grad_cross[r, 1] = mixed_grad[3 * held :, at]
    out_part = product(mixed[...], low_rows[...], NT)
    if not last:
        out_carried[...] = out_part
        return
    out_part = (out_part + out_carried[...]).astype(BF16)
    shared[...] = jnp.zeros_like(shared)
    for place in range(4):
        line = row_sum(sums_total[place].T)
        shared[place : place + 1, :width] = jnp.sum(line, axis=0, keepdims=True)
    for j in range(blocks):
        line = row_sum(bias_total[j].T)
        shared[pl.ds(4 + (index ^ j), 1), :BLOCK] = jnp.sum(line, axis=0, keepdims=True)
    shared_low = shared[...].astype(BF16)
    for k, target in enumerate((out_own, out_near.at[0], out_cross, out_near.at[1])):
        target[:held, 384:] = jnp.zeros((held, LANES - 384), BF16)
        target[:held, :width] = out_part[k * held : (k + 1) * held]
        target[held:, :] = shared_low


def norm_back_kernel(rows, lengths, hidden, columns, *refs):
    middle_grads, refs = refs[:2], refs[2:]
    own_parts, near_parts = refs[0 : 2 * rows : 2], refs[1 : 2 * rows : 2]
    crossed, (out,) = refs[2 * rows : 2 * rows + rows // 2], refs[2 * rows + rows // 2 :]
    cross_parts = [part.at[place] for part in crossed for place in range(2)]
    gain = columns[:, 0:1]
    for row in range(rows):
        place = row_of(lengths, row, rows)
        unit, inverse = norm_columns(hidden[place].astype(F32))
        grad = (
            own_parts[row][...].astype(F32)
            + near_parts[row][0].astype(F32)
            + cross_parts[row][...].astype(F32)
        )
        half = rows // 2
        result = middle_grads[row // half][row % half] + norm_columns_back(
            grad, unit, inverse, gain
        )
        out[place] = result.astype(BF16)


def add_pieces_kernel(even, beside, *outs):
    for i, out in enumerate(outs):
        out[...] = (even[i].astype(F32) + beside[i].astype(F32)).astype(BF16)


def own_piece_kernel(first, second, fourth, sixth, norm_sums, out):
    size = first.shape[0]
    total = first[...].astype(F32) + second[...].astype(F32)
    total = total + fourth[...].astype(F32) + sixth[...].astype(F32)
    out[:size, :] = total.astype(BF16)
    width = norm_sums.shape[1]
    values = norm_sums[...]
    high = values.astype(BF16)
    rest = (values - high.astype(F32)).astype(BF16)
    out[size:, 384:] = jnp.zeros((16, LANES - 384), BF16)
    out[size:, :width] = jnp.concatenate([high.astype(F32), rest.astype(F32)]).astype(BF16)


def feed_sum_kernel(info, first, second, fourth, sixth, keep, send, rows):
    total = first[...].astype(F32) + second[...].astype(F32)
    rows[...] = total + fourth[...].astype(F32) + sixth[...].astype(F32)
    size = keep.shape[0]
    chip = info[0] >> 1
    keep[...] = rows[at_block(chip, size), :].astype(BF16)
    send[...] = rows[at_block(1 - chip, size), :].astype(BF16)


def feed_pair_kernel(info, kept, came, mine, other, rows):
    rows[...] = kept[...].astype(F32) + came[...].astype(F32)
    size = mine.shape[0]
    core = info[0] & 1
    mine[...] = rows[at_block(core, size), :].astype(BF16)
    other[...] = rows[at_block(1 - core, size), :].astype(BF16)


def unpack_kernel(info, *refs):
    evens, beside = refs[:4], refs[4]
    refs = refs[5:]
    if len(refs) > 12:
        mine, came, refs = refs[0], refs[1], refs[2:]
        up_grad, down_grad = refs[10:12]
        refs = refs[:10] + refs[12:]
        count = up_grad.shape[1]

        def write(up, down):
            up_grad[...] = up[:, :count].astype(F32)
            down_grad[...] = down[...].astype(F32).T[:count, :]

        pl.when(info[0] & 1 == 0)(lambda: write(mine, came))
        pl.when(info[0] & 1 == 1)(lambda: write(came, mine))
    weight_grad, bias_grad, out_grad, gain, shift, out_bias, down_bias, up_bias = refs[:8]
    norm_gain, norm_shift, whole, line = refs[8:]
    size = whole.shape[0] // 8
    width = weight_grad.shape[1]
    norms = [evens[0][size:, :].astype(F32) + beside[0, size:, :].astype(F32)]
    for i in range(4):
        whole[at_block(info[1] ^ (2 * i), size), :] = evens[i][:size, :].astype(F32)
        whole[at_block(info[1] ^ (2 * i + 1), size), :] = beside[i, :size, :].astype(F32)
        if i > 0:
            norms.append(evens[i][size:, :].astype(F32) + beside[i, size:, :].astype(F32))
    norms = (norms[0] + norms[1]) + (norms[2] + norms[3])
    norms = norms[:8] + norms[8:16]
    norm_gain[...] = norms[0:1, :width]
    norm_shift[...] = norms[1:2, :width]
    columns = weight_grad.shape[2]
    for c in range(3):
        turned = whole[c * columns : (c + 1) * columns, :].T
        weight_grad[c] = turned[:width, :]
        bias_grad[c : c + 1, :] = turned[width : width + 1, :]
    out_grad[...] = whole[3 * columns : 4 * columns, :width]
    for place, target in enumerate((gain, shift, out_bias, down_bias)):
        target[...] = whole[4 * columns + place : 4 * columns + place + 1, :width]
    block = up_bias.shape[0] // 8
    for j in range(8):
        line[:, j * block : (j + 1) * block] = whole[
            4 * columns + 4 + j : 4 * columns + 5 + j, :block
        ]
    up_bias[...] = line[0, :]


def swap(values, axis, bit):
    size = lax.axis_size(axis)
    return lax.ppermute(values, axis, [(i, i ^ bit) for i in range(size)])


def gather_four(own, *others):
    beside = swap(own, "tensor", 1)
    across = swap(own, "tensor", 2)
    return [own, beside, across, swap(after(across, *others), "tensor", 1)]


def spread_four(own, near, cross, beside, *others):
    across = swap(cross, "tensor", 2)
    return [own, beside, across, swap(after(across, *others), "tensor", 1)]


def add_low(*parts):
    total = parts[0].astype(F32)
    for part in parts[1:]:
        total = total + part.astype(F32)
    return total.astype(BF16)


def gather_feed_plain(up, down, core):
    pair = jnp.stack([up, down.T])
    pair = lax.all_gather(pair, "tensor", axis=1, tiled=True)
    pair = lax.all_gather(pair, "dp", axis=2, tiled=True)
    pair = pair.reshape(2, pair.shape[1], 8, -1).transpose(0, 2, 1, 3)
    pair = jnp.pad(pair, ((0, 0), (0, 0), (0, 0), (0, BLOCK - pair.shape[3])))
    pair = jnp.where(core == 0, pair, pair[::-1])
    feeds = []
    for half in (pair[0], pair[1]):
        feeds += [half[0], half[1], half[2], half[3], half[4::2], half[5::2]]
    return feeds


def scatter_feed_plain(kept, sent, core, hidden_count):
    grads = jnp.stack([kept, sent]).swapaxes(1, 2).reshape(2, 8, *kept.shape[2:])
    grads = jnp.where(core == 0, grads, grads[::-1]).astype(F32)
    grads = grads[:, :, :, : hidden_count * lax.axis_size("dp") // 8]
    grads = grads.transpose(0, 2, 1, 3).reshape(2, grads.shape[2], -1)
    grads = lax.psum_scatter(grads, "dp", scatter_dimension=2, tiled=True)
    grads = lax.psum_scatter(grads, "tensor", scatter_dimension=1, tiled=True)
    return grads[0], grads[1].T


def sum_pieces(even, beside, norm_sums):
    parts = call(
        add_pieces_kernel,
        (even, beside),
        [shape(even.shape[1:], BF16)] * 4,
        limit=4,
    )
    parts = [parts[0]] + [swap(parts[i], "dp", 2 * i) for i in (1, 2, 3)]
    norm_sums = norm_sums + swap(norm_sums, "tensor", 1)
    (own,) = call(
        own_piece_kernel,
        (*parts, norm_sums),
        [shape((even.shape[1] + 16, LANES), BF16)],
        limit=4,
    )
    back = [own] + [swap(own, "dp", e) for e in (2, 4, 6)]
    return back + [swap(jnp.stack(back), "dp", 1)], own


def sum_pieces_plain(even, odd, norm_sums):
    even, odd = (lax.psum(part.astype(F32), "dp").astype(BF16) for part in (even, odd))
    norm_sums = lax.psum(norm_sums, ("dp", "tensor"))
    high = norm_sums.astype(BF16)
    rest = (norm_sums - high.astype(F32)).astype(BF16)
    rows = jnp.concatenate([high, rest])
    rows = jnp.pad(rows, ((0, 0), (0, LANES - rows.shape[1])))
    even = jnp.concatenate([even, jnp.stack([rows] + [jnp.zeros_like(rows)] * 3)], axis=1)
    odd = jnp.concatenate([odd, jnp.zeros((4, *rows.shape), BF16)], axis=1)
    return [even[i] for i in range(4)] + [odd]


def shards(
    hidden_in,
    attn_gain,
    attn_shift,
    query_key_value_weight,
    query_key_value_bias,
    attention_output_weight,
    out_bias,
    ffn_gain,
    ffn_shift,
    up_projection_weight,
    up_projection_bias,
    down_projection_weight,
    down_bias,
    lengths,
    cotangent,
):
    chunks = lax.axis_size("tensor")
    ring = lax.axis_size("dp") == 8
    position = lax.axis_index("tensor")
    index = lax.axis_index("dp") if ring else jnp.int32(0)
    core = position & 1
    rows, chunk, width = hidden_in.shape
    full = chunk * chunks
    columns = query_key_value_weight.shape[2]
    heads = columns // HEAD_DIM
    hidden_count = up_projection_weight.shape[1]
    blocks = 8
    half = rows // 2

    info = jnp.stack([position, index]).astype(jnp.int32)
    lengths = lengths.astype(jnp.int32)
    inner_table, outer_table = (jnp.asarray(table) for table in rotary_constants(chunk, chunks))
    hidden = hidden_in.transpose(0, 2, 1)
    given = cotangent.transpose(0, 2, 1)

    if ring:
        inputs = (info, up_projection_weight, down_projection_weight)
        (pair,) = call(
            pair_kernel,
            inputs,
            [shape((columns, 2 * BLOCK), BF16)],
            scratch=[pltpu.VMEM(part.shape, part.dtype) for part in inputs[1:]]
            + [pltpu.SemaphoreType.DMA((2,))],
            in_specs=[smem()] + hbm(2),
            limit=4,
            tiles=20,
        )
        pair_across = swap(pair, "tensor", 2)
    inputs = (
        lengths,
        after(hidden, pair) if ring else hidden,
        attn_gain[None],
        attn_shift[None],
        attention_output_weight,
    )
    first, second = call(
        norm_kernel,
        inputs,
        [
            shape((half * width, chunk), BF16),
            shape((half * width + 2 * columns, chunk), BF16),
        ],
        scratch=[pltpu.VMEM(part.shape, part.dtype) for part in inputs[1:]]
        + [pltpu.VMEM((128, width), F32), pltpu.SemaphoreType.DMA((8,))],
        in_specs=[smem()] + hbm(4),
        limit=8,
        tiles=80,
    )
    inputs = (
        info,
        attn_gain[None],
        attn_shift[None],
        out_bias[None],
        ffn_gain[None],
        ffn_shift[None],
        down_bias[None],
        up_projection_bias[None],
        query_key_value_weight,
        query_key_value_bias,
    )
    weight, weight_turned, vectors, bias, up_bias, vector_rows = call(
        lambda *refs: prepare_kernel(heads, *refs),
        inputs,
        [
            shape((3 * columns, width), BF16),
            shape((width, 3 * columns), BF16),
            shape((width, 128), F32),
            shape((3 * columns, 128), F32),
            shape((BLOCK, 128), F32),
            shape((8, width), F32),
        ],
        scratch=[
            pltpu.VMEM((3 * columns, width), F32),
            pltpu.VMEM((128, BLOCK), F32),
        ]
        + [pltpu.VMEM(part.shape, part.dtype) for part in inputs[1:]]
        + [pltpu.SemaphoreType.DMA((9,))],
        in_specs=[smem()] + hbm(len(inputs) - 1),
        limit=8,
        tiles=60,
    )
    if ring:
        parts = [
            pair,
            swap(pair, "tensor", 1),
            pair_across,
            swap(after(pair_across, first), "tensor", 1),
        ]
        (own_feed,) = call(
            lambda *refs: assemble_kernel(chunks, *refs),
            (info, *parts),
            [shape((width, BLOCK), BF16)],
            scratch=[pltpu.VMEM((width, BLOCK), F32)],
            in_specs=[smem()] + vmem(chunks),
            limit=6,
            tiles=20,
        )
        came = [swap(own_feed, "dp", e) for e in (2, 4, 6)]
        beside = swap(own_feed, "dp", 1)
        second_beside = swap(came[0], "dp", 1)
        gathered = [
            gather_four(after(first, pair_across), own_feed, came[0], beside, weight)
        ]
    else:
        gathered = [gather_four(first)]

    kept = []
    mixed = []
    for g in range(2):
        if g == 1 and ring:
            gathered[1][0] = after(gathered[1][0], duo, beside, second_beside, mixed[0][3])
        inputs = (info, lengths, *gathered[g], weight, bias, inner_table, outer_table)
        outs = call(
            lambda *refs, g=g: attend_kernel(heads, chunks, chunk, g * half, half, *refs),
            inputs,
            [
                shape((half, 128, chunk), BF16),
                shape((half, 128, chunk), BF16),
                shape((half, 2, 128, chunk), BF16),
            ]
            + [shape((half, heads, HEAD_ROWS, full), BF16)] * 3
            + [
                shape((half, 8, full), F32),
                shape((half, 128, full), F32),
                shape((half, width, full), BF16),
            ],
            scratch=[
                pltpu.VMEM((heads, full, HEAD_ROWS), BF16),
                pltpu.VMEM((8, full), F32),
                pltpu.VMEM((3 * columns, full), F32),
                pltpu.VMEM((half, width, full), BF16),
                pltpu.SemaphoreType.DMA((half,)),
            ],
            in_specs=[smem(), smem()] + vmem(len(inputs) - 2),
            out_specs=vmem(8) + hbm(),
            limit=14,
            tiles=400,
        )
        kept.append(outs[3:])
        mixed.append(list(outs[:3]) + [swap(outs[1], "tensor", 1)])
        if g == 0:
            gathered.append(gather_four(after(second, gathered[0][2]), outs[0]))
            if ring:
                duo = jnp.stack([after(part, mixed[0][3], second_beside) for part in came[1:]])
                duo_beside = swap(duo, "dp", 1)
            else:
                feeds = gather_feed_plain(up_projection_weight, down_projection_weight, core)

    if ring:
        duo_beside = after(duo_beside, kept[1][0])
        feeds = [own_feed, beside, came[0], second_beside, duo, duo_beside]
        feeds += [swap(part, "tensor", 1) for part in feeds]
    feed_outs = []
    for g in range(2):
        last = g == 1
        others = (kept[1][0],) if g == 0 else (feed_outs[0][2],)
        ready = (mixed[1][3],) if g == 0 else (mixed_near,)
        inputs = (
            info,
            lengths,
            hidden,
            after(given, *ready),
            vectors,
            up_bias,
            *spread_four(*mixed[g], *others),
            *gathered[1],
        )
        if last:
            inputs = inputs + tuple(feed_outs[0][5:]) + (feed_outs[0][0],)
        else:
            inputs = inputs + tuple(feeds)
        carried = [
            shape((2, width, blocks * BLOCK), BF16),
            shape((2, width, blocks * BLOCK), F32),
            shape((chunks * 128, width), F32),
            shape((4, width, 128), F32),
            shape((blocks, BLOCK, 128), F32),
        ]
        sent = [
            shape((2, blocks // 2, width, BLOCK), BF16),
            shape((2, blocks // 2, width, BLOCK), BF16),
            shape((144, LANES), BF16),
            shape((2, 144, LANES), BF16),
            shape((144, LANES), BF16),
        ]
        tokens = half * chunk
        outs = call(
            lambda *refs, g=g, last=last: feed_kernel(
                chunks, blocks, g * half, half, last, *refs
            ),
            inputs,
            [
                shape((rows if last else half, width, chunk), BF16),
                shape((half, width, chunk), F32),
                shape((half, 128, chunk), BF16),
                shape((half, 128, chunk), BF16),
                shape((half, 2, 128, chunk), BF16),
            ]
            + (sent if last else carried),
            scratch=[
                pltpu.VMEM((chunks * 128, width), BF16),
                pltpu.VMEM((chunks * 128, tokens), BF16),
                pltpu.VMEM((width, tokens), F32),
                pltpu.VMEM((width, tokens), BF16),
                pltpu.VMEM((width, tokens), BF16),
                pltpu.VMEM((width, tokens), F32),
                pltpu.VMEM((width, tokens), F32),
                pltpu.VMEM((2, 2 * BLOCK, tokens), F32),
                pltpu.VMEM((2, 2 * BLOCK, tokens), F32),
                pltpu.VMEM((2, 2 * BLOCK, tokens), BF16),
                pltpu.VMEM((2, 2 * BLOCK, tokens), BF16),
                pltpu.VMEM((4, width, 128), F32),
                pltpu.VMEM((blocks, BLOCK, 128), F32),
                pltpu.VMEM((16, LANES), F32),
                pltpu.SemaphoreType.DMA((2, blocks)),
            ],
            in_specs=[smem(), smem()]
            + (
                vmem(len(inputs) - 2)
                if last
                else vmem(len(inputs) - 2 - len(feeds)) + [pl.BlockSpec(memory_space=pl.ANY)] * len(feeds)
            ),
            limit=22,
            tiles=500,
        )
        feed_outs.append(outs)
        if g == 0:
            mixed_near = swap(outs[3], "tensor", 1)
    hidden_out = feed_outs[1][0]
    middle_grads = [outs[1] for outs in feed_outs]
    feed_kept, feed_sent, out_own, out_near, out_cross = feed_outs[1][5:]

    mixed_grads = [spread_four(*feed_outs[0][2:5], mixed_near, feed_outs[1][2])]
    feed_sent, out_near = after((feed_sent, out_near), mixed_grads[0][3])
    out_came = swap(out_near, "tensor", 1)
    feed_came = swap(feed_sent, "tensor", 1)
    running = None
    reduced = []
    crossing = []
    for r in range(rows):
        last = r == rows - 1
        g = r // half
        inputs = (
            info,
            lengths,
            *mixed_grads[g],
            *kept[g],
            weight_turned,
            inner_table,
            outer_table,
        )
        if last and ring:
            running = after(running, *evens)
        if r > 0:
            inputs = inputs + (running,)
        if last:
            inputs = inputs + (out_own, out_came, out_across, weight, vector_rows)
        outs = call(
            lambda *refs, r=r, last=last: attend_back_kernel(
                heads, chunks, chunk, r, r % half, r == 0, last, *refs
            ),
            inputs,
            [
                shape((width, chunk), BF16),
                shape((2, width, chunk), BF16),
                shape((width, chunk), BF16),
            ]
            + (
                [shape((4, 64, LANES), BF16)] * 2 + [shape((8, width), F32)]
                if last
                else [shape((3 * columns, LANES + 128), F32)]
            ),
            scratch=[
                pltpu.VMEM((128, full), BF16),
                pltpu.VMEM((heads, HEAD_ROWS, full), BF16),
                pltpu.VMEM((heads, HEAD_ROWS, full), BF16),
                pltpu.VMEM((heads, full, HEAD_ROWS), BF16),
                pltpu.VMEM((heads, full, HEAD_ROWS), BF16),
                pltpu.VMEM((3, columns, full), F32),
                pltpu.VMEM((3 * columns, full), BF16),
                pltpu.VMEM((512, LANES), F32),
                pltpu.VMEM((width, full), BF16),
                pltpu.SemaphoreType.DMA(()),
            ],
            in_specs=[smem(), smem()] + vmem(9) + hbm() + vmem(len(inputs) - 12),
            limit=12,
            tiles=420,
        )
        if last:
            outs = list(outs)
            even, odd, norm_sums = outs[3:]
            if ring:
                odd = after(odd, reduced[5], *feed_came)
                beside_pieces = swap(odd, "dp", 1)
                norm_sums = norm_sums + swap(norm_sums, "tensor", 2)
                outs[1] = after(outs[1], beside_pieces, norm_sums)
        near = swap(outs[1], "tensor", 1)
        reduced += [outs[0], near, None]
        crossing.append((outs[2], near))
        if r >= 2:
            pair_sum = jnp.stack(
                [
                    add_low(after(cross, outs[0], out_across), near[1])
                    for cross, near in crossing[2 * r - 4 : 2 * r - 2]
                ]
            )
            reduced[3 * (2 * r - 3) + 2] = swap(pair_sum, "tensor", 2)
        if not last:
            running = outs[3]
        if r == 1:
            mixed_near = swap(feed_outs[1][3], "tensor", 1)
            mixed_grads.append(spread_four(*feed_outs[1][2:5], mixed_near, outs[0]))
        if r == 0:
            out_across = swap(
                add_low(after(out_cross, outs[0]), out_came[1]), "tensor", 2
            )
            if ring:
                feed_odd = add_low(after(feed_kept[1], outs[0]), feed_came[1])
                running = after(running, feed_odd)
                feed_odd = swap(feed_odd, "dp", 1)
        if r == 2 and ring:
            feed_kept = after(feed_kept, outs[0])
            evens = [
                add_low(feed_kept[0, i], feed_came[0, i], feed_odd[i]) for i in range(4)
            ]
            feed_came = [swap(evens[i], "dp", 2 * i) for i in (1, 2, 3)]
    own_parts = [part for place, part in enumerate(reduced) if place % 3 < 2]
    cross_parts = [part for part in reduced[2::3] if part is not None]
    inputs = (lengths, hidden, vectors, *middle_grads, *own_parts, *cross_parts)
    (grad_hidden,) = call(
        lambda *refs: norm_back_kernel(rows, *refs),
        inputs,
        [shape((rows, width, chunk), BF16)],
        in_specs=[smem()] + vmem(len(inputs) - 1),
        limit=12,
        tiles=120,
    )
    if ring:
        parts, own = sum_pieces(even, beside_pieces, norm_sums)
    else:
        parts = sum_pieces_plain(even, odd, norm_sums)
    if ring:
        keep, send = call(
            feed_sum_kernel,
            (info, after(evens[0], own), *feed_came),
            [shape((width // 2, BLOCK), BF16)] * 2,
            scratch=[pltpu.VMEM((width, BLOCK), F32)],
            in_specs=[smem()] + vmem(4),
            limit=4,
            tiles=20,
        )
        mine, other = call(
            feed_pair_kernel,
            (info, keep, after(swap(send, "tensor", 2), grad_hidden)),
            [shape((columns, BLOCK), BF16)] * 2,
            scratch=[pltpu.VMEM((width // 2, BLOCK), F32)],
            in_specs=[smem()] + vmem(2),
            limit=4,
            tiles=20,
        )
        feed_parts = (mine, swap(other, "tensor", 1))
    else:
        grad_up_weight, grad_down_weight = scatter_feed_plain(
            feed_kept, feed_sent, core, hidden_count
        )

    inputs = (info, *parts) + (feed_parts if ring else ())
    outs = [
        shape((3, width, columns), F32),
        shape((3, columns), F32),
        shape((columns, width), F32),
    ]
    outs += [shape((1, width), F32)] * 4
    outs += [shape(up_projection_bias.shape, F32)]
    outs += [shape((1, width), F32)] * 2
    if ring:
        outs += [shape((columns, hidden_count), F32), shape((hidden_count, columns), F32)]
    outs = call(
        unpack_kernel,
        inputs,
        outs,
        scratch=[
            pltpu.VMEM((512, LANES), F32),
            pltpu.VMEM((1, up_projection_bias.shape[0]), F32),
        ],
        in_specs=[smem()] + vmem(len(inputs) - 1),
        limit=8,
        tiles=60,
    )
    grad_qkv_weight, grad_qkv_bias, grad_out_weight = outs[:3]
    grad_ffn_gain, grad_ffn_shift, grad_out_bias, grad_down_bias, grad_up_bias = outs[3:8]
    grad_attn_gain, grad_attn_shift = outs[8:10]
    if ring:
        grad_up_weight, grad_down_weight = outs[10:]
    return (
        hidden_out.transpose(0, 2, 1),
        grad_hidden.transpose(0, 2, 1),
        grad_attn_gain[0],
        grad_attn_shift[0],
        grad_qkv_weight,
        grad_qkv_bias,
        grad_out_weight,
        grad_out_bias[0],
        grad_ffn_gain[0],
        grad_ffn_shift[0],
        grad_up_weight,
        grad_up_bias,
        grad_down_weight,
        grad_down_bias[0],
    )


def solution(mesh):
    return jax.shard_map(
        shards,
        mesh=mesh,
        in_specs=(
            P("dp", "tensor", None),
            P(),
            P(),
            P(None, None, "tensor"),
            P(None, "tensor"),
            P("tensor", None),
            P(),
            P(),
            P(),
            P("tensor", "dp"),
            P(),
            P("dp", "tensor"),
            P(),
            P("dp"),
            P("dp", "tensor", None),
        ),
        out_specs=(
            P("dp", "tensor", None),
            P("dp", "tensor", None),
            P(),
            P(),
            P(None, None, "tensor"),
            P(None, "tensor"),
            P("tensor", None),
            P(),
            P(),
            P(),
            P("tensor", "dp"),
            P(),
            P("dp", "tensor"),
            P(),
        ),
        check_vma=False,
    )
```
